32 devices in a mesh: row: 2 (over x), col: 16 (over z, y, core).
Axes of the slice: x: 2, y: 2, z: 4, core: 2. Of those that a mesh axis runs over, the one named last changes fastest.
Arguments:
- tokens: bfloat16 [25216, 768], P(('row', 'col')), may hold values from -6 to 6
- keep_mask: int32 [128, 197], P(('row', 'col')), may hold values from 0 to 1, as said below
- w_qkv: bfloat16 [768, 2304], replicated, may hold values from -0.3125 to 0.3125
- w_out: bfloat16 [768, 768], replicated, may hold values from -0.3125 to 0.3125
- w_up: bfloat16 [768, 3072], replicated, may hold values from -0.4375 to 0.4375
- w_down: bfloat16 [3072, 768], replicated, may hold values from -0.109375 to 0.109375
- vectors: float32 [8, 768], replicated, may hold values from -3 to 3, as said below
- up_bias: float32 [3072], replicated, may hold values from -3 to 3
- w_proj: bfloat16 [768, 512], replicated, may hold values from -0.21875 to 0.21875
- texts: bfloat16 [128, 512], P(('row', 'col')), may hold values from -0.29882812 to 0.29882812
- pair_index: int32 [128], replicated, may hold values from 0 to 127, each once
- logit_scale: float32 [1], replicated, may hold values from 30 to 60
Outputs:
- loss: float32 [1], replicated
- token_grad: float32 [25216, 768], P(('row', 'col'))
- qkv_grad: float32 [768, 2304], P('col')
- out_grad: float32 [768, 768], P('col')
- up_grad: float32 [768, 3072], P('col')
- down_grad: float32 [3072, 768], P('col')
- vectors_grad: float32 [8, 768], P(None, 'col')
- up_bias_grad: float32 [3072], P('col')
- proj_grad: float32 [768, 512], P('col')
- text_grad: float32 [128, 512], P(('row', 'col'))
The draws below stay inside these ranges and needn't reach their ends.
Inputs may be any that keep to these rules, and one draw needn't show every extreme that they name: `keep_mask`: column 0 of every row is 1; the number of kept tokens varies from image to image. `vectors`: rows 0 and 5 are gains, the others biases.
All inputs are finite; a program needn't handle non-finite values.
Results may differ from the reference program's by a relative error of at most 0.017.
Values may be sent and summed in bfloat16 or wider, within the bound.
A program may use at most 192 MiB of HBM per device.

```python
import jax
import jax.numpy as jnp
from jax import lax

D = 768
HEADS = 12
HEAD_DIM = 64
FF = 3072
EMB = 512
SEQ = 197
IMAGES = 128
TOKENS = 25216


def draw_keep_mask(key, part):
    count_key, rank_key = jax.random.split(jax.random.fold_in(key, 11))
    counts = jax.random.randint(count_key, (IMAGES, 1), SEQ // 8, SEQ + 1)
    ranks = jax.random.randint(rank_key, (IMAGES, SEQ), 0, SEQ)
    first = jnp.arange(SEQ)[None, :] == 0
    return jnp.where(first | (ranks < counts), 1, 0).astype(jnp.int32)


def draw_vectors(key, part):
    gain_key, shift_key = jax.random.split(jax.random.fold_in(key, 23))
    gains = 1.0 + 0.2 * jax.random.normal(gain_key, (8, D), jnp.float32)
    shifts = 0.4 * jax.random.normal(shift_key, (8, D), jnp.float32)
    row_ids = jnp.arange(8)[:, None]
    is_gain = (row_ids == 0) | (row_ids == 5)
    is_small = (row_ids == 1) | (row_ids == 3) | (row_ids == 6)
    shifts = jnp.where(is_small, 0.125 * shifts, shifts)
    return jnp.clip(jnp.where(is_gain, gains, shifts), -3.0, 3.0).astype(jnp.float32)


def raised(result, stream_key, source, target, blocks, factor):
    owner, partner = [(jnp.arange(result.shape[position]) // (result.shape[position] // blocks)).reshape([-1 if axis == position else 1 for axis in range(result.ndim)]) for position in (source, target)]
    chosen = jax.random.permutation(stream_key, blocks)[partner]
    strong = (owner == chosen) | (owner == (partner + blocks // 2) % blocks)
    return jnp.where(strong, factor * result, result)


def steps_of(key, extent, cuts, least, largest):
    loudness, own = 1.0, jax.random.fold_in(key, 6)
    for position, parts in cuts:
        steps = jnp.exp(jax.random.uniform(jax.random.fold_in(own, position), (parts,), jnp.float32, least / len(cuts), largest / len(cuts)))
        loudness = loudness * jnp.repeat(steps, extent[position] // parts).reshape([-1 if axis == position else 1 for axis in range(len(extent))])
    return loudness


def normal_values(rng, dims, scale, bound, shards=(), dtype=jnp.bfloat16):
    result = scale * jax.random.normal(rng, dims, jnp.float32)
    if shards:
        result = result * steps_of(rng, dims, shards, -0.22, 0.18)
    return jnp.clip(result, -bound, bound).astype(dtype)


def bell_draw_with(rng, dims, deviation, most, cuts, heavy, held_as=jnp.bfloat16):
    entries = deviation * jax.random.normal(rng, dims, jnp.float32)
    if cuts:
        entries = entries * steps_of(rng, dims, cuts, -0.22, 0.18)
    return jnp.clip(raised(entries, jax.random.fold_in(rng, 3), *heavy), -most, most).astype(held_as)


def setup_inputs(seed: int = 0) -> dict:
    arg_keys = jax.random.split(jax.random.key(seed), 13)
    return {
        "tokens": bell_draw_with(arg_keys[0], (TOKENS, D), 1.0, 6.0, ((0, 32),), (0, 1, 32, 2.75)),
        "keep_mask": draw_keep_mask(jax.random.fold_in(arg_keys[12], 71), 0),
        "w_qkv": normal_values(arg_keys[2], (D, 3 * D), (D // 2) ** -0.5, 0.3125),
        "w_out": normal_values(arg_keys[3], (D, D), (D // 2) ** -0.5, 0.3125),
        "w_up": normal_values(arg_keys[4], (D, FF), (D // 4) ** -0.5, 0.4375),
        "w_down": normal_values(arg_keys[5], (FF, D), FF ** -0.5, 0.109375),
        "vectors": draw_vectors(jax.random.fold_in(arg_keys[12], 71), 0),
        "up_bias": normal_values(arg_keys[7], (FF,), 0.5, 3.0, (), jnp.float32),
        "w_proj": normal_values(arg_keys[8], (D, EMB), D ** -0.5, 0.21875),
        "texts": normal_values(arg_keys[9], (IMAGES, EMB), 0.044, 0.29882812, ((0, 32),)),
        "pair_index": jax.random.permutation(arg_keys[10], IMAGES).astype(jnp.int32),
        "logit_scale": jnp.clip(jax.random.uniform(arg_keys[11], (1,), jnp.float32, 30.0, 60.0), 30.0, 60.0),
    }


@jax.custom_vjp
def low(v):
    return lax.optimization_barrier(v.astype(jnp.bfloat16)).astype(jnp.float32)

@jax.custom_vjp
def low_back(v):
    return v

def low_keep(v):
    return (low(v), None)

def low_pass(kept, grad):
    return (grad,)

def back_keep(v):
    return (v, None)

def back_low(kept, grad):
    return (low(grad),)
low.defvjp(low_keep, low_pass)
low_back.defvjp(back_keep, back_low)

def matmul_high(left, right):
    return jnp.matmul(left, right, precision=lax.Precision.HIGHEST)

def layer_norm(values, gain, shift):
    mean_val = lax.optimization_barrier(jnp.mean(values, axis=-1, keepdims=True))
    centred = values - mean_val
    spread = lax.optimization_barrier(jnp.mean(centred * centred, axis=-1, keepdims=True))
    return centred * lax.rsqrt(spread + 1e-06) * gain + shift

def encoder_block(inputs, keep, w_qkv, w_out, w_up, w_down, vectors, up_bias):
    group_size = inputs.shape[0]
    normed = low(layer_norm(inputs, vectors[0], vectors[1]))
    projected = matmul_high(normed, w_qkv)
    queries = low(low_back(projected[..., :D] + vectors[2]))
    key_rows = low(low_back(projected[..., D:2 * D]))
    value_rows = low(low_back(projected[..., 2 * D:] + vectors[3]))
    head_shape = (group_size, SEQ, HEADS, HEAD_DIM)
    queries = queries.reshape(head_shape)
    key_rows = key_rows.reshape(head_shape)
    value_rows = value_rows.reshape(head_shape)
    raw = jnp.einsum('gqhd,gkhd->ghqk', queries, key_rows, precision=lax.Precision.HIGHEST)
    allowed = keep[:, None, None, :] > 0
    scores = low_back(jnp.where(allowed, raw * HEAD_DIM ** (-0.5), -1e+30))
    probs = jax.nn.softmax(scores, axis=-1)
    probs_low = low(probs)
    attended = jnp.einsum('ghqk,gkhd->gqhd', probs_low, value_rows, precision=lax.Precision.HIGHEST)
    attended = low(low_back(attended.reshape(group_size, SEQ, D)))
    branch = low_back(matmul_high(attended, w_out) + vectors[4])
    resid = inputs + branch
    normed_two = low(layer_norm(resid, vectors[5], vectors[6]))
    hidden = low_back(matmul_high(normed_two, w_up) + up_bias)
    activ = low(jax.nn.gelu(hidden, approximate=False))
    mlp_out = low_back(matmul_high(activ, w_down) + vectors[7])
    outputs = resid + mlp_out
    keep_float = keep.astype(jnp.float32)
    pooled = lax.optimization_barrier(jnp.sum(outputs * keep_float[:, :, None], axis=1))
    return pooled / lax.optimization_barrier(jnp.sum(keep_float, axis=1))[:, None]

def contrastive(pooled, w_proj, texts, pair_index, logit_scale):
    latent = matmul_high(pooled, w_proj)
    embeds = latent * lax.rsqrt(lax.optimization_barrier(jnp.sum(latent * latent, axis=-1, keepdims=True)) + 1e-06)
    sent = low(embeds)
    logits = logit_scale[0] * matmul_high(sent, texts.T)
    row_lse = jax.nn.logsumexp(logits, axis=1)
    col_lse = jax.nn.logsumexp(logits, axis=0)
    positives = jnp.take_along_axis(logits, pair_index[:, None], axis=1)
    return 0.5 * (jnp.sum(row_lse) + jnp.sum(col_lse)) - jnp.sum(positives)

def reference(tokens, keep_mask, w_qkv, w_out, w_up, w_down, vectors, up_bias, w_proj, texts, pair_index, logit_scale):
    group_size = 16
    block_count = IMAGES // group_size
    masks = keep_mask.reshape(block_count, group_size, SEQ)
    floats = (tokens.astype(jnp.float32), w_qkv.astype(jnp.float32), w_out.astype(jnp.float32), w_up.astype(jnp.float32), w_down.astype(jnp.float32), vectors.astype(jnp.float32), up_bias.astype(jnp.float32), w_proj.astype(jnp.float32), texts.astype(jnp.float32))

    def total(tok_all, wq_all, wo_all, wu_all, wd_all, vec_all, ub_all, wp_all, txt_all):
        images = tok_all.reshape(block_count, group_size, SEQ, D)

        def one_group(inputs, keep):
            return encoder_block(inputs, keep, wq_all, wo_all, wu_all, wd_all, vec_all, ub_all)
        checked = jax.checkpoint(one_group)

        def scan_step(carry, item):
            return (carry, checked(item[0], item[1]))
        _, pooled = lax.scan(scan_step, None, (images, masks))
        pooled = pooled.reshape(IMAGES, D)
        return contrastive(pooled, wp_all, txt_all, pair_index, logit_scale)
    summed, pullback = jax.vjp(total, *floats)
    grads = pullback(jnp.ones_like(summed))
    loss = (summed / IMAGES).reshape(1)
    return (loss, grads[0], grads[1], grads[2], grads[3], grads[4], grads[5], grads[6], grads[7], grads[8])
```

```python
from functools import partial

import jax
import jax.numpy as jnp
from jax import lax
from jax.sharding import PartitionSpec as P

D = 768
HEADS = 12
HEAD_DIM = 64
SEQ = 197


HIGH = lax.Precision.HIGHEST


def norm_forward(values, gain, shift):
    mean_val = jnp.mean(values, axis=-1, keepdims=True)
    centred = values - mean_val
    inv_std = lax.rsqrt(jnp.mean(centred * centred, axis=-1, keepdims=True) + 1e-06)
    scaled = centred * inv_std
    return (scaled * gain + shift, scaled, inv_std)


def norm_backward(grad_in, scaled, inv_std, gain):
    weighted = grad_in * gain
    inner = weighted - jnp.mean(weighted, axis=-1, keepdims=True)
    inner = inner - scaled * jnp.mean(weighted * scaled, axis=-1, keepdims=True)
    return (inner * inv_std, jnp.sum(grad_in * scaled, axis=0), jnp.sum(grad_in, axis=0))


def per_device(
    tokens,
    keep_mask,
    w_qkv,
    w_out,
    w_up,
    w_down,
    vectors,
    up_bias,
    w_proj,
    texts,
    pair_index,
    logit_scale,
):
    images = keep_mask.shape[0]
    rows = tokens.shape[0]
    total_images = pair_index.shape[0]
    scale_qk = HEAD_DIM ** (-0.5)
    head_shape = (images, SEQ, HEADS, HEAD_DIM)
    inputs = tokens.astype(jnp.float32)
    keep_float = keep_mask.astype(jnp.float32)
    normed, scaled_one, inv_one = norm_forward(inputs, vectors[0], vectors[1])
    normed_b = normed.astype(jnp.bfloat16)
    projected = jnp.dot(normed_b, w_qkv, preferred_element_type=jnp.float32)
    queries = (projected[:, :D] + vectors[2]).astype(jnp.bfloat16).reshape(head_shape)
    key_rows = projected[:, D : 2 * D].astype(jnp.bfloat16).reshape(head_shape)
    value_rows = (projected[:, 2 * D :] + vectors[3]).astype(jnp.bfloat16).reshape(head_shape)
    raw = jnp.einsum("nqhd,nkhd->nhqk", queries, key_rows, preferred_element_type=jnp.float32)
    allowed = keep_mask[:, None, None, :] > 0
    scores = jnp.where(allowed, raw * scale_qk, -1e30)
    probs = jax.nn.softmax(scores, axis=-1)
    probs_b = probs.astype(jnp.bfloat16)
    attended = jnp.einsum(
        "nhqk,nkhd->nqhd", probs_b, value_rows, preferred_element_type=jnp.float32
    )
    attended = attended.reshape(rows, D).astype(jnp.bfloat16)
    resid = inputs + jnp.dot(attended, w_out, preferred_element_type=jnp.float32) + vectors[4]
    normed_two, scaled_two, inv_two = norm_forward(resid, vectors[5], vectors[6])
    normed_two_b = normed_two.astype(jnp.bfloat16)
    hidden = jnp.dot(normed_two_b, w_up, preferred_element_type=jnp.float32) + up_bias
    activ_b = jax.nn.gelu(hidden, approximate=False).astype(jnp.bfloat16)
    counts = jnp.sum(keep_float, axis=1)
    activ_sum = jnp.einsum(
        "nsf,ns->nf",
        activ_b.reshape(images, SEQ, -1),
        keep_mask.astype(jnp.bfloat16),
        preferred_element_type=jnp.float32,
    )
    resid_sum = jnp.sum(resid.reshape(images, SEQ, D) * keep_float[:, :, None], axis=1)
    pooled_sum = resid_sum + jnp.dot(activ_sum, w_down.astype(jnp.float32), precision=HIGH)
    pooled = pooled_sum / counts[:, None] + vectors[7]
    sent = jnp.concatenate([pooled, jnp.broadcast_to(counts[:, None], (images, 128))], axis=1)
    gathered = lax.all_gather(sent, ("row", "col"), axis=0, tiled=True)
    all_texts = lax.all_gather(texts, ("row", "col"), axis=0, tiled=True).astype(jnp.float32)
    pooled_all, counts_all = gathered[:, :D], gathered[:, D : D + 1]
    proj_float = w_proj.astype(jnp.float32)
    latent = jnp.dot(pooled_all, proj_float, precision=HIGH)
    inv_norm = lax.rsqrt(jnp.sum(latent * latent, axis=-1, keepdims=True) + 1e-06)
    embeds = latent * inv_norm
    embeds_f = embeds.astype(jnp.bfloat16).astype(jnp.float32)
    logit_mult = logit_scale[0]
    first_image = lax.axis_index(("row", "col")) * images
    all_ids = jnp.arange(total_images, dtype=jnp.int32)
    match = (pair_index[:, None] == all_ids[None, :]).astype(jnp.float32)
    logits = logit_mult * jnp.dot(
        embeds_f.astype(jnp.bfloat16), all_texts.astype(jnp.bfloat16).T,
        preferred_element_type=jnp.float32,
    )
    row_lse = jax.nn.logsumexp(logits, axis=1)
    col_lse = jax.nn.logsumexp(logits, axis=0)
    summed = 0.5 * (jnp.sum(row_lse) + jnp.sum(col_lse)) - jnp.sum(logits * match)
    grad_logits = (
        0.5 * jnp.exp(logits - row_lse[:, None]) + 0.5 * jnp.exp(logits - col_lse[None, :]) - match
    )
    embed_grad = logit_mult * jnp.dot(grad_logits, all_texts, precision=HIGH)
    own_cols = lax.dynamic_slice_in_dim(grad_logits, first_image, images, axis=1)
    text_grad = logit_mult * jnp.dot(own_cols.T, embeds_f, precision=HIGH)
    grad_latent = inv_norm * (
        embed_grad - embeds * jnp.sum(embeds * embed_grad, axis=-1, keepdims=True)
    )
    shards = lax.axis_size("col")
    mine = lax.axis_index("col")
    own_pooled = lax.dynamic_slice_in_dim(pooled_all, mine * (D // shards), D // shards, axis=1)
    grad_proj = jnp.dot(own_pooled.T, grad_latent, precision=HIGH)
    grad_pooled = jnp.dot(grad_latent, proj_float.T, precision=HIGH)
    image_grads = (grad_pooled / counts_all).astype(jnp.bfloat16)
    ff = w_up.shape[1]
    pieces = activ_sum.reshape(images, shards, ff // shards).transpose(1, 0, 2)
    pieces = lax.all_to_all(pieces, "col", split_axis=0, concat_axis=0, tiled=True)
    pieces = pieces.reshape(images * shards, ff // shards)
    pieces = lax.all_gather(pieces, "row", axis=0, tiled=True)
    grad_down = jnp.dot(pieces.T, image_grads.astype(jnp.float32), precision=HIGH)
    own_grads = lax.dynamic_slice_in_dim(grad_pooled / counts_all, first_image, images)
    own_rounded = own_grads.astype(jnp.bfloat16)
    grad_outputs = (keep_float[:, :, None] * own_grads[:, None, :]).reshape(rows, D)
    grad_down_bias = jnp.sum(counts[:, None] * own_rounded.astype(jnp.float32), axis=0)
    image_activ = jnp.dot(own_rounded, w_down.T, preferred_element_type=jnp.float32)
    grad_activ = (keep_float[:, :, None] * image_activ[:, None, :]).reshape(rows, ff)
    _, gelu_pull = jax.vjp(partial(jax.nn.gelu, approximate=False), hidden)
    grad_hidden = gelu_pull(grad_activ)[0].astype(jnp.bfloat16)
    grad_up = jnp.dot(normed_two_b.T, grad_hidden, preferred_element_type=jnp.float32)
    grad_up_bias = jnp.sum(grad_hidden.astype(jnp.float32), axis=0)
    grad_normed_two = jnp.dot(grad_hidden, w_up.T, preferred_element_type=jnp.float32)
    back_two, gain_two, shift_two = norm_backward(grad_normed_two, scaled_two, inv_two, vectors[5])
    grad_resid = grad_outputs + back_two
    grad_branch = grad_resid.astype(jnp.bfloat16)
    grad_out = jnp.dot(attended.T, grad_branch, preferred_element_type=jnp.float32)
    grad_out_bias = jnp.sum(grad_branch.astype(jnp.float32), axis=0)
    grad_attended = jnp.dot(grad_branch, w_out.T, preferred_element_type=jnp.float32)
    grad_attended = grad_attended.astype(jnp.bfloat16).reshape(head_shape)
    grad_values = jnp.einsum(
        "nhqk,nqhd->nkhd", probs_b, grad_attended, preferred_element_type=jnp.float32
    ).astype(jnp.bfloat16)
    grad_probs = jnp.einsum(
        "nqhd,nkhd->nhqk", grad_attended, value_rows, preferred_element_type=jnp.float32
    )
    grad_scores = probs * (grad_probs - jnp.sum(probs * grad_probs, axis=-1, keepdims=True))
    grad_scores = grad_scores.astype(jnp.bfloat16)
    grad_queries = jnp.einsum(
        "nhqk,nkhd->nqhd", grad_scores, key_rows, preferred_element_type=jnp.float32
    )
    grad_queries = (grad_queries * scale_qk).astype(jnp.bfloat16).reshape(rows, D)
    grad_keys = jnp.einsum(
        "nhqk,nqhd->nkhd", grad_scores, queries, preferred_element_type=jnp.float32
    )
    grad_keys = (grad_keys * scale_qk).astype(jnp.bfloat16).reshape(rows, D)
    grad_values = grad_values.reshape(rows, D)
    grad_projected = jnp.concatenate([grad_queries, grad_keys, grad_values], axis=1)
    grad_qkv = jnp.dot(normed_b.T, grad_projected, preferred_element_type=jnp.float32)
    grad_normed = jnp.dot(grad_projected, w_qkv.T, preferred_element_type=jnp.float32)
    back_one, gain_one, shift_one = norm_backward(grad_normed, scaled_one, inv_one, vectors[0])
    token_grad = grad_resid + back_one
    grad_vectors = jnp.stack(
        [
            gain_one,
            shift_one,
            jnp.sum(grad_queries.astype(jnp.float32), axis=0),
            jnp.sum(grad_values.astype(jnp.float32), axis=0),
            grad_out_bias,
            gain_two,
            shift_two,
            grad_down_bias,
        ],
        axis=1,
    )
    wide = [grad_qkv, grad_out, grad_up, grad_vectors, grad_up_bias]
    shares = []
    for grad in wide:
        part = lax.psum_scatter(
            grad.astype(jnp.bfloat16), "col", scatter_dimension=0, tiled=True
        )
        shares.append(lax.psum(part, "row").astype(jnp.float32))
    loss = (summed / total_images).reshape(1)
    return (
        loss,
        token_grad,
        shares[0],
        shares[1],
        shares[2],
        grad_down,
        shares[3].T,
        shares[4],
        grad_proj,
        text_grad,
    )


def solution(mesh):
    in_specs = (
        P(("row", "col"), None),
        P(("row", "col"), None),
        P(),
        P(),
        P(),
        P(),
        P(),
        P(),
        P(),
        P(("row", "col"), None),
        P(),
        P(),
    )
    out_specs = (
        P(),
        P(("row", "col"), None),
        P("col", None),
        P("col", None),
        P("col", None),
        P("col", None),
        P(None, "col"),
        P("col"),
        P("col", None),
        P(("row", "col"), None),
    )
    return jax.shard_map(
        per_device, mesh=mesh, in_specs=in_specs, out_specs=out_specs, check_vma=False
    )
```

```python
import functools

import jax
import jax.numpy as jnp
from jax import lax
from jax.experimental import pallas as pl
from jax.experimental.pallas import tpu as pltpu
from jax.sharding import PartitionSpec as P

HIGH = lax.Precision.HIGHEST

D = 768
HEADS = 12
HEAD_DIM = 64
SEQ = 197
ROWS = 208
WIN = 256
TILE = 256
F32 = jnp.float32
BF = jnp.bfloat16
NT = (((1,), (1,)), ((), ()))
TN = (((0,), (0,)), ((), ()))


def mm(a, b, dims=(((1,), (0,)), ((), ()))):
    return lax.dot_general(a, b, dims, preferred_element_type=F32)


def head_masks():
    lane = lax.broadcasted_iota(jnp.int32, (1, TILE), 1) // HEAD_DIM
    return [(lane == h).astype(F32).astype(BF) for h in range(TILE // HEAD_DIM)]


def gelu_pair(u):
    z = jnp.abs(u)
    t = 1.0 / (1.0 + (0.3275911 * 0.7071067811865476) * z)
    e = jnp.exp(-0.5 * (u * u))
    poly = 0.5 * 1.061405429
    for c in (-1.453152027, 1.421413741, -0.284496736, 0.254829592):
        poly = poly * t + 0.5 * c
    tail = poly * t * e
    cdf = jnp.where(u >= 0.0, 1.0 - tail, tail)
    return u * cdf, cdf + (0.3989422804014327 * u) * e


def forward_kernel(
    images, ff,
    tok_ref, keep_ref, wqkv_h, wout_h, wup_h, wdown_h, vec_ref, upb_ref,
    h1_h, qkv_h, p_h, o_h, h2_h, xh2_h, rstd_h, gk_h, apool_ref, pooled_ref,
    wqkv, wout, wup, wdown, xs, h1, qkv, p_s, o_s, h2, xh2, rstd, gk, a_s, keep8, kmask, kcol, bias, acc,
    in_sem, out_sem,
):
    n_quads = D // TILE
    n_ff = ff // TILE
    loads = []
    for k, (src, dst) in enumerate(((wqkv_h, wqkv), (wout_h, wout), (wup_h, wup), (wdown_h, wdown))):
        c = pltpu.make_async_copy(src, dst, in_sem.at[k])
        c.start()
        loads.append(c)
    stores = []

    def send(k, src, dst):
        c = pltpu.make_async_copy(src, dst, out_sem.at[k])
        c.start()
        stores.append(c)

    total = images * SEQ
    last = total // 16 * 16
    xs[last:, :] = jnp.zeros_like(xs[last:, :])
    xs[0:last, :] = tok_ref[0:last, :].astype(F32)
    if last < total:
        xs[last:total, :] = tok_ref[last:total, :].astype(F32)
    keep8[...] = jnp.zeros_like(keep8)
    keep8[0:images, 0:SEQ] = keep_ref[...].astype(F32)
    kb = keep8[...]
    rid = lax.broadcasted_iota(jnp.int32, kb.shape, 0)
    for i in range(images):
        kmask[i] = jnp.where(rid == i, kb, 0.0).astype(BF)
        one = jnp.ones((kb.shape[0], 128), F32).astype(BF)
        kcol[i * ROWS:(i + 1) * ROWS, :] = mm(kmask[i], one, TN)[0:ROWS]
    bias[0:1, 0:D] = vec_ref[2:3, :]
    bias[0:1, D:2 * D] = jnp.zeros((1, D), F32)
    bias[0:1, 2 * D:] = vec_ref[3:4, :]
    for i in range(images):
        x = xs[i * SEQ:i * SEQ + ROWS, :]
        cen = x - jnp.mean(x, axis=1, keepdims=True)
        inv = lax.rsqrt(jnp.mean(cen * cen, axis=1, keepdims=True) + 1e-6)
        h1[i * ROWS:(i + 1) * ROWS, :] = (cen * inv * vec_ref[0:1, :] + vec_ref[1:2, :]).astype(BF)
    send(0, h1, h1_h)
    loads[0].wait()
    span = images * ROWS
    pad = qkv.shape[1] - span
    for t in range(3 * n_quads):
        qkv[t, span:, :] = jnp.zeros((pad, TILE), BF)

    def proj(t, _):
        col = pl.multiple_of(t * TILE, TILE)
        r = mm(h1[...], wqkv[:, pl.ds(col, TILE)]) + bias[0:1, pl.ds(col, TILE)]
        r = r * jnp.where(t < n_quads, HEAD_DIM ** -0.5, 1.0)
        qkv[t, 0:span, :] = r.astype(BF)
        return 0

    lax.fori_loop(0, 3 * n_quads, proj, 0)
    send(1, qkv, qkv_h)
    masks = head_masks()

    def attend(it, _):
        i = it // n_quads
        j = it % n_quads
        r0 = pl.multiple_of(i * ROWS, 16)
        q4 = qkv[j, pl.ds(r0, ROWS), :]
        k4 = qkv[n_quads + j, pl.ds(r0, WIN), :]
        v4 = qkv[2 * n_quads + j, pl.ds(r0, WIN), :]
        valid = keep8[pl.ds(i, 1), :] > 0.0
        out = jnp.zeros((ROWS, TILE), F32)
        for h, m in enumerate(masks):
            s = mm(q4 * m, k4, NT)
            s = jnp.where(valid, s, -1e30)
            e = jnp.exp(s - jnp.max(s, axis=1, keepdims=True))
            pb = (e * (1.0 / jnp.sum(e, axis=1, keepdims=True))).astype(BF)
            p_s[it, h * ROWS:(h + 1) * ROWS, :] = pb
            out = out + mm(pb, v4 * m)
        o_s[j, pl.ds(r0, ROWS), :] = out.astype(BF)
        return 0

    lax.fori_loop(0, images * n_quads, attend, 0)
    send(2, p_s, p_h)
    send(3, o_s, o_h)
    loads[1].wait()
    pooled_ref[...] = jnp.zeros_like(pooled_ref)
    for i in range(images):
        rows = slice(i * ROWS, (i + 1) * ROWS)
        x = xs[i * SEQ:i * SEQ + ROWS, :]
        y = x + vec_ref[4:5, :]
        for j in range(n_quads):
            y = y + mm(o_s[j, rows, :], wout[j * TILE:(j + 1) * TILE, :])
        kc = kcol[rows, 0:1]
        pooled_ref[i:i + 1, 0:D] = jnp.sum(y * kc, axis=0, keepdims=True)
        cen = y - jnp.mean(y, axis=1, keepdims=True)
        inv = lax.rsqrt(jnp.mean(cen * cen, axis=1, keepdims=True) + 1e-6)
        xh = cen * inv
        xh2[rows, :] = xh.astype(BF)
        rstd[rows, :] = jnp.broadcast_to(inv, (ROWS, 128))
        h2[rows, :] = (xh * vec_ref[5:6, :] + vec_ref[6:7, :]).astype(BF)
    send(4, h2, h2_h)
    send(5, xh2, xh2_h)
    send(6, rstd, rstd_h)
    loads[2].wait()
    loads[3].wait()
    acc[...] = jnp.zeros_like(acc)
    a_s[span:, :] = jnp.zeros((a_s.shape[0] - span, TILE), BF)

    def feed(t, _):
        col = pl.multiple_of(t * TILE, TILE)
        ub = upb_ref[0:1, pl.ds(col, TILE)]
        for i in range(images):
            rows = slice(i * ROWS, (i + 1) * ROWS)
            u = mm(h2[rows, :], wup[:, pl.ds(col, TILE)]) + ub
            a, g = gelu_pair(u)
            a_s[rows, :] = a.astype(BF)
            gk[t, rows, :] = (g * kcol[rows, 0:1]).astype(BF)
        ap = jnp.zeros((kmask.shape[1], TILE), F32)
        for i in range(images):
            ap = ap + mm(kmask[i], a_s[i * ROWS:i * ROWS + WIN, :])
        apool_ref[t] = ap
        hi = ap.astype(BF)
        lo = (ap - hi.astype(F32)).astype(BF)
        w = wdown[pl.ds(col, TILE), :]
        acc[...] += mm(hi, w) + mm(lo, w)
        pltpu.make_async_copy(gk.at[t], gk_h.at[t], out_sem.at[7]).start()
        return 0

    lax.fori_loop(0, n_ff, feed, 0)
    cnt = jnp.sum(kb, axis=1, keepdims=True)[0:8]
    inv = 1.0 / jnp.maximum(cnt, 1.0)
    pooled_ref[:, 0:D] = (pooled_ref[:, 0:D] + acc[0:8, :]) * inv + vec_ref[7:8, :]
    pooled_ref[:, D:] = jnp.broadcast_to(cnt, (8, 128))
    for c in stores:
        c.wait()
    for t in range(n_ff):
        pltpu.make_async_copy(gk.at[t], gk_h.at[t], out_sem.at[7]).wait()


def forward_call(images, ff, tokens, keep, wqkv, wout, wup, wdown, vec, upb):
    span = images * ROWS
    nq = D // TILE
    wide = span + WIN - ROWS
    outs = [
        ((span, D), BF), ((3 * nq, wide, TILE), BF), ((images * nq, 4 * ROWS, TILE), BF),
        ((nq, span, TILE), BF), ((span, D), BF), ((span, D), BF), ((span, 128), F32),
        ((ff // TILE, span, TILE), BF), ((ff // TILE, 16, TILE), F32), ((8, D + 128), F32),
    ]
    anyspec = pl.BlockSpec(memory_space=pl.ANY)
    vm = pl.BlockSpec(memory_space=pltpu.VMEM)
    scratch = [
        pltpu.VMEM((D, 3 * D), BF), pltpu.VMEM((D, D), BF), pltpu.VMEM((D, ff), BF), pltpu.VMEM((ff, D), BF),
        pltpu.VMEM(((images - 1) * SEQ + ROWS + 7 & -8, D), F32),
    ] + [pltpu.VMEM(*o) for o in outs[:8]] + [
        pltpu.VMEM((wide, TILE), BF), pltpu.VMEM((16, WIN), F32), pltpu.VMEM((images, 16, WIN), BF),
        pltpu.VMEM((span, 128), F32), pltpu.VMEM((1, 3 * D), F32), pltpu.VMEM((16, D), F32),
        pltpu.SemaphoreType.DMA((4,)), pltpu.SemaphoreType.DMA((8,)),
    ]
    return pl.pallas_call(
        functools.partial(forward_kernel, images, ff),
        out_shape=[jax.ShapeDtypeStruct(s, d) for s, d in outs],
        in_specs=[vm, vm] + [anyspec] * 4 + [vm, vm],
        out_specs=[anyspec] * 8 + [vm, vm],
        scratch_shapes=scratch,
        compiler_params=pltpu.CompilerParams(vmem_limit_bytes=60 * 2**20),
        name="block_forward",
    )(tokens, keep, wqkv, wout, wup, wdown, vec, upb)


def backward_kernel(
    images, ff,
    tok_ref, keep_ref, dy_ref, vec_ref,
    wqkv_h, wout_h, wup_h, wdown_h, h1_h, qkv_h, p_h, o_h, h2_h, xh2_h, rstd_h, gk_h,
    tg_ref, g_ref, vg_ref, ub_ref,
    wqkv, wout, wup, wdown, h1, qkv, p_s, o_s, h2, xh2, rstd, du,
    xs, dx, db, do_s, dp_s, h1t, h2t, keep8, kcol, da_s,
    in_sem, gk_sem, p_sem,
):
    n_quads = D // TILE
    n_ff = ff // TILE
    span = images * ROWS
    masks = head_masks()
    loads = {}
    for k, (name, src, dst) in enumerate((
        ("wdown", wdown_h, wdown), ("h2", h2_h, h2), ("wup", wup_h, wup), ("xh2", xh2_h, xh2),
        ("rstd", rstd_h, rstd), ("wout", wout_h, wout), ("o", o_h, o_s), ("qkv", qkv_h, qkv),
        ("h1", h1_h, h1), ("wqkv", wqkv_h, wqkv),
    )):
        loads[name] = pltpu.make_async_copy(src, dst, in_sem.at[k])
    for name in ("wdown", "h2"):
        loads[name].start()
    gks = []
    for t in range(n_ff):
        c = pltpu.make_async_copy(gk_h.at[t], du.at[:, t * TILE:(t + 1) * TILE], gk_sem.at[t])
        c.start()
        gks.append(c)
    for name in ("wup", "xh2", "rstd", "wout", "o", "qkv", "h1", "wqkv"):
        loads[name].start()

    def pcopy(i, j, slot):
        return pltpu.make_async_copy(p_h.at[i * n_quads + j], p_s.at[slot], p_sem.at[slot])

    pcopy(0, 0, 0).start()

    total = images * SEQ
    last = total // 16 * 16
    xs[last:, :] = jnp.zeros_like(xs[last:, :])
    xs[0:last, :] = tok_ref[0:last, :].astype(F32)
    if last < total:
        xs[last:total, :] = tok_ref[last:total, :].astype(F32)
    keep8[...] = jnp.zeros_like(keep8)
    keep8[0:images, 0:SEQ] = keep_ref[...].astype(F32)
    kb = keep8[...]
    rid = lax.broadcasted_iota(jnp.int32, kb.shape, 0)
    one = jnp.ones((kb.shape[0], 128), F32).astype(BF)
    for i in range(images):
        km = jnp.where(rid == i, kb, 0.0).astype(BF)
        kcol[i * ROWS:(i + 1) * ROWS, :] = mm(km, one, TN)[0:ROWS]

    dy = dy_ref[...]
    dyb = dy.astype(BF)
    cnt = jnp.sum(kb, axis=1, keepdims=True)[0:8]
    vg_ref[7:8, :] = jnp.sum(dyb.astype(F32) * cnt, axis=0, keepdims=True)
    dy16 = jnp.concatenate([dyb, jnp.zeros((8, D), BF)], axis=0)
    loads["wdown"].wait()

    def spread(t, _):
        col = pl.multiple_of(t * TILE, TILE)
        da_s[:, pl.ds(col, TILE)] = mm(dy16, wdown[pl.ds(col, TILE), :], NT)
        return 0

    lax.fori_loop(0, n_ff, spread, 0)
    loads["h2"].wait()
    h2t[...] = h2[...].T
    for c in gks:
        c.wait()

    def expand(t, _):
        col = pl.multiple_of(t * TILE, TILE)
        ub = jnp.zeros((1, TILE), F32)
        for i in range(images):
            rows = slice(i * ROWS, (i + 1) * ROWS)
            d = du[rows, pl.ds(col, TILE)].astype(F32) * da_s[i:i + 1, pl.ds(col, TILE)]
            ub = ub + jnp.sum(d, axis=0, keepdims=True)
            du[rows, pl.ds(col, TILE)] = d.astype(BF)
        ub_ref[:, pl.ds(col, TILE)] = ub
        part = mm(h2t[...], du[:, pl.ds(col, TILE)])
        c3 = pl.multiple_of((t % 3) * TILE, TILE)
        g_ref[t // 3, :, pl.ds(c3, TILE)] = part.astype(BF)
        return 0

    lax.fori_loop(0, n_ff, expand, 0)
    loads["wup"].wait()

    def down(n, _):
        col = pl.multiple_of(n * TILE, TILE)
        dx[:, pl.ds(col, TILE)] = mm(du[...], wup[pl.ds(col, TILE), :], NT)
        return 0

    lax.fori_loop(0, n_quads, down, 0)
    for name in ("xh2", "rstd", "wout", "o"):
        loads[name].wait()
    g2 = jnp.zeros((1, D), F32)
    b2 = jnp.zeros((1, D), F32)
    bo = jnp.zeros((1, D), F32)
    for i in range(images):
        rows = slice(i * ROWS, (i + 1) * ROWS)
        dh = dx[rows, :]
        xh = xh2[rows, :].astype(F32)
        g2 = g2 + jnp.sum(dh * xh, axis=0, keepdims=True)
        b2 = b2 + jnp.sum(dh, axis=0, keepdims=True)
        c = dh * vec_ref[5:6, :]
        m1 = jnp.mean(c, axis=1, keepdims=True)
        m2 = jnp.mean(c * xh, axis=1, keepdims=True)
        r = dy[i:i + 1, :] * kcol[rows, 0:1] + rstd[rows, 0:1] * (c - m1 - xh * m2)
        dx[rows, :] = r
        rb = r.astype(BF)
        db[rows, :] = rb
        bo = bo + jnp.sum(rb.astype(F32), axis=0, keepdims=True)
    vg_ref[5:6, :] = g2
    vg_ref[6:7, :] = b2
    vg_ref[4:5, :] = bo
    for j in range(n_quads):
        sl = slice(j * TILE, (j + 1) * TILE)
        do_s[j] = mm(db[...], wout[sl, :], NT).astype(BF)
        for n in range(n_quads):
            g_ref[4, sl, n * TILE:(n + 1) * TILE] = mm(
                o_s[j], db[:, n * TILE:(n + 1) * TILE], TN).astype(BF)
    for name in ("qkv", "h1"):
        loads[name].wait()
    h1t[...] = h1[...].T

    def quad(j, _):
        def attend(i, _):
            r0 = pl.multiple_of(i * ROWS, 16)
            step = j * images + i
            slot = step % 2
            nxt = step + 1

            @pl.when(nxt < n_quads * images)
            def _():
                pcopy(nxt % images, nxt // images, nxt % 2).start()

            pcopy(i, j, slot).wait()
            q4 = qkv[j, pl.ds(r0, ROWS), :]
            k4 = qkv[n_quads + j, pl.ds(r0, WIN), :]
            v4 = qkv[2 * n_quads + j, pl.ds(r0, WIN), :]
            d4 = do_s[j, pl.ds(r0, ROWS), :]
            dq = jnp.zeros((ROWS, TILE), F32)
            dk = jnp.zeros((WIN, TILE), F32)
            dv = jnp.zeros((WIN, TILE), F32)
            for h, m in enumerate(masks):
                pb = p_s[slot, h * ROWS:(h + 1) * ROWS, :]
                dm = d4 * m
                dv = dv + mm(pb, dm, TN)
                dpr = mm(dm, v4, NT)
                pf = pb.astype(F32)
                ds = (pf * (dpr - jnp.sum(pf * dpr, axis=1, keepdims=True))).astype(BF)
                dq = dq + mm(ds, k4 * m)
                dk = dk + mm(ds, q4 * m, TN)
            dq = dq * HEAD_DIM ** -0.5
            for s, val in enumerate((dq, dk[0:ROWS], dv[0:ROWS])):
                col = pl.multiple_of(s * D + j * TILE, TILE)
                dp_s[pl.ds(r0, ROWS), pl.ds(col, TILE)] = val.astype(BF)
            return 0

        lax.fori_loop(0, images, attend, 0)
        for s in range(3):
            col = pl.multiple_of(s * D + j * TILE, TILE)
            g_ref[5 + j, :, s * TILE:(s + 1) * TILE] = mm(h1t[...], dp_s[:, pl.ds(col, TILE)]).astype(BF)
        return 0

    lax.fori_loop(0, n_quads, quad, 0)
    vg_ref[2:3, :] = jnp.sum(dp_s[:, 0:D].astype(F32), axis=0, keepdims=True)
    vg_ref[3:4, :] = jnp.sum(dp_s[:, 2 * D:].astype(F32), axis=0, keepdims=True)
    loads["wqkv"].wait()
    g1 = jnp.zeros((1, D), F32)
    b1 = jnp.zeros((1, D), F32)
    for i in range(images):
        rows = slice(i * ROWS, (i + 1) * ROWS)
        dh = mm(dp_s[rows, :], wqkv[...], NT)
        x = xs[i * SEQ:i * SEQ + ROWS, :]
        cen = x - jnp.mean(x, axis=1, keepdims=True)
        inv = lax.rsqrt(jnp.mean(cen * cen, axis=1, keepdims=True) + 1e-6)
        xh = cen * inv
        g1 = g1 + jnp.sum(dh * xh, axis=0, keepdims=True)
        b1 = b1 + jnp.sum(dh, axis=0, keepdims=True)
        c = dh * vec_ref[0:1, :]
        m1 = jnp.mean(c, axis=1, keepdims=True)
        m2 = jnp.mean(c * xh, axis=1, keepdims=True)
        r = dx[rows, :] + inv * (c - m1 - xh * m2)
        tg_ref[i * SEQ:(i + 1) * SEQ, :] = r[0:SEQ]
    vg_ref[0:1, :] = g1
    vg_ref[1:2, :] = b1


def backward_call(images, ff, tokens, keep, dy, vec, wqkv, wout, wup, wdown, acts):
    span = images * ROWS
    nq = D // TILE
    wide = span + WIN - ROWS
    anyspec = pl.BlockSpec(memory_space=pl.ANY)
    vm = pl.BlockSpec(memory_space=pltpu.VMEM)
    outs = [((images * SEQ, D), F32), ((ff // D + 4, D, D), BF), ((8, D), F32), ((1, ff), F32)]
    scratch = [
        pltpu.VMEM((D, 3 * D), BF), pltpu.VMEM((D, D), BF), pltpu.VMEM((D, ff), BF), pltpu.VMEM((ff, D), BF),
        pltpu.VMEM((span, D), BF), pltpu.VMEM((3 * nq, wide, TILE), BF), pltpu.VMEM((2, 4 * ROWS, TILE), BF),
        pltpu.VMEM((nq, span, TILE), BF), pltpu.VMEM((span, D), BF), pltpu.VMEM((span, D), BF),
        pltpu.VMEM((span, 128), F32), pltpu.VMEM((span, ff), BF),
        pltpu.VMEM(((images - 1) * SEQ + ROWS + 7 & -8, D), F32), pltpu.VMEM((span, D), F32),
        pltpu.VMEM((span, D), BF), pltpu.VMEM((nq, span, TILE), BF), pltpu.VMEM((span, 3 * D), BF),
        pltpu.VMEM((D, span), BF), pltpu.VMEM((D, span), BF), pltpu.VMEM((16, WIN), F32),
        pltpu.VMEM((span, 128), F32), pltpu.VMEM((16, ff), F32),
        pltpu.SemaphoreType.DMA((10,)), pltpu.SemaphoreType.DMA((ff // TILE,)), pltpu.SemaphoreType.DMA((2,)),
    ]
    return pl.pallas_call(
        functools.partial(backward_kernel, images, ff),
        out_shape=[jax.ShapeDtypeStruct(s, d) for s, d in outs],
        in_specs=[vm] * 4 + [anyspec] * 12,
        out_specs=[vm] * 4,
        scratch_shapes=scratch,
        compiler_params=pltpu.CompilerParams(vmem_limit_bytes=62 * 2**20),
        name="block_backward",
    )(tokens, keep, dy, vec, wqkv, wout, wup, wdown, *acts)


def per_device(
    tokens,
    keep_mask,
    w_qkv,
    w_out,
    w_up,
    w_down,
    vectors,
    up_bias,
    w_proj,
    texts,
    pair_index,
    logit_scale,
):
    images = keep_mask.shape[0]
    rows = tokens.shape[0]
    total_images = pair_index.shape[0]
    ff = w_up.shape[1]
    acts = forward_call(
        images, ff, tokens, keep_mask, w_qkv, w_out, w_up, w_down, vectors, up_bias.reshape(1, ff)
    )
    activ_sum = acts[8].transpose(1, 0, 2).reshape(16, ff)[:images]
    sent = acts[9][:images]
    gathered = lax.all_gather(sent, ("row", "col"), axis=0, tiled=True)
    all_texts = lax.all_gather(texts, ("row", "col"), axis=0, tiled=True).astype(jnp.float32)
    pooled_all, counts_all = gathered[:, :D], gathered[:, D : D + 1]
    proj_float = w_proj.astype(jnp.float32)
    latent = jnp.dot(pooled_all, proj_float, precision=HIGH)
    inv_norm = lax.rsqrt(jnp.sum(latent * latent, axis=-1, keepdims=True) + 1e-06)
    embeds = latent * inv_norm
    embeds_f = embeds.astype(jnp.bfloat16).astype(jnp.float32)
    logit_mult = logit_scale[0]
    first_image = lax.axis_index(("row", "col")) * images
    all_ids = jnp.arange(total_images, dtype=jnp.int32)
    match = (pair_index[:, None] == all_ids[None, :]).astype(jnp.float32)
    logits = logit_mult * jnp.dot(
        embeds_f.astype(jnp.bfloat16), all_texts.astype(jnp.bfloat16).T,
        preferred_element_type=jnp.float32,
    )
    row_lse = jax.nn.logsumexp(logits, axis=1)
    col_lse = jax.nn.logsumexp(logits, axis=0)
    summed = 0.5 * (jnp.sum(row_lse) + jnp.sum(col_lse)) - jnp.sum(logits * match)
    grad_logits = (
        0.5 * jnp.exp(logits - row_lse[:, None]) + 0.5 * jnp.exp(logits - col_lse[None, :]) - match
    )
    embed_grad = logit_mult * jnp.dot(grad_logits, all_texts, precision=HIGH)
    own_cols = lax.dynamic_slice_in_dim(grad_logits, first_image, images, axis=1)
    text_grad = logit_mult * jnp.dot(own_cols.T, embeds_f, precision=HIGH)
    grad_latent = inv_norm * (
        embed_grad - embeds * jnp.sum(embeds * embed_grad, axis=-1, keepdims=True)
    )
    shards = lax.axis_size("col")
    mine = lax.axis_index("col")
    own_pooled = lax.dynamic_slice_in_dim(pooled_all, mine * (D // shards), D // shards, axis=1)
    grad_proj = jnp.dot(own_pooled.T, grad_latent, precision=HIGH)
    grad_pooled = jnp.dot(grad_latent, proj_float.T, precision=HIGH)
    image_grads = (grad_pooled / counts_all).astype(jnp.bfloat16)
    pieces = activ_sum.reshape(images, shards, ff // shards).transpose(1, 0, 2)
    pieces = lax.all_to_all(pieces, "col", split_axis=0, concat_axis=0, tiled=True)
    pieces = pieces.reshape(images * shards, ff // shards)
    pieces = lax.all_gather(pieces, "row", axis=0, tiled=True)
    grad_down = jnp.dot(pieces.T, image_grads.astype(jnp.float32), precision=HIGH)
    own_grads = lax.dynamic_slice_in_dim(grad_pooled / counts_all, first_image, images)
    dy = jnp.concatenate([own_grads, jnp.zeros((8 - images, D), jnp.float32)], axis=0)
    token_grad, grads, grad_vectors, grad_up_bias = backward_call(
        images, ff, tokens, keep_mask, dy, vectors, w_qkv, w_out, w_up, w_down, acts[:8]
    )
    part = lax.psum_scatter(grads, "col", scatter_dimension=1, tiled=True)
    part = lax.psum(part, "row").astype(jnp.float32)
    n_up = ff // D
    up_share = part[:n_up].transpose(1, 0, 2).reshape(-1, ff)
    out_share = part[n_up]
    qkv_share = part[n_up + 1 :].reshape(D // TILE, -1, 3, TILE).transpose(1, 2, 0, 3)
    qkv_share = qkv_share.reshape(-1, 3 * D)
    small = jnp.concatenate([grad_vectors, grad_up_bias.reshape(ff // D, D)], axis=0)
    small = lax.psum(small, ("row", "col"))
    vec_share = lax.dynamic_slice_in_dim(small[:8], mine * (D // shards), D // shards, axis=1)
    bias_share = lax.dynamic_slice_in_dim(small[8:].reshape(ff), mine * (ff // shards), ff // shards)
    loss = (summed / total_images).reshape(1)
    return (
        loss,
        token_grad,
        qkv_share,
        out_share,
        up_share,
        grad_down,
        vec_share,
        bias_share,
        grad_proj,
        text_grad,
    )


def solution(mesh):
    in_specs = (
        P(("row", "col"), None),
        P(("row", "col"), None),
        P(),
        P(),
        P(),
        P(),
        P(),
        P(),
        P(),
        P(("row", "col"), None),
        P(),
        P(),
    )
    out_specs = (
        P(),
        P(("row", "col"), None),
        P("col", None),
        P("col", None),
        P("col", None),
        P("col", None),
        P(None, "col"),
        P("col"),
        P("col", None),
        P(("row", "col"), None),
    )
    return jax.shard_map(
        per_device, mesh=mesh, in_specs=in_specs, out_specs=out_specs, check_vma=False
    )
```

```python
import functools

import jax
import jax.numpy as jnp
from jax import lax
from jax.experimental import pallas as pl
from jax.experimental.pallas import tpu as pltpu
from jax.sharding import PartitionSpec as P

D = 768
HEADS = 12
HEAD_DIM = 64
SEQ = 197
EMB = 512
ROWS = 208
WIN = 256
TILE = 256
F32 = jnp.float32
BF = jnp.bfloat16
NT = (((1,), (1,)), ((), ()))
TN = (((0,), (0,)), ((), ()))


def mm(a, b, dims=(((1,), (0,)), ((), ()))):
    return lax.dot_general(a, b, dims, preferred_element_type=F32)


def head_masks():
    lane = lax.broadcasted_iota(jnp.int32, (1, TILE), 1) // HEAD_DIM
    return [(lane == h).astype(F32).astype(BF) for h in range(TILE // HEAD_DIM)]


def gelu_pair(u):
    z = jnp.abs(u)
    t = 1.0 / (1.0 + (0.3275911 * 0.7071067811865476) * z)
    e = jnp.exp(-0.5 * (u * u))
    poly = 0.5 * 1.061405429
    for c in (-1.453152027, 1.421413741, -0.284496736, 0.254829592):
        poly = poly * t + 0.5 * c
    tail = poly * t * e
    cdf = jnp.where(u >= 0.0, 1.0 - tail, tail)
    return u * cdf, cdf + (0.3989422804014327 * u) * e


def forward_kernel(
    images, ff,
    tok_ref, keep_ref, wqkv_h, wout_h, wup_h, wdown_h, vec_ref, upb_ref,
    h1_h, qkv_h, p_h, o_h, h2_h, xh2_h, rstd_h, gk_h, apool_ref, pooled_ref,
    wqkv, wout, wup, wdown, xs, h1, qkv, p_s, o_s, h2, xh2, rstd, gk, a_s, keep8, kmask, kcol, bias, acc,
    in_sem, out_sem,
):
    n_quads = D // TILE
    n_ff = ff // TILE
    loads = []
    for k, (src, dst) in enumerate(((wqkv_h, wqkv), (wout_h, wout), (wup_h, wup), (wdown_h, wdown))):
        c = pltpu.make_async_copy(src, dst, in_sem.at[k])
        c.start()
        loads.append(c)
    stores = []

    def send(k, src, dst):
        c = pltpu.make_async_copy(src, dst, out_sem.at[k])
        c.start()
        stores.append(c)

    total = images * SEQ
    last = total // 16 * 16
    xs[last:, :] = jnp.zeros_like(xs[last:, :])
    xs[0:last, :] = tok_ref[0:last, :].astype(F32)
    if last < total:
        xs[last:total, :] = tok_ref[last:total, :].astype(F32)
    keep8[...] = jnp.zeros_like(keep8)
    keep8[0:images, 0:SEQ] = keep_ref[...].astype(F32)
    kb = keep8[...]
    rid = lax.broadcasted_iota(jnp.int32, kb.shape, 0)
    for i in range(images):
        kmask[i] = jnp.where(rid == i, kb, 0.0).astype(BF)
        one = jnp.ones((kb.shape[0], 128), F32).astype(BF)
        kcol[i * ROWS:(i + 1) * ROWS, :] = mm(kmask[i], one, TN)[0:ROWS]
    bias[0:1, 0:D] = vec_ref[2:3, :]
    bias[0:1, D:2 * D] = jnp.zeros((1, D), F32)
    bias[0:1, 2 * D:] = vec_ref[3:4, :]
    for i in range(images):
        x = xs[i * SEQ:i * SEQ + ROWS, :]
        cen = x - jnp.mean(x, axis=1, keepdims=True)
        inv = lax.rsqrt(jnp.mean(cen * cen, axis=1, keepdims=True) + 1e-6)
        h1[i * ROWS:(i + 1) * ROWS, :] = (cen * inv * vec_ref[0:1, :] + vec_ref[1:2, :]).astype(BF)
    send(0, h1, h1_h)
    loads[0].wait()
    span = images * ROWS
    pad = qkv.shape[1] - span
    for t in range(3 * n_quads):
        qkv[t, span:, :] = jnp.zeros((pad, TILE), BF)

    def proj(t, _):
        col = pl.multiple_of(t * TILE, TILE)
        r = mm(h1[...], wqkv[:, pl.ds(col, TILE)]) + bias[0:1, pl.ds(col, TILE)]
        r = r * jnp.where(t < n_quads, HEAD_DIM ** -0.5, 1.0)
        qkv[t, 0:span, :] = r.astype(BF)
        return 0

    lax.fori_loop(0, 3 * n_quads, proj, 0)
    send(1, qkv, qkv_h)
    masks = head_masks()

    def attend(it, _):
        i = it // n_quads
        j = it % n_quads
        r0 = pl.multiple_of(i * ROWS, 16)
        q4 = qkv[j, pl.ds(r0, ROWS), :]
        k4 = qkv[n_quads + j, pl.ds(r0, WIN), :]
        v4 = qkv[2 * n_quads + j, pl.ds(r0, WIN), :]
        valid = keep8[pl.ds(i, 1), :] > 0.0
        out = jnp.zeros((ROWS, TILE), F32)
        for h, m in enumerate(masks):
            s = mm(q4 * m, k4, NT)
            s = jnp.where(valid, s, -1e30)
            e = jnp.exp(s - jnp.max(s, axis=1, keepdims=True))
            pb = (e * (1.0 / jnp.sum(e, axis=1, keepdims=True))).astype(BF)
            p_s[it, h * ROWS:(h + 1) * ROWS, :] = pb
            out = out + mm(pb, v4 * m)
        o_s[j, pl.ds(r0, ROWS), :] = out.astype(BF)
        return 0

    lax.fori_loop(0, images * n_quads, attend, 0)
    send(2, p_s, p_h)
    send(3, o_s, o_h)
    loads[1].wait()
    pooled_ref[...] = jnp.zeros_like(pooled_ref)
    for i in range(images):
        rows = slice(i * ROWS, (i + 1) * ROWS)
        x = xs[i * SEQ:i * SEQ + ROWS, :]
        y = x + vec_ref[4:5, :]
        for j in range(n_quads):
            y = y + mm(o_s[j, rows, :], wout[j * TILE:(j + 1) * TILE, :])
        kc = kcol[rows, 0:1]
        pooled_ref[i:i + 1, 0:D] = jnp.sum(y * kc, axis=0, keepdims=True)
        cen = y - jnp.mean(y, axis=1, keepdims=True)
        inv = lax.rsqrt(jnp.mean(cen * cen, axis=1, keepdims=True) + 1e-6)
        xh = cen * inv
        xh2[rows, :] = xh.astype(BF)
        rstd[rows, :] = jnp.broadcast_to(inv, (ROWS, 128))
        h2[rows, :] = (xh * vec_ref[5:6, :] + vec_ref[6:7, :]).astype(BF)
    send(4, h2, h2_h)
    send(5, xh2, xh2_h)
    send(6, rstd, rstd_h)
    loads[2].wait()
    loads[3].wait()
    acc[...] = jnp.zeros_like(acc)
    a_s[span:, :] = jnp.zeros((a_s.shape[0] - span, TILE), BF)

    def feed(t, _):
        col = pl.multiple_of(t * TILE, TILE)
        ub = upb_ref[0:1, pl.ds(col, TILE)]
        for i in range(images):
            rows = slice(i * ROWS, (i + 1) * ROWS)
            u = mm(h2[rows, :], wup[:, pl.ds(col, TILE)]) + ub
            a, g = gelu_pair(u)
            a_s[rows, :] = a.astype(BF)
            gk[t, rows, :] = (g * kcol[rows, 0:1]).astype(BF)
        ap = jnp.zeros((kmask.shape[1], TILE), F32)
        for i in range(images):
            ap = ap + mm(kmask[i], a_s[i * ROWS:i * ROWS + WIN, :])
        at = pl.multiple_of((t % n_quads) * TILE, TILE)
        apool_ref[t // n_quads, :, pl.ds(at, TILE)] = ap[0:8]
        hi = ap.astype(BF)
        lo = (ap - hi.astype(F32)).astype(BF)
        w = wdown[pl.ds(col, TILE), :]
        acc[...] += mm(hi, w) + mm(lo, w)
        pltpu.make_async_copy(gk.at[t], gk_h.at[t], out_sem.at[7]).start()
        return 0

    lax.fori_loop(0, n_ff, feed, 0)
    cnt = jnp.sum(kb, axis=1, keepdims=True)[0:8]
    inv = 1.0 / jnp.maximum(cnt, 1.0)
    pooled_ref[:, 0:D] = (pooled_ref[:, 0:D] + acc[0:8, :]) * inv + vec_ref[7:8, :]
    pooled_ref[:, D:] = jnp.broadcast_to(cnt, (8, 128))
    for c in stores:
        c.wait()
    for t in range(n_ff):
        pltpu.make_async_copy(gk.at[t], gk_h.at[t], out_sem.at[7]).wait()


def forward_call(images, ff, tokens, keep, wqkv, wout, wup, wdown, vec, upb):
    span = images * ROWS
    nq = D // TILE
    wide = span + WIN - ROWS
    outs = [
        ((span, D), BF), ((3 * nq, wide, TILE), BF), ((images * nq, 4 * ROWS, TILE), BF),
        ((nq, span, TILE), BF), ((span, D), BF), ((span, D), BF), ((span, 128), F32),
        ((ff // TILE, span, TILE), BF), ((ff // D, 8, D), F32), ((8, D + 128), F32),
    ]
    anyspec = pl.BlockSpec(memory_space=pl.ANY)
    vm = pl.BlockSpec(memory_space=pltpu.VMEM)
    scratch = [
        pltpu.VMEM((D, 3 * D), BF), pltpu.VMEM((D, D), BF), pltpu.VMEM((D, ff), BF), pltpu.VMEM((ff, D), BF),
        pltpu.VMEM(((images - 1) * SEQ + ROWS + 7 & -8, D), F32),
    ] + [pltpu.VMEM(*o) for o in outs[:8]] + [
        pltpu.VMEM((wide, TILE), BF), pltpu.VMEM((16, WIN), F32), pltpu.VMEM((images, 16, WIN), BF),
        pltpu.VMEM((span, 128), F32), pltpu.VMEM((1, 3 * D), F32), pltpu.VMEM((16, D), F32),
        pltpu.SemaphoreType.DMA((4,)), pltpu.SemaphoreType.DMA((8,)),
    ]
    return pl.pallas_call(
        functools.partial(forward_kernel, images, ff),
        out_shape=[jax.ShapeDtypeStruct(s, d) for s, d in outs],
        in_specs=[vm, vm] + [anyspec] * 4 + [vm, vm],
        out_specs=[anyspec] * 8 + [vm, vm],
        scratch_shapes=scratch,
        compiler_params=pltpu.CompilerParams(vmem_limit_bytes=60 * 2**20),
        name="block_forward",
    )(tokens, keep, wqkv, wout, wup, wdown, vec, upb)


def backward_kernel(
    images, ff,
    tok_ref, keep_ref, dy_ref, da_s, vec_ref,
    wqkv_h, wout_h, wup_h, h1_h, qkv_h, p_h, o_h, h2_h, xh2_h, rstd_h, gk_h,
    tg_ref, g_ref, vg_ref, ub_ref,
    wqkv, wout, wup, h1, qkv, p_s, o_s, h2, xh2, rstd, du,
    xs, dx, db, do_s, dp_s, h1t, h2t, keep8, kcol,
    in_sem, gk_sem, p_sem,
):
    n_quads = D // TILE
    n_ff = ff // TILE
    span = images * ROWS
    masks = head_masks()
    loads = {}
    for k, (name, src, dst) in enumerate((
        ("h2", h2_h, h2), ("wup", wup_h, wup), ("xh2", xh2_h, xh2),
        ("rstd", rstd_h, rstd), ("wout", wout_h, wout), ("o", o_h, o_s), ("qkv", qkv_h, qkv),
        ("h1", h1_h, h1), ("wqkv", wqkv_h, wqkv),
    )):
        loads[name] = pltpu.make_async_copy(src, dst, in_sem.at[k])
    for name in ("h2",):
        loads[name].start()
    gks = []
    for t in range(n_ff):
        c = pltpu.make_async_copy(gk_h.at[t], du.at[:, t * TILE:(t + 1) * TILE], gk_sem.at[t])
        c.start()
        gks.append(c)
    for name in ("wup", "xh2", "rstd", "wout", "o", "qkv", "h1", "wqkv"):
        loads[name].start()

    def pcopy(i, j, slot):
        return pltpu.make_async_copy(p_h.at[i * n_quads + j], p_s.at[slot], p_sem.at[slot])

    pcopy(0, 0, 0).start()

    total = images * SEQ
    last = total // 16 * 16
    xs[last:, :] = jnp.zeros_like(xs[last:, :])
    xs[0:last, :] = tok_ref[0:last, :].astype(F32)
    if last < total:
        xs[last:total, :] = tok_ref[last:total, :].astype(F32)
    keep8[...] = jnp.zeros_like(keep8)
    keep8[0:images, 0:SEQ] = keep_ref[...].astype(F32)
    kb = keep8[...]
    rid = lax.broadcasted_iota(jnp.int32, kb.shape, 0)
    one = jnp.ones((kb.shape[0], 128), F32).astype(BF)
    for i in range(images):
        km = jnp.where(rid == i, kb, 0.0).astype(BF)
        kcol[i * ROWS:(i + 1) * ROWS, :] = mm(km, one, TN)[0:ROWS]

    dy = dy_ref[...]
    dyb = dy.astype(BF)
    cnt = jnp.sum(kb, axis=1, keepdims=True)[0:8]
    vg_ref[7:8, :] = jnp.sum(dyb.astype(F32) * cnt, axis=0, keepdims=True)
    loads["h2"].wait()
    h2t[...] = h2[...].T
    for c in gks:
        c.wait()

    def expand(t, _):
        col = pl.multiple_of(t * TILE, TILE)
        ub = jnp.zeros((1, TILE), F32)
        for i in range(images):
            rows = slice(i * ROWS, (i + 1) * ROWS)
            d = du[rows, pl.ds(col, TILE)].astype(F32) * da_s[i:i + 1, pl.ds(col, TILE)]
            ub = ub + jnp.sum(d, axis=0, keepdims=True)
            du[rows, pl.ds(col, TILE)] = d.astype(BF)
        ub_ref[:, pl.ds(col, TILE)] = ub
        part = mm(h2t[...], du[:, pl.ds(col, TILE)])
        c3 = pl.multiple_of((t % 3) * TILE, TILE)
        g_ref[t // 3, :, pl.ds(c3, TILE)] = part.astype(BF)
        return 0

    lax.fori_loop(0, n_ff, expand, 0)
    loads["wup"].wait()

    def down(n, _):
        col = pl.multiple_of(n * TILE, TILE)
        dx[:, pl.ds(col, TILE)] = mm(du[...], wup[pl.ds(col, TILE), :], NT)
        return 0

    lax.fori_loop(0, n_quads, down, 0)
    for name in ("xh2", "rstd", "wout", "o"):
        loads[name].wait()
    g2 = jnp.zeros((1, D), F32)
    b2 = jnp.zeros((1, D), F32)
    bo = jnp.zeros((1, D), F32)
    for i in range(images):
        rows = slice(i * ROWS, (i + 1) * ROWS)
        dh = dx[rows, :]
        xh = xh2[rows, :].astype(F32)
        g2 = g2 + jnp.sum(dh * xh, axis=0, keepdims=True)
        b2 = b2 + jnp.sum(dh, axis=0, keepdims=True)
        c = dh * vec_ref[5:6, :]
        m1 = jnp.mean(c, axis=1, keepdims=True)
        m2 = jnp.mean(c * xh, axis=1, keepdims=True)
        r = dy[i:i + 1, :] * kcol[rows, 0:1] + rstd[rows, 0:1] * (c - m1 - xh * m2)
        dx[rows, :] = r
        rb = r.astype(BF)
        db[rows, :] = rb
        bo = bo + jnp.sum(rb.astype(F32), axis=0, keepdims=True)
    vg_ref[5:6, :] = g2
    vg_ref[6:7, :] = b2
    vg_ref[4:5, :] = bo
    for j in range(n_quads):
        sl = slice(j * TILE, (j + 1) * TILE)
        do_s[j] = mm(db[...], wout[sl, :], NT).astype(BF)
        for n in range(n_quads):
            g_ref[4, sl, n * TILE:(n + 1) * TILE] = mm(
                o_s[j], db[:, n * TILE:(n + 1) * TILE], TN).astype(BF)
    for name in ("qkv", "h1"):
        loads[name].wait()
    h1t[...] = h1[...].T

    def quad(j, _):
        def attend(i, _):
            r0 = pl.multiple_of(i * ROWS, 16)
            step = j * images + i
            slot = step % 2
            nxt = step + 1

            @pl.when(nxt < n_quads * images)
            def _():
                pcopy(nxt % images, nxt // images, nxt % 2).start()

            pcopy(i, j, slot).wait()
            q4 = qkv[j, pl.ds(r0, ROWS), :]
            k4 = qkv[n_quads + j, pl.ds(r0, WIN), :]
            v4 = qkv[2 * n_quads + j, pl.ds(r0, WIN), :]
            d4 = do_s[j, pl.ds(r0, ROWS), :]
            dq = jnp.zeros((ROWS, TILE), F32)
            dk = jnp.zeros((WIN, TILE), F32)
            dv = jnp.zeros((WIN, TILE), F32)
            for h, m in enumerate(masks):
                pb = p_s[slot, h * ROWS:(h + 1) * ROWS, :]
                dm = d4 * m
                dv = dv + mm(pb, dm, TN)
                dpr = mm(dm, v4, NT)
                pf = pb.astype(F32)
                ds = (pf * (dpr - jnp.sum(pf * dpr, axis=1, keepdims=True))).astype(BF)
                dq = dq + mm(ds, k4 * m)
                dk = dk + mm(ds, q4 * m, TN)
            dq = dq * HEAD_DIM ** -0.5
            for s, val in enumerate((dq, dk[0:ROWS], dv[0:ROWS])):
                col = pl.multiple_of(s * D + j * TILE, TILE)
                dp_s[pl.ds(r0, ROWS), pl.ds(col, TILE)] = val.astype(BF)
            return 0

        lax.fori_loop(0, images, attend, 0)
        for s in range(3):
            col = pl.multiple_of(s * D + j * TILE, TILE)
            g_ref[5 + j, :, s * TILE:(s + 1) * TILE] = mm(h1t[...], dp_s[:, pl.ds(col, TILE)]).astype(BF)
        return 0

    lax.fori_loop(0, n_quads, quad, 0)
    vg_ref[2:3, :] = jnp.sum(dp_s[:, 0:D].astype(F32), axis=0, keepdims=True)
    vg_ref[3:4, :] = jnp.sum(dp_s[:, 2 * D:].astype(F32), axis=0, keepdims=True)
    loads["wqkv"].wait()
    g1 = jnp.zeros((1, D), F32)
    b1 = jnp.zeros((1, D), F32)
    for i in range(images):
        rows = slice(i * ROWS, (i + 1) * ROWS)
        dh = mm(dp_s[rows, :], wqkv[...], NT)
        x = xs[i * SEQ:i * SEQ + ROWS, :]
        cen = x - jnp.mean(x, axis=1, keepdims=True)
        inv = lax.rsqrt(jnp.mean(cen * cen, axis=1, keepdims=True) + 1e-6)
        xh = cen * inv
        g1 = g1 + jnp.sum(dh * xh, axis=0, keepdims=True)
        b1 = b1 + jnp.sum(dh, axis=0, keepdims=True)
        c = dh * vec_ref[0:1, :]
        m1 = jnp.mean(c, axis=1, keepdims=True)
        m2 = jnp.mean(c * xh, axis=1, keepdims=True)
        r = dx[rows, :] + inv * (c - m1 - xh * m2)
        tg_ref[i * SEQ:(i + 1) * SEQ, :] = r[0:SEQ]
    vg_ref[0:1, :] = g1
    vg_ref[1:2, :] = b1


def backward_call(images, ff, tokens, keep, dy, da, vec, wqkv, wout, wup, acts):
    span = images * ROWS
    nq = D // TILE
    wide = span + WIN - ROWS
    anyspec = pl.BlockSpec(memory_space=pl.ANY)
    vm = pl.BlockSpec(memory_space=pltpu.VMEM)
    outs = [((images * SEQ, D), F32), ((ff // D + 4, D, D), BF), ((8, D), F32), ((1, ff), F32)]
    scratch = [
        pltpu.VMEM((D, 3 * D), BF), pltpu.VMEM((D, D), BF), pltpu.VMEM((D, ff), BF),
        pltpu.VMEM((span, D), BF), pltpu.VMEM((3 * nq, wide, TILE), BF), pltpu.VMEM((2, 4 * ROWS, TILE), BF),
        pltpu.VMEM((nq, span, TILE), BF), pltpu.VMEM((span, D), BF), pltpu.VMEM((span, D), BF),
        pltpu.VMEM((span, 128), F32), pltpu.VMEM((span, ff), BF),
        pltpu.VMEM(((images - 1) * SEQ + ROWS + 7 & -8, D), F32), pltpu.VMEM((span, D), F32),
        pltpu.VMEM((span, D), BF), pltpu.VMEM((nq, span, TILE), BF), pltpu.VMEM((span, 3 * D), BF),
        pltpu.VMEM((D, span), BF), pltpu.VMEM((D, span), BF), pltpu.VMEM((16, WIN), F32),
        pltpu.VMEM((span, 128), F32),
        pltpu.SemaphoreType.DMA((10,)), pltpu.SemaphoreType.DMA((ff // TILE,)), pltpu.SemaphoreType.DMA((2,)),
    ]
    return pl.pallas_call(
        functools.partial(backward_kernel, images, ff),
        out_shape=[jax.ShapeDtypeStruct(s, d) for s, d in outs],
        in_specs=[vm] * 5 + [anyspec] * 11,
        out_specs=[vm] * 4,
        scratch_shapes=scratch,
        compiler_params=pltpu.CompilerParams(vmem_limit_bytes=62 * 2**20),
        name="block_backward",
    )(tokens, keep, dy, da, vec, wqkv, wout, wup, *acts)


def split3(x):
    hi = x.astype(BF)
    r = x - hi.astype(F32)
    mid = r.astype(BF)
    lo = (r - mid.astype(F32)).astype(BF)
    return hi, mid, lo


NN = (((1,), (0,)), ((), ()))
MESH = pl.DeviceIdType.MESH


def mm3(x, w, dims=NN):
    hi, mid, lo = split3(x)
    return (mm(lo, w, dims) + mm(mid, w, dims)) + mm(hi, w, dims)


def place(cz, cy):
    row = lax.axis_index("row")
    col = lax.axis_index("col")
    return row, col // (2 * cy), lax.rem(col // 2, cy), lax.rem(col, 2)


def head_kernel(
    n_row, cz, cy, images, ff,
    pooled_ref, texts_ref, apool_ref, pair_ref, scale_ref, wproj_ref, wdown_h,
    loss_ref, dy_ref, da_ref, text_ref, proj_ref, down_ref,
    pg, ax, ag, wdown, p_all, t_all, c_all, a_all, gproj, gdown,
    in_sem, zs, zr, ps, pr, cs, cr,
):
    x, z, y, core = place(cz, cy)
    load = pltpu.make_async_copy(wdown_h, wdown, in_sem.at[0])
    load.start()
    half = D // 2
    plane = n_row * cy
    spot = x * cy + y

    def device(xx, zz, yy, cc):
        return (xx, (zz * cy + yy) * 2 + cc)

    z_peers = [lax.rem(z + k, cz) for k in range(1, cz)]
    p_peers = [lax.rem(spot + k, plane) for k in range(1, plane)]
    bar = pltpu.get_barrier_semaphore()
    for zz in z_peers:
        pl.semaphore_signal(bar, inc=1, device_id=device(x, zz, y, core), device_id_type=MESH)
    for pp in p_peers:
        pl.semaphore_signal(bar, inc=1, device_id=device(pp // cy, z, lax.rem(pp, cy), core), device_id_type=MESH)
    pl.semaphore_signal(bar, inc=1, device_id=device(x, z, y, 1 - core), device_id_type=MESH)
    mine = jnp.concatenate([
        pooled_ref[0:images, 0:D],
        jnp.concatenate([texts_ref[...].astype(F32), pooled_ref[0:images, D:], jnp.zeros((images, D - EMB - 128), F32)], axis=1),
    ], axis=0)
    pg[x, z, y, core] = mine
    for g in range(cz):
        ax[g, 0:images] = apool_ref[g, 0:images, 0:half]
        ax[g, images:] = apool_ref[g, 0:images, half:]
    ag[x, z, y, core] = ax[z]
    pl.semaphore_wait(bar, cz - 1 + plane - 1 + 1)

    def stage(src, dst, sems, slot, devs):
        out = []
        for k, (s, dev) in enumerate(zip(src, devs)):
            c = pltpu.make_async_remote_copy(
                s, dst, sems[0].at[slot, k], sems[1].at[slot, k], device_id=dev, device_id_type=MESH)
            c.start()
            out.append(c)
        return out

    z_devs = [device(x, zz, y, core) for zz in z_peers]
    p_devs = [device(pp // cy, z, lax.rem(pp, cy), core) for pp in p_peers]
    c_devs = [device(x, z, y, 1 - core)]
    own = pg.at[x, z, y, core]
    first = stage([own] * len(z_devs), own, (zs, zr), 0, z_devs)
    first_a = stage([ax.at[zz] for zz in z_peers], ag.at[x, z, y, core], (zs, zr), 1, z_devs)
    for c in first:
        c.wait()
    own = pg.at[x, :, y, core]
    second = stage([own] * len(p_devs), own, (ps, pr), 0, p_devs)
    for c in first_a:
        c.wait()
    own = ag.at[x, :, y, core]
    second_a = stage([own] * len(p_devs), own, (ps, pr), 1, p_devs)
    for c in second:
        c.wait()
    own = pg.at[:, :, :, core]
    third = stage([own], own, (cs, cr), 0, c_devs)
    for c in second_a:
        c.wait()
    own = ag.at[:, :, :, core]
    third_a = stage([own], own, (cs, cr), 1, c_devs)
    for c in third:
        c.wait()
    n_col = cz * cy * 2
    n_img = n_row * n_col * images
    for d in range(n_row * n_col):
        rows = slice(d * images, (d + 1) * images)
        at = (d // n_col, d % n_col // (2 * cy), d // 2 % cy, d % 2)
        p_all[rows, :] = pg[at + (slice(0, images), slice(0, D))]
        t_all[rows, :] = pg[at + (slice(images, 2 * images), slice(0, EMB))]
        c_all[rows, :] = pg[at + (slice(images, 2 * images), slice(EMB, EMB + 128))]
    scale = scale_ref[0]
    pooled = p_all[...]
    latent = mm3(pooled, wproj_ref[...])
    norm = lax.rsqrt(jnp.sum(latent * latent, axis=1, keepdims=True) + 1e-6)
    embeds = latent * norm
    eb = embeds.astype(BF)
    tb = t_all[...].astype(BF)
    logits = scale * mm(eb, tb, NT)
    row_max = jnp.max(logits, axis=1, keepdims=True)
    row_exp = jnp.exp(logits - row_max)
    row_sum = jnp.sum(row_exp, axis=1, keepdims=True)
    col_max = jnp.max(logits, axis=0, keepdims=True)
    col_exp = jnp.exp(logits - col_max)
    col_sum = jnp.sum(col_exp, axis=0, keepdims=True)
    ids = lax.broadcasted_iota(jnp.int32, (n_img, n_img), 0)
    match = (ids == pair_ref[...]).astype(F32).T
    grad = 0.5 * (row_exp / row_sum) + 0.5 * (col_exp / col_sum) - match
    lse = jnp.sum(row_max + jnp.log(row_sum), axis=0, keepdims=True) + jnp.sum(
        col_max + jnp.log(col_sum), axis=1, keepdims=True)
    hits = jnp.sum(jnp.sum(logits * match, axis=1, keepdims=True), axis=0, keepdims=True)
    loss_ref[...] = (0.5 * lse - hits) * (1.0 / n_img)
    de = scale * mm3(grad, tb)
    dz = norm * (de - embeds * jnp.sum(embeds * de, axis=1, keepdims=True))
    image_grad = mm3(dz, wproj_ref[...], NT) / c_all[:, 0:1]
    dev = x * n_col + (z * cy + y) * 2 + core
    want = lax.broadcasted_iota(jnp.int32, (16, n_img), 0) + dev * images
    have = lax.broadcasted_iota(jnp.int32, (16, n_img), 1)
    pick = (want == have).astype(F32).astype(BF)
    hi, mid, lo = split3(image_grad)
    dy = (mm(pick, lo) + mm(pick, mid)) + mm(pick, hi)
    dy_ref[...] = dy[0:8]
    dyb = dy.astype(BF)
    load.wait()

    def spread(t, _):
        col = pl.multiple_of(t * TILE, TILE)
        da_ref[:, pl.ds(col, TILE)] = mm(dyb, wdown[pl.ds(col, TILE), :], NT)[0:8]
        return 0

    lax.fori_loop(0, ff // TILE, spread, 0)
    g_hi, g_mid, g_lo = split3(grad)
    own_grad = (mm(pick, g_lo, NT) + mm(pick, g_mid, NT)) + mm(pick, g_hi, NT)
    text_ref[...] = (scale * mm3(own_grad, eb))[0:images]
    p_hi, p_lo, _ = split3(pooled)
    d_hi, d_lo, _ = split3(dz)
    gproj[...] = (mm(p_lo, d_hi, TN) + mm(p_hi, d_lo, TN)) + mm(p_hi, d_hi, TN)
    n_proj = D // n_col
    at = pl.multiple_of(((z * cy + y) * 2 + core) * n_proj, 8)
    proj_ref[...] = gproj[pl.ds(at, n_proj), :]
    for c in third_a:
        c.wait()
    for d in range(n_row * n_col):
        rows = slice(d * images, (d + 1) * images)
        at = (d // n_col, d % n_col // (2 * cy), d // 2 % cy, d % 2)
        a_all[rows, 0:half] = ag[at + (slice(0, images),)]
        a_all[rows, half:] = ag[at + (slice(images, 2 * images),)]
    acts = a_all[...]
    a_hi = acts.astype(BF)
    a_lo = (acts - a_hi.astype(F32)).astype(BF)
    for n in range(D // TILE):
        sl = slice(n * TILE, (n + 1) * TILE)
        gdown[:, sl] = mm(a_lo, hi[:, sl], TN) + mm(a_hi, hi[:, sl], TN)
    n_down = ff // n_col
    at = pl.multiple_of((y * 2 + core) * n_down, 8)
    down_ref[...] = gdown[pl.ds(at, n_down), :]


def head_call(n_row, n_col, images, ff, pooled, texts, apool, pair, scale, wproj, wdown):
    cz = ff // D
    cy = n_col // (2 * cz)
    n_img = n_row * n_col * images
    vm = pl.BlockSpec(memory_space=pltpu.VMEM)
    outs = [(1, 1), (8, D), (8, ff), (images, EMB), (D // n_col, EMB), (ff // n_col, D)]
    plane = n_row * cy
    grid = (n_row, cz, cy, 2, 2 * images)
    scratch = [
        pltpu.VMEM(grid + (D,), F32), pltpu.VMEM((cz, 2 * images, D // 2), F32), pltpu.VMEM(grid + (D // 2,), F32),
        pltpu.VMEM((ff, D), BF), pltpu.VMEM((n_img, D), F32), pltpu.VMEM((n_img, EMB), F32),
        pltpu.VMEM((n_img, 128), F32), pltpu.VMEM((n_img, D), F32), pltpu.VMEM((D, EMB), F32), pltpu.VMEM((D, D), F32),
        pltpu.SemaphoreType.DMA((1,)), pltpu.SemaphoreType.DMA((2, cz)), pltpu.SemaphoreType.DMA((2, cz)),
        pltpu.SemaphoreType.DMA((2, plane)), pltpu.SemaphoreType.DMA((2, plane)),
        pltpu.SemaphoreType.DMA((2, 1)), pltpu.SemaphoreType.DMA((2, 1)),
    ]
    return pl.pallas_call(
        functools.partial(head_kernel, n_row, cz, cy, images, ff),
        out_shape=[jax.ShapeDtypeStruct(s, F32) for s in outs],
        in_specs=[vm] * 4 + [pl.BlockSpec(memory_space=pltpu.SMEM), vm, pl.BlockSpec(memory_space=pl.ANY)],
        out_specs=[vm] * len(outs),
        scratch_shapes=scratch,
        compiler_params=pltpu.CompilerParams(
            vmem_limit_bytes=60 * 2**20, collective_id=0, has_side_effects=True),
        name="contrastive_head",
    )(pooled, texts, apool, pair, scale, wproj, wdown)


def per_device(
    tokens,
    keep_mask,
    w_qkv,
    w_out,
    w_up,
    w_down,
    vectors,
    up_bias,
    w_proj,
    texts,
    pair_index,
    logit_scale,
):
    images = keep_mask.shape[0]
    ff = w_up.shape[1]
    n_row, shards = lax.axis_size("row"), lax.axis_size("col")
    mine = lax.axis_index("col")
    acts = forward_call(
        images, ff, tokens, keep_mask, w_qkv, w_out, w_up, w_down, vectors, up_bias.reshape(1, ff)
    )
    loss, dy, da, text_grad, grad_proj, grad_down = head_call(
        n_row, shards, images, ff, acts[9], texts, acts[8], pair_index.reshape(1, -1), logit_scale, w_proj, w_down
    )
    token_grad, grads, grad_vectors, grad_up_bias = backward_call(
        images, ff, tokens, keep_mask, dy, da, vectors, w_qkv, w_out, w_up, acts[:8]
    )
    part = lax.psum_scatter(grads, "col", scatter_dimension=1, tiled=True)
    part = lax.psum(part, "row").astype(jnp.float32)
    n_up = ff // D
    up_share = part[:n_up].transpose(1, 0, 2).reshape(-1, ff)
    out_share = part[n_up]
    qkv_share = part[n_up + 1 :].reshape(D // TILE, -1, 3, TILE).transpose(1, 2, 0, 3)
    qkv_share = qkv_share.reshape(-1, 3 * D)
    small = jnp.concatenate([grad_vectors, grad_up_bias.reshape(ff // D, D)], axis=0)
    small = lax.psum(small, ("row", "col"))
    vec_share = lax.dynamic_slice_in_dim(small[:8], mine * (D // shards), D // shards, axis=1)
    bias_share = lax.dynamic_slice_in_dim(small[8:].reshape(ff), mine * (ff // shards), ff // shards)
    return (
        loss.reshape(1),
        token_grad,
        qkv_share,
        out_share,
        up_share,
        grad_down,
        vec_share,
        bias_share,
        grad_proj,
        text_grad,
    )


def solution(mesh):
    in_specs = (
        P(("row", "col"), None),
        P(("row", "col"), None),
        P(),
        P(),
        P(),
        P(),
        P(),
        P(),
        P(),
        P(("row", "col"), None),
        P(),
        P(),
    )
    out_specs = (
        P(),
        P(("row", "col"), None),
        P("col", None),
        P("col", None),
        P("col", None),
        P("col", None),
        P(None, "col"),
        P("col"),
        P("col", None),
        P(("row", "col"), None),
    )
    return jax.shard_map(
        per_device, mesh=mesh, in_specs=in_specs, out_specs=out_specs, check_vma=False
    )
```

```python
import functools

import jax
import jax.numpy as jnp
from jax import lax
from jax.experimental import pallas as pl
from jax.experimental.pallas import tpu as pltpu
from jax.sharding import PartitionSpec as P

D = 768
HEADS = 12
HEAD_DIM = 64
SEQ = 197
EMB = 512
ROWS = 208
WIN = 256
TILE = 256
F32 = jnp.float32
BF = jnp.bfloat16
NT = (((1,), (1,)), ((), ()))
TN = (((0,), (0,)), ((), ()))


def mm(a, b, dims=(((1,), (0,)), ((), ()))):
    return lax.dot_general(a, b, dims, preferred_element_type=F32)


def head_masks():
    lane = lax.broadcasted_iota(jnp.int32, (1, TILE), 1) // HEAD_DIM
    return [(lane == h).astype(F32).astype(BF) for h in range(TILE // HEAD_DIM)]


def gelu_pair(u):
    z = jnp.abs(u)
    t = 1.0 / (1.0 + (0.3275911 * 0.7071067811865476) * z)
    e = jnp.exp(-0.5 * (u * u))
    poly = 0.5 * 1.061405429
    for c in (-1.453152027, 1.421413741, -0.284496736, 0.254829592):
        poly = poly * t + 0.5 * c
    tail = poly * t * e
    cdf = jnp.where(u >= 0.0, 1.0 - tail, tail)
    return u * cdf, cdf + (0.3989422804014327 * u) * e


def forward_kernel(
    images, ff,
    tok_ref, keep_ref, wqkv_h, wout_h, wup_h, wdown_h, vec_ref, upb_ref,
    h1t_h, qkv_h, p_h, ot_h, h2t_h, xh1_h, xh2_h, rstd1_h, rstd2_h, kcol_h, gk_h, apool_ref, pooled_ref,
    wqkv, wout, wup, wdown, xs, h1t, qkv, p_s, ot, h2t, xh1, xh2, rstd1, rstd2, kcol, gk,
    h1, o_s, h2, a_s, keep8, kmask, bias, acc,
    in_sem, out_sem,
):
    n_quads = D // TILE
    n_ff = ff // TILE
    loads = []
    for k, (src, dst) in enumerate(((wqkv_h, wqkv), (wout_h, wout), (wup_h, wup), (wdown_h, wdown))):
        c = pltpu.make_async_copy(src, dst, in_sem.at[k])
        c.start()
        loads.append(c)
    stores = []

    def send(k, src, dst):
        c = pltpu.make_async_copy(src, dst, out_sem.at[k])
        c.start()
        stores.append(c)

    total = images * SEQ
    last = total // 16 * 16
    xs[last:, :] = jnp.zeros_like(xs[last:, :])
    xs[0:last, :] = tok_ref[0:last, :].astype(F32)
    if last < total:
        xs[last:total, :] = tok_ref[last:total, :].astype(F32)
    keep8[...] = jnp.zeros_like(keep8)
    keep8[0:images, 0:SEQ] = keep_ref[...].astype(F32)
    kb = keep8[...]
    rid = lax.broadcasted_iota(jnp.int32, kb.shape, 0)
    for i in range(images):
        kmask[i] = jnp.where(rid == i, kb, 0.0).astype(BF)
        one = jnp.ones((kb.shape[0], 128), F32).astype(BF)
        kcol[i * ROWS:(i + 1) * ROWS, :] = mm(kmask[i], one, TN)[0:ROWS]
    send(0, kcol, kcol_h)
    bias[0:1, 0:D] = vec_ref[2:3, :]
    bias[0:1, D:2 * D] = jnp.zeros((1, D), F32)
    bias[0:1, 2 * D:] = vec_ref[3:4, :]
    for i in range(images):
        x = xs[i * SEQ:i * SEQ + ROWS, :]
        cen = x - jnp.mean(x, axis=1, keepdims=True)
        inv = lax.rsqrt(jnp.mean(cen * cen, axis=1, keepdims=True) + 1e-6)
        xh = cen * inv
        rows = slice(i * ROWS, (i + 1) * ROWS)
        xh1[rows, :] = xh.astype(BF)
        rstd1[rows, :] = jnp.broadcast_to(inv, (ROWS, 128))
        h1[rows, :] = (xh * vec_ref[0:1, :] + vec_ref[1:2, :]).astype(BF)
    send(8, xh1, xh1_h)
    send(9, rstd1, rstd1_h)
    h1t[...] = h1[...].T
    send(10, h1t, h1t_h)
    loads[0].wait()
    span = images * ROWS
    pad = qkv.shape[1] - span
    for t in range(3 * n_quads):
        qkv[t, span:, :] = jnp.zeros((pad, TILE), BF)

    def proj(t, _):
        col = pl.multiple_of(t * TILE, TILE)
        r = mm(h1[...], wqkv[:, pl.ds(col, TILE)]) + bias[0:1, pl.ds(col, TILE)]
        r = r * jnp.where(t < n_quads, HEAD_DIM ** -0.5, 1.0)
        qkv[t, 0:span, :] = r.astype(BF)
        return 0

    lax.fori_loop(0, 3 * n_quads, proj, 0)
    send(1, qkv, qkv_h)
    masks = head_masks()

    def attend(it, _):
        i = it // n_quads
        j = it % n_quads
        r0 = pl.multiple_of(i * ROWS, 16)
        q4 = qkv[j, pl.ds(r0, ROWS), :]
        k4 = qkv[n_quads + j, pl.ds(r0, WIN), :]
        v4 = qkv[2 * n_quads + j, pl.ds(r0, WIN), :]
        valid = keep8[pl.ds(i, 1), :] > 0.0
        out = jnp.zeros((ROWS, TILE), F32)
        for h, m in enumerate(masks):
            s = mm(q4 * m, k4, NT)
            s = jnp.where(valid, s, -1e30)
            e = jnp.exp(s - jnp.max(s, axis=1, keepdims=True))
            pb = (e * (1.0 / jnp.sum(e, axis=1, keepdims=True))).astype(BF)
            p_s[it, h * ROWS:(h + 1) * ROWS, :] = pb
            out = out + mm(pb, v4 * m)
        o_s[j, pl.ds(r0, ROWS), :] = out.astype(BF)
        return 0

    lax.fori_loop(0, images * n_quads, attend, 0)
    send(2, p_s, p_h)
    for j in range(n_quads):
        ot[j * TILE:(j + 1) * TILE, :] = o_s[j].T
    send(3, ot, ot_h)
    loads[1].wait()
    pooled_ref[...] = jnp.zeros_like(pooled_ref)
    for i in range(images):
        rows = slice(i * ROWS, (i + 1) * ROWS)
        x = xs[i * SEQ:i * SEQ + ROWS, :]
        y = x + vec_ref[4:5, :]
        for j in range(n_quads):
            y = y + mm(o_s[j, rows, :], wout[j * TILE:(j + 1) * TILE, :])
        kc = kcol[rows, 0:1]
        pooled_ref[i:i + 1, 0:D] = jnp.sum(y * kc, axis=0, keepdims=True)
        cen = y - jnp.mean(y, axis=1, keepdims=True)
        inv = lax.rsqrt(jnp.mean(cen * cen, axis=1, keepdims=True) + 1e-6)
        xh = cen * inv
        xh2[rows, :] = xh.astype(BF)
        rstd2[rows, :] = jnp.broadcast_to(inv, (ROWS, 128))
        h2[rows, :] = (xh * vec_ref[5:6, :] + vec_ref[6:7, :]).astype(BF)
    h2t[...] = h2[...].T
    send(4, h2t, h2t_h)
    send(5, xh2, xh2_h)
    send(6, rstd2, rstd2_h)
    loads[2].wait()
    loads[3].wait()
    acc[...] = jnp.zeros_like(acc)
    a_s[span:, :] = jnp.zeros((a_s.shape[0] - span, TILE), BF)

    def feed(t, _):
        col = pl.multiple_of(t * TILE, TILE)
        ub = upb_ref[0:1, pl.ds(col, TILE)]
        for i in range(images):
            rows = slice(i * ROWS, (i + 1) * ROWS)
            u = mm(h2[rows, :], wup[:, pl.ds(col, TILE)]) + ub
            a, g = gelu_pair(u)
            a_s[rows, :] = a.astype(BF)
            gk[t, rows, :] = (g * kcol[rows, 0:1]).astype(BF)
        ap = jnp.zeros((kmask.shape[1], TILE), F32)
        for i in range(images):
            ap = ap + mm(kmask[i], a_s[i * ROWS:i * ROWS + WIN, :])
        at = pl.multiple_of((t % n_quads) * TILE, TILE)
        apool_ref[t // n_quads, :, pl.ds(at, TILE)] = ap[0:8]
        hi = ap.astype(BF)
        lo = (ap - hi.astype(F32)).astype(BF)
        w = wdown[pl.ds(col, TILE), :]
        acc[...] += mm(hi, w) + mm(lo, w)
        pltpu.make_async_copy(gk.at[t], gk_h.at[t], out_sem.at[7]).start()
        return 0

    lax.fori_loop(0, n_ff, feed, 0)
    cnt = jnp.sum(kb, axis=1, keepdims=True)[0:8]
    inv = 1.0 / jnp.maximum(cnt, 1.0)
    pooled_ref[:, 0:D] = (pooled_ref[:, 0:D] + acc[0:8, :]) * inv + vec_ref[7:8, :]
    pooled_ref[:, D:] = jnp.broadcast_to(cnt, (8, 128))
    for c in stores:
        c.wait()
    for t in range(n_ff):
        pltpu.make_async_copy(gk.at[t], gk_h.at[t], out_sem.at[7]).wait()


def forward_call(images, ff, tokens, keep, wqkv, wout, wup, wdown, vec, upb):
    span = images * ROWS
    nq = D // TILE
    wide = span + WIN - ROWS
    outs = [
        ((D, span), BF), ((3 * nq, wide, TILE), BF), ((images * nq, 4 * ROWS, TILE), BF),
        ((D, span), BF), ((D, span), BF), ((span, D), BF), ((span, D), BF), ((span, 128), F32), ((span, 128), F32),
        ((span, 128), F32), ((ff // TILE, span, TILE), BF), ((ff // D, 8, D), F32), ((8, D + 128), F32),
    ]
    anyspec = pl.BlockSpec(memory_space=pl.ANY)
    vm = pl.BlockSpec(memory_space=pltpu.VMEM)
    scratch = [
        pltpu.VMEM((D, 3 * D), BF), pltpu.VMEM((D, D), BF), pltpu.VMEM((D, ff), BF), pltpu.VMEM((ff, D), BF),
        pltpu.VMEM(((images - 1) * SEQ + ROWS + 7 & -8, D), F32),
    ] + [pltpu.VMEM(*o) for o in outs[:11]] + [
        pltpu.VMEM((span, D), BF), pltpu.VMEM((nq, span, TILE), BF), pltpu.VMEM((span, D), BF),
        pltpu.VMEM((wide, TILE), BF), pltpu.VMEM((16, WIN), F32), pltpu.VMEM((images, 16, WIN), BF),
        pltpu.VMEM((1, 3 * D), F32), pltpu.VMEM((16, D), F32),
        pltpu.SemaphoreType.DMA((4,)), pltpu.SemaphoreType.DMA((11,)),
    ]
    return pl.pallas_call(
        functools.partial(forward_kernel, images, ff),
        out_shape=[jax.ShapeDtypeStruct(s, d) for s, d in outs],
        in_specs=[vm, vm] + [anyspec] * 4 + [vm, vm],
        out_specs=[anyspec] * 11 + [vm, vm],
        scratch_shapes=scratch,
        compiler_params=pltpu.CompilerParams(vmem_limit_bytes=60 * 2**20),
        name="block_forward",
    )(tokens, keep, wqkv, wout, wup, wdown, vec, upb)


def split3(x):
    hi = x.astype(BF)
    r = x - hi.astype(F32)
    mid = r.astype(BF)
    lo = (r - mid.astype(F32)).astype(BF)
    return hi, mid, lo


NN = (((1,), (0,)), ((), ()))
MESH = pl.DeviceIdType.MESH


def mm3(x, w, dims=NN):
    hi, mid, lo = split3(x)
    return (mm(lo, w, dims) + mm(mid, w, dims)) + mm(hi, w, dims)


def place(cz, cy):
    row = lax.axis_index("row")
    col = lax.axis_index("col")
    return row, col // (2 * cy), lax.rem(col // 2, cy), lax.rem(col, 2)


def head_kernel(
    n_row, cz, cy, images, ff,
    pooled_ref, texts_ref, apool_ref, pair_ref, scale_ref, wproj_ref, wdown_h,
    loss_ref, dy_ref, da_ref, text_ref, proj_ref, down_ref,
    pg, ax, ag, wdown, p_all, t_all, c_all, a_all, gproj, gdown,
    in_sem, zs, zr, ps, pr, cs, cr,
):
    x, z, y, core = place(cz, cy)
    load = pltpu.make_async_copy(wdown_h, wdown, in_sem.at[0])
    load.start()
    half = D // 2
    plane = n_row * cy
    spot = x * cy + y

    def device(xx, zz, yy, cc):
        return (xx, (zz * cy + yy) * 2 + cc)

    z_peers = [lax.rem(z + k, cz) for k in range(1, cz)]
    p_peers = [lax.rem(spot + k, plane) for k in range(1, plane)]
    bar = pltpu.get_barrier_semaphore()
    for zz in z_peers:
        pl.semaphore_signal(bar, inc=1, device_id=device(x, zz, y, core), device_id_type=MESH)
    for pp in p_peers:
        pl.semaphore_signal(bar, inc=1, device_id=device(pp // cy, z, lax.rem(pp, cy), core), device_id_type=MESH)
    pl.semaphore_signal(bar, inc=1, device_id=device(x, z, y, 1 - core), device_id_type=MESH)
    mine = jnp.concatenate([
        pooled_ref[0:images, 0:D],
        jnp.concatenate([texts_ref[...].astype(F32), pooled_ref[0:images, D:], jnp.zeros((images, D - EMB - 128), F32)], axis=1),
    ], axis=0)
    pg[x, z, y, core] = mine
    for g in range(cz):
        ax[g, 0:images] = apool_ref[g, 0:images, 0:half]
        ax[g, images:] = apool_ref[g, 0:images, half:]
    ag[x, z, y, core] = ax[z]
    pl.semaphore_wait(bar, cz - 1 + plane - 1 + 1)

    def stage(src, dst, sems, slot, devs):
        out = []
        for k, (s, dev) in enumerate(zip(src, devs)):
            c = pltpu.make_async_remote_copy(
                s, dst, sems[0].at[slot, k], sems[1].at[slot, k], device_id=dev, device_id_type=MESH)
            c.start()
            out.append(c)
        return out

    z_devs = [device(x, zz, y, core) for zz in z_peers]
    p_devs = [device(pp // cy, z, lax.rem(pp, cy), core) for pp in p_peers]
    c_devs = [device(x, z, y, 1 - core)]
    own = pg.at[x, z, y, core]
    first = stage([own] * len(z_devs), own, (zs, zr), 0, z_devs)
    first_a = stage([ax.at[zz] for zz in z_peers], ag.at[x, z, y, core], (zs, zr), 1, z_devs)
    for c in first:
        c.wait()
    own = pg.at[x, :, y, core]
    second = stage([own] * len(p_devs), own, (ps, pr), 0, p_devs)
    for c in first_a:
        c.wait()
    own = ag.at[x, :, y, core]
    second_a = stage([own] * len(p_devs), own, (ps, pr), 1, p_devs)
    for c in second:
        c.wait()
    own = pg.at[:, :, :, core]
    third = stage([own], own, (cs, cr), 0, c_devs)
    for c in second_a:
        c.wait()
    own = ag.at[:, :, :, core]
    third_a = stage([own], own, (cs, cr), 1, c_devs)
    for c in third:
        c.wait()
    n_col = cz * cy * 2
    n_img = n_row * n_col * images
    for d in range(n_row * n_col):
        rows = slice(d * images, (d + 1) * images)
        at = (d // n_col, d % n_col // (2 * cy), d // 2 % cy, d % 2)
        p_all[rows, :] = pg[at + (slice(0, images), slice(0, D))]
        t_all[rows, :] = pg[at + (slice(images, 2 * images), slice(0, EMB))]
        c_all[rows, :] = pg[at + (slice(images, 2 * images), slice(EMB, EMB + 128))]
    scale = scale_ref[0]
    pooled = p_all[...]
    latent = mm3(pooled, wproj_ref[...])
    norm = lax.rsqrt(jnp.sum(latent * latent, axis=1, keepdims=True) + 1e-6)
    embeds = latent * norm
    eb = embeds.astype(BF)
    tb = t_all[...].astype(BF)
    logits = scale * mm(eb, tb, NT)
    row_max = jnp.max(logits, axis=1, keepdims=True)
    row_exp = jnp.exp(logits - row_max)
    row_sum = jnp.sum(row_exp, axis=1, keepdims=True)
    col_max = jnp.max(logits, axis=0, keepdims=True)
    col_exp = jnp.exp(logits - col_max)
    col_sum = jnp.sum(col_exp, axis=0, keepdims=True)
    ids = lax.broadcasted_iota(jnp.int32, (n_img, n_img), 0)
    match = (ids == pair_ref[...]).astype(F32).T
    grad = 0.5 * (row_exp / row_sum) + 0.5 * (col_exp / col_sum) - match
    lse = jnp.sum(row_max + jnp.log(row_sum), axis=0, keepdims=True) + jnp.sum(
        col_max + jnp.log(col_sum), axis=1, keepdims=True)
    hits = jnp.sum(jnp.sum(logits * match, axis=1, keepdims=True), axis=0, keepdims=True)
    loss_ref[...] = (0.5 * lse - hits) * (1.0 / n_img)
    de = scale * mm3(grad, tb)
    dz = norm * (de - embeds * jnp.sum(embeds * de, axis=1, keepdims=True))
    image_grad = mm3(dz, wproj_ref[...], NT) / c_all[:, 0:1]
    dev = x * n_col + (z * cy + y) * 2 + core
    want = lax.broadcasted_iota(jnp.int32, (16, n_img), 0) + dev * images
    have = lax.broadcasted_iota(jnp.int32, (16, n_img), 1)
    pick = (want == have).astype(F32).astype(BF)
    hi, mid, lo = split3(image_grad)
    dy = (mm(pick, lo) + mm(pick, mid)) + mm(pick, hi)
    dy_ref[...] = dy[0:8]
    dyb = dy.astype(BF)
    load.wait()

    def spread(t, _):
        col = pl.multiple_of(t * TILE, TILE)
        da_ref[:, pl.ds(col, TILE)] = mm(dyb, wdown[pl.ds(col, TILE), :], NT)[0:8]
        return 0

    lax.fori_loop(0, ff // TILE, spread, 0)
    g_hi, g_mid, g_lo = split3(grad)
    own_grad = (mm(pick, g_lo, NT) + mm(pick, g_mid, NT)) + mm(pick, g_hi, NT)
    text_ref[...] = (scale * mm3(own_grad, eb))[0:images]
    p_hi, p_lo, _ = split3(pooled)
    d_hi, d_lo, _ = split3(dz)
    gproj[...] = (mm(p_lo, d_hi, TN) + mm(p_hi, d_lo, TN)) + mm(p_hi, d_hi, TN)
    n_proj = D // n_col
    at = pl.multiple_of(((z * cy + y) * 2 + core) * n_proj, 8)
    proj_ref[...] = gproj[pl.ds(at, n_proj), :]
    for c in third_a:
        c.wait()
    for d in range(n_row * n_col):
        rows = slice(d * images, (d + 1) * images)
        at = (d // n_col, d % n_col // (2 * cy), d // 2 % cy, d % 2)
        a_all[rows, 0:half] = ag[at + (slice(0, images),)]
        a_all[rows, half:] = ag[at + (slice(images, 2 * images),)]
    acts = a_all[...]
    a_hi = acts.astype(BF)
    a_lo = (acts - a_hi.astype(F32)).astype(BF)
    for n in range(D // TILE):
        sl = slice(n * TILE, (n + 1) * TILE)
        gdown[:, sl] = mm(a_lo, hi[:, sl], TN) + mm(a_hi, hi[:, sl], TN)
    n_down = ff // n_col
    at = pl.multiple_of((y * 2 + core) * n_down, 8)
    down_ref[...] = gdown[pl.ds(at, n_down), :]


def head_call(n_row, n_col, images, ff, pooled, texts, apool, pair, scale, wproj, wdown):
    cz = ff // D
    cy = n_col // (2 * cz)
    n_img = n_row * n_col * images
    vm = pl.BlockSpec(memory_space=pltpu.VMEM)
    outs = [(1, 1), (8, D), (8, ff), (images, EMB), (D // n_col, EMB), (ff // n_col, D)]
    plane = n_row * cy
    grid = (n_row, cz, cy, 2, 2 * images)
    scratch = [
        pltpu.VMEM(grid + (D,), F32), pltpu.VMEM((cz, 2 * images, D // 2), F32), pltpu.VMEM(grid + (D // 2,), F32),
        pltpu.VMEM((ff, D), BF), pltpu.VMEM((n_img, D), F32), pltpu.VMEM((n_img, EMB), F32),
        pltpu.VMEM((n_img, 128), F32), pltpu.VMEM((n_img, D), F32), pltpu.VMEM((D, EMB), F32), pltpu.VMEM((D, D), F32),
        pltpu.SemaphoreType.DMA((1,)), pltpu.SemaphoreType.DMA((2, cz)), pltpu.SemaphoreType.DMA((2, cz)),
        pltpu.SemaphoreType.DMA((2, plane)), pltpu.SemaphoreType.DMA((2, plane)),
        pltpu.SemaphoreType.DMA((2, 1)), pltpu.SemaphoreType.DMA((2, 1)),
    ]
    return pl.pallas_call(
        functools.partial(head_kernel, n_row, cz, cy, images, ff),
        out_shape=[jax.ShapeDtypeStruct(s, F32) for s in outs],
        in_specs=[vm] * 4 + [pl.BlockSpec(memory_space=pltpu.SMEM), vm, pl.BlockSpec(memory_space=pl.ANY)],
        out_specs=[vm] * len(outs),
        scratch_shapes=scratch,
        compiler_params=pltpu.CompilerParams(
            vmem_limit_bytes=60 * 2**20, collective_id=0, has_side_effects=True),
        name="contrastive_head",
    )(pooled, texts, apool, pair, scale, wproj, wdown)


def backward_kernel(
    n_row, cz, cy, images, ff, n_a,
    dy_ref, da_ref, vec_ref,
    wqkv_h, wout_h, wup_h, h1t_h, qkv_h, p_h, ot_h, h2t_h, xh1_h, xh2_h, rstd1_h, rstd2_h, kcol_h, gk_h,
    tg_ref, qg_ref, og_ref, ug_ref, small_ref,
    wqkv, wout, wup, h1t, qkv, ot, h2t, xh1, xh2, rstd1, rstd2, kcol, p_s, du, dx, db, do_s, dp_s,
    g, r0, r1a, r1b, r2a, r2b, r3a, r3b, r4b, res, vc, vp, vz,
    in_sem, gk_sem, p_sem, s_sem, r_sem, vs_sem, vr_sem,
):
    n_quads = D // TILE
    n_ff = ff // TILE
    n_up = ff // D
    n_chunks = n_up + 1 + n_quads
    masks = head_masks()
    x, z, y, core = place(cz, cy)
    two = n_a < D
    n_h = (D - n_a) // 2
    plane = n_row * cy
    spot = x * cy + y

    def device(xx, zz, yy, cc):
        return (xx, (zz * cy + yy) * 2 + cc)

    core_dev = device(x, z, y, 1 - core)
    y_peers = [lax.rem(y + k, cy) for k in range(1, cy)]
    z_peers = [lax.rem(z + k, cz) for k in range(1, cz)]
    x_peers = [lax.rem(x + k, n_row) for k in range(1, n_row)]
    p_peers = [lax.rem(spot + k, plane) for k in range(1, plane)]
    z_devs = [device(x, zz, y, core) for zz in z_peers]
    y_devs = [device(x, z, yy, core) for yy in y_peers]
    x_devs = [device(xx, z, y, core) for xx in x_peers]
    p_devs = [device(pp // cy, z, lax.rem(pp, cy), core) for pp in p_peers]

    loads = {}
    for k, (name, src, dst) in enumerate((
        ("kcol", kcol_h, kcol), ("h2t", h2t_h, h2t), ("wup", wup_h, wup), ("xh2", xh2_h, xh2),
        ("rstd2", rstd2_h, rstd2), ("wout", wout_h, wout), ("ot", ot_h, ot), ("qkv", qkv_h, qkv),
        ("h1t", h1t_h, h1t), ("wqkv", wqkv_h, wqkv), ("xh1", xh1_h, xh1), ("rstd1", rstd1_h, rstd1),
    )):
        loads[name] = pltpu.make_async_copy(src, dst, in_sem.at[k])

    def gcopy(t):
        col = pl.multiple_of(t * TILE, TILE)
        return pltpu.make_async_copy(gk_h.at[t], du.at[:, pl.ds(col, TILE)], gk_sem.at[t])

    loads["h2t"].start()
    for t in range(n_ff):
        gcopy(t).start()
    for name in ("kcol", "wup", "xh2", "rstd2", "wout", "ot", "qkv", "h1t", "wqkv", "xh1", "rstd1"):
        loads[name].start()

    def pcopy(step):
        i = lax.rem(step, images)
        j = step // images
        slot = lax.rem(step, 2)
        return pltpu.make_async_copy(p_h.at[i * n_quads + j], p_s.at[slot], p_sem.at[slot])

    pcopy(0).start()
    bar = pltpu.get_barrier_semaphore()
    for dev in z_devs + p_devs + [core_dev]:
        pl.semaphore_signal(bar, inc=1, device_id=dev, device_id_type=MESH)
    pl.semaphore_wait(bar, len(z_devs) + len(p_devs) + 1)

    half = lambda which: pl.ds(pl.multiple_of(n_a + which * n_h, 128), n_h)

    def copies(p, c):
        if p == 0:
            out = [(g.at[lax.rem(c, 2), :, :, 1 - core], r0.at[c], core_dev)]
        elif p == 1:
            out = [(r0.at[c, :, yy, :, 0:n_a], r1a.at[c, k], dev) for k, (yy, dev) in enumerate(zip(y_peers, y_devs))]
            if two:
                out += [(r0.at[c, :, :, :, half(1 - x)], r1b.at[c], x_devs[0])]
        elif p == 2:
            out = [(r1a.at[c, 0, zz], r2a.at[c, k], dev) for k, (zz, dev) in enumerate(zip(z_peers, z_devs))]
            if two:
                out += [(r1b.at[c, :, yy], r2b.at[c, k], dev) for k, (yy, dev) in enumerate(zip(y_peers, y_devs))]
        elif p == 3:
            out = [(r3a.at[c, x], r3a.at[c, x], dev) for dev in x_devs]
            if two:
                out += [(r2b.at[c, 0, zz], r3b.at[c, k], dev) for k, (zz, dev) in enumerate(zip(z_peers, z_devs))]
        else:
            out = [(r3b.at[c, 0], r4b.at[c], x_devs[0])] if two else []
        base = p * s_sem.shape[1] // 5
        return [
            pltpu.make_async_remote_copy(
                src, dst, s_sem.at[c, base + k], r_sem.at[c, base + k], device_id=dev, device_id_type=MESH)
            for k, (src, dst, dev) in enumerate(out)
        ]

    def finish(p, c):
        up = lambda v: v.astype(F32)
        if p == 0:
            r0[c] = (up(r0[c]) + up(g[lax.rem(c, 2), :, :, core])).astype(BF)
        elif p == 1:
            v = up(r0[c, :, y, :, 0:n_a])
            for k in range(cy - 1):
                v = v + up(r1a[c, k])
            r1a[c, 0] = v.astype(BF)
            if two:
                r1b[c] = (up(r1b[c]) + up(r0[c, :, :, :, half(x)])).astype(BF)
        elif p == 2:
            v = up(r1a[c, 0, z])
            for k in range(cz - 1):
                v = v + up(r2a[c, k])
            r3a[c, x] = v.astype(BF)
            if two:
                v = up(r1b[c, :, y])
                for k in range(cy - 1):
                    v = v + up(r2b[c, k])
                r2b[c, 0] = v.astype(BF)
        elif p == 3:
            v = up(r3a[c, 0])
            for k in range(1, n_row):
                v = v + up(r3a[c, k])
            res[c, :, 0:n_a] = v
            if two:
                v = up(r2b[c, 0, z])
                for k in range(cz - 1):
                    v = v + up(r3b[c, k])
                v = v.astype(BF)
                r3b[c, 0] = v
                res[c, :, half(x)] = up(v)
        elif two:
            res[c, :, half(1 - x)] = up(r4b[c])

    def begin(p, c):
        for d in copies(p, c):
            d.start()

    def advance(p, c):
        for d in copies(p, c):
            d.wait()
        finish(p, c)
        if p < 4:
            begin(p + 1, c)

    first = n_up + 2
    last_unit = first + 2 * n_quads + images

    def chunk_at(n):
        odd = jnp.maximum((n - (n_up - 1)) // 2, 0)
        return n - odd

    def has_chunk(n):
        return (n >= 0) & ((n < n_up) | ((lax.rem(n - n_up, 2) == 1) & (n < first + 2 * n_quads)))

    def tick(n):
        @pl.when(has_chunk(n))
        def _():
            begin(0, chunk_at(n))

        for p in range(4, -1, -1):
            m = n - 1 - p

            @pl.when(has_chunk(m))
            def _(p=p, m=m):
                advance(p, chunk_at(m))

    def put(c, tt, part):
        col = pl.multiple_of(tt * TILE, TILE)
        g[lax.rem(c, 2), :, :, :, :, pl.ds(col, TILE)] = part.reshape(g.shape[1:5] + (TILE,)).astype(BF)

    def unit_up(n):
        def expand(tt, _):
            t = n * n_quads + tt
            col = pl.multiple_of(t * TILE, TILE)
            gcopy(t).wait()
            ub = jnp.zeros((1, TILE), F32)
            for i in range(images):
                rows = slice(i * ROWS, (i + 1) * ROWS)
                d = du[rows, pl.ds(col, TILE)].astype(F32) * da_ref[i:i + 1, pl.ds(col, TILE)]
                ub = ub + jnp.sum(d, axis=0, keepdims=True)
                du[rows, pl.ds(col, TILE)] = d.astype(BF)
            scol = pl.multiple_of(tt * TILE, TILE)
            small_ref[pl.ds(8 + n, 1), pl.ds(scol, TILE)] = ub
            put(n, tt, mm(h2t[...], du[:, pl.ds(col, TILE)]))
            return 0

        lax.fori_loop(0, n_quads, expand, 0)

    def unit_down():
        loads["wup"].wait()

        def down(n, _):
            col = pl.multiple_of(n * TILE, TILE)
            dx[:, pl.ds(col, TILE)] = mm(du[...], wup[pl.ds(col, TILE), :], NT)
            return 0

        lax.fori_loop(0, n_quads, down, 0)

    def unit_mid():
        for name in ("kcol", "xh2", "rstd2", "wout", "ot"):
            loads[name].wait()
        dy = dy_ref[...]
        dyb = dy.astype(BF).astype(F32)
        g2 = jnp.zeros((1, D), F32)
        b2 = jnp.zeros((1, D), F32)
        bo = jnp.zeros((1, D), F32)
        bd = jnp.zeros((1, D), F32)
        for i in range(images):
            rows = slice(i * ROWS, (i + 1) * ROWS)
            kc = kcol[rows, 0:1]
            bd = bd + jnp.sum(kc, axis=0, keepdims=True) * dyb[i:i + 1, :]
            dh = dx[rows, :]
            xh = xh2[rows, :].astype(F32)
            g2 = g2 + jnp.sum(dh * xh, axis=0, keepdims=True)
            b2 = b2 + jnp.sum(dh, axis=0, keepdims=True)
            c = dh * vec_ref[5:6, :]
            m1 = jnp.mean(c, axis=1, keepdims=True)
            m2 = jnp.mean(c * xh, axis=1, keepdims=True)
            r = dy[i:i + 1, :] * kc + rstd2[rows, 0:1] * (c - m1 - xh * m2)
            dx[rows, :] = r
            rb = r.astype(BF)
            db[rows, :] = rb
            bo = bo + jnp.sum(rb.astype(F32), axis=0, keepdims=True)
        small_ref[0:4, :] = jnp.zeros((4, D), F32)
        small_ref[4:5, :] = bo
        small_ref[5:6, :] = g2
        small_ref[6:7, :] = b2
        small_ref[7:8, :] = bd
        for j in range(n_quads):
            sl = slice(j * TILE, (j + 1) * TILE)
            do_s[j] = mm(db[...], wout[sl, :], NT).astype(BF)
            put(n_up, j, mm(ot[...], db[:, sl]))
        for name in ("qkv", "h1t"):
            loads[name].wait()

    def unit_attend(m):
        j = m // 2

        def attend(ii, _):
            i = lax.rem(m, 2) * (images // 2) + ii
            r0_ = pl.multiple_of(i * ROWS, 16)
            step = j * images + i
            slot = lax.rem(step, 2)

            @pl.when(step + 1 < n_quads * images)
            def _():
                pcopy(step + 1).start()

            pcopy(step).wait()
            q4 = qkv[j, pl.ds(r0_, ROWS), :]
            k4 = qkv[n_quads + j, pl.ds(r0_, WIN), :]
            v4 = qkv[2 * n_quads + j, pl.ds(r0_, WIN), :]
            d4 = do_s[j, pl.ds(r0_, ROWS), :]
            dq = jnp.zeros((ROWS, TILE), F32)
            dk = jnp.zeros((WIN, TILE), F32)
            dv = jnp.zeros((WIN, TILE), F32)
            for h, mask in enumerate(masks):
                pb = p_s[slot, h * ROWS:(h + 1) * ROWS, :]
                dm = d4 * mask
                dv = dv + mm(pb, dm, TN)
                dpr = mm(dm, v4, NT)
                pf = pb.astype(F32)
                ds = (pf * (dpr - jnp.sum(pf * dpr, axis=1, keepdims=True))).astype(BF)
                dq = dq + mm(ds, k4 * mask)
                dk = dk + mm(ds, q4 * mask, TN)
            dq = dq * HEAD_DIM ** -0.5
            dv = dv[0:ROWS]
            sl = pl.ds(pl.multiple_of(j * TILE, TILE), TILE)
            small_ref[2:3, sl] += jnp.sum(dq, axis=0, keepdims=True)
            small_ref[3:4, sl] += jnp.sum(dv, axis=0, keepdims=True)
            for s, val in enumerate((dq, dk[0:ROWS], dv)):
                col = pl.multiple_of(s * D + j * TILE, TILE)
                dp_s[pl.ds(r0_, ROWS), pl.ds(col, TILE)] = val.astype(BF)
            return 0

        lax.fori_loop(0, images // 2, attend, 0)

        @pl.when(lax.rem(m, 2) == 1)
        def _():
            for s in range(3):
                col = pl.multiple_of(s * D + j * TILE, TILE)
                put(n_up + 1 + j, s, mm(h1t[...], dp_s[:, pl.ds(col, TILE)]))

    def unit_norm(i):
        @pl.when(i == 0)
        def _():
            for name in ("wqkv", "xh1", "rstd1"):
                loads[name].wait()

        rows = pl.ds(pl.multiple_of(i * ROWS, 16), ROWS)
        dh = mm(dp_s[rows, :], wqkv[...], NT)
        xh = xh1[rows, :].astype(F32)
        small_ref[0:1, :] += jnp.sum(dh * xh, axis=0, keepdims=True)
        small_ref[1:2, :] += jnp.sum(dh, axis=0, keepdims=True)
        c = dh * vec_ref[0:1, :]
        m1 = jnp.mean(c, axis=1, keepdims=True)
        m2 = jnp.mean(c * xh, axis=1, keepdims=True)
        r = dx[rows, :] + rstd1[rows, 0:1] * (c - m1 - xh * m2)
        for k in range(images):
            @pl.when(i == k)
            def _(k=k):
                tg_ref[k * SEQ:(k + 1) * SEQ, :] = r[0:SEQ]

    small_ref[...] = jnp.zeros_like(small_ref)
    loads["h2t"].wait()

    def unit(n, _):
        @pl.when(n < n_up)
        def _():
            unit_up(n)

        @pl.when(n == n_up)
        def _():
            unit_down()

        @pl.when(n == n_up + 1)
        def _():
            unit_mid()

        @pl.when((n >= first) & (n < first + 2 * n_quads))
        def _():
            unit_attend(n - first)

        @pl.when(n >= first + 2 * n_quads)
        def _():
            unit_norm(n - first - 2 * n_quads)

        tick(n)
        return 0

    lax.fori_loop(0, last_unit, unit, 0)

    def spread(src, sems, slot, devs):
        out = []
        for k, dev in enumerate(devs):
            d = pltpu.make_async_remote_copy(
                src, src, vs_sem.at[slot, k], vr_sem.at[slot, k], device_id=dev, device_id_type=MESH)
            d.start()
            out.append(d)
        return out

    def total(ref, count):
        v = ref[0]
        for k in range(1, count):
            v = v + ref[k]
        return v

    n = last_unit
    last_start = first + 2 * n_quads - 1
    vc[core] = small_ref[...]
    going = spread(vc.at[core], None, 0, [core_dev])
    for p in range(n - 1 - last_start, 5):
        advance(p, n_chunks - 1)
        for d in going:
            d.wait()
        going = []
        if p == n - 1 - last_start:
            vp[spot] = total(vc, 2)
            going = spread(vp.at[spot], None, 1, p_devs)
    for d in going:
        d.wait()
    vz[z] = total(vp, plane)
    for d in spread(vz.at[z], None, 2, z_devs):
        d.wait()
    small_ref[...] = total(vz, cz)
    for c in range(n_up):
        ug_ref[:, c * D:(c + 1) * D] = res[c]
    og_ref[...] = res[n_up]
    for j in range(n_quads):
        for s in range(3):
            qg_ref[:, s * D + j * TILE:s * D + (j + 1) * TILE] = res[n_up + 1 + j, :, s * TILE:(s + 1) * TILE]


def backward_call(n_row, n_col, images, ff, dy, da, vec, wqkv, wout, wup, acts):
    span = images * ROWS
    nq = D // TILE
    wide = span + WIN - ROWS
    cz = ff // D
    cy = n_col // (2 * cz)
    blk = D // n_col
    n_a = 256 if n_row == 2 else D
    n_h = max((D - n_a) // 2, 128)
    n_ch = ff // D + 1 + nq
    plane = n_row * cy
    n_sem = 5 * (max(cy, cz, n_row) - 1 + max(cy, cz))
    anyspec = pl.BlockSpec(memory_space=pl.ANY)
    vm = pl.BlockSpec(memory_space=pltpu.VMEM)
    outs = [(images * SEQ, D), (blk, 3 * D), (blk, D), (blk, ff), (16, D)]
    B16 = lambda *s: pltpu.VMEM(s, BF)
    B32 = lambda *s: pltpu.VMEM(s, F32)
    scratch = [
        B16(D, 3 * D), B16(D, D), B16(D, ff), B16(D, span), B16(3 * nq, wide, TILE), B16(D, span), B16(D, span),
        B16(span, D), B16(span, D), B32(span, 128), B32(span, 128), B32(span, 128),
        B16(2, 4 * ROWS, TILE), B16(span, ff), B32(span, D), B16(span, D), B16(nq, span, TILE), B16(span, 3 * D),
        B16(2, cz, cy, 2, blk, D), B16(n_ch, cz, cy, blk, D),
        B16(n_ch, cy - 1, cz, blk, n_a), B16(n_ch, cz, cy, blk, n_h),
        B16(n_ch, cz - 1, blk, n_a), B16(n_ch, cy - 1, cz, blk, n_h),
        B16(n_ch, n_row, blk, n_a), B16(n_ch, cz - 1, blk, n_h), B16(n_ch, blk, n_h), B32(n_ch, blk, D),
        B32(2, 16, D), B32(plane, 16, D), B32(cz, 16, D),
        pltpu.SemaphoreType.DMA((12,)), pltpu.SemaphoreType.DMA((ff // TILE,)), pltpu.SemaphoreType.DMA((2,)),
        pltpu.SemaphoreType.DMA((n_ch, n_sem)), pltpu.SemaphoreType.DMA((n_ch, n_sem)),
        pltpu.SemaphoreType.DMA((3, plane)), pltpu.SemaphoreType.DMA((3, plane)),
    ]
    return pl.pallas_call(
        functools.partial(backward_kernel, n_row, cz, cy, images, ff, n_a),
        out_shape=[jax.ShapeDtypeStruct(s, F32) for s in outs],
        in_specs=[vm] * 3 + [anyspec] * 14,
        out_specs=[vm] * len(outs),
        scratch_shapes=scratch,
        compiler_params=pltpu.CompilerParams(
            vmem_limit_bytes=62 * 2**20, collective_id=1, has_side_effects=True),
        name="block_backward",
    )(dy, da, vec, wqkv, wout, wup, *acts)


def per_device(
    tokens,
    keep_mask,
    w_qkv,
    w_out,
    w_up,
    w_down,
    vectors,
    up_bias,
    w_proj,
    texts,
    pair_index,
    logit_scale,
):
    images = keep_mask.shape[0]
    ff = w_up.shape[1]
    n_row, shards = lax.axis_size("row"), lax.axis_size("col")
    mine = lax.axis_index("col")
    acts = forward_call(
        images, ff, tokens, keep_mask, w_qkv, w_out, w_up, w_down, vectors, up_bias.reshape(1, ff)
    )
    loss, dy, da, text_grad, grad_proj, grad_down = head_call(
        n_row, shards, images, ff, acts[12], texts, acts[11], pair_index.reshape(1, -1), logit_scale, w_proj, w_down
    )
    token_grad, qkv_share, out_share, up_share, small = backward_call(
        n_row, shards, images, ff, dy, da, vectors, w_qkv, w_out, w_up, acts[:11]
    )
    vec_share = lax.dynamic_slice_in_dim(small[:8], mine * (D // shards), D // shards, axis=1)
    bias_share = lax.dynamic_slice_in_dim(small[8 : 8 + ff // D].reshape(ff), mine * (ff // shards), ff // shards)
    return (
        loss.reshape(1),
        token_grad,
        qkv_share,
        out_share,
        up_share,
        grad_down,
        vec_share,
        bias_share,
        grad_proj,
        text_grad,
    )


def solution(mesh):
    in_specs = (
        P(("row", "col"), None),
        P(("row", "col"), None),
        P(),
        P(),
        P(),
        P(),
        P(),
        P(),
        P(),
        P(("row", "col"), None),
        P(),
        P(),
    )
    out_specs = (
        P(),
        P(("row", "col"), None),
        P("col", None),
        P("col", None),
        P("col", None),
        P("col", None),
        P(None, "col"),
        P("col"),
        P("col", None),
        P(("row", "col"), None),
    )
    return jax.shard_map(
        per_device, mesh=mesh, in_specs=in_specs, out_specs=out_specs, check_vma=False
    )
```

```python
import functools

import jax
import jax.numpy as jnp
from jax import lax
from jax.experimental import pallas as pl
from jax.experimental.pallas import tpu as pltpu
from jax.sharding import PartitionSpec as P

D = 768
HEADS = 12
HEAD_DIM = 64
SEQ = 197
EMB = 512
ROWS = 208
WIN = 256
TILE = 256
F32 = jnp.float32
BF = jnp.bfloat16
NT = (((1,), (1,)), ((), ()))
TN = (((0,), (0,)), ((), ()))


def mm(a, b, dims=(((1,), (0,)), ((), ()))):
    return lax.dot_general(a, b, dims, preferred_element_type=F32)


def head_masks():
    lane = lax.broadcasted_iota(jnp.int32, (1, TILE), 1) // HEAD_DIM
    return [(lane == h).astype(F32).astype(BF) for h in range(TILE // HEAD_DIM)]


def gelu_pair(u):
    z = jnp.abs(u)
    t = 1.0 / (1.0 + (0.3275911 * 0.7071067811865476) * z)
    e = jnp.exp(-0.5 * (u * u))
    poly = 0.5 * 1.061405429
    for c in (-1.453152027, 1.421413741, -0.284496736, 0.254829592):
        poly = poly * t + 0.5 * c
    tail = poly * t * e
    cdf = jnp.where(u >= 0.0, 1.0 - tail, tail)
    return u * cdf, cdf + (0.3989422804014327 * u) * e


def forward_kernel(
    images, ff,
    tok_ref, keep_ref, wqkv_h, wout_h, wup_h, wdown_h, vec_ref, upb_ref,
    h1t_h, qkv_h, p_h, ot_h, h2t_h, xh1_h, xh2_h, rstd1_h, rstd2_h, kcol_h, gk_h, apool_ref, pooled_ref,
    wqkv, wout, wup, wdown, xs, h1t, qkv, p_s, ot, h2t, xh1, xh2, rstd1, rstd2, kcol, gk,
    h1, o_s, h2, a_s, keep8, kmask, bias, acc,
    in_sem, out_sem,
):
    n_quads = D // TILE
    n_ff = ff // TILE
    loads = []
    for k, (src, dst) in enumerate(((wqkv_h, wqkv), (wout_h, wout), (wup_h, wup), (wdown_h, wdown))):
        c = pltpu.make_async_copy(src, dst, in_sem.at[k])
        c.start()
        loads.append(c)
    stores = []

    def send(k, src, dst):
        c = pltpu.make_async_copy(src, dst, out_sem.at[k])
        c.start()
        stores.append(c)

    total = images * SEQ
    last = total // 16 * 16
    xs[last:, :] = jnp.zeros_like(xs[last:, :])
    xs[0:last, :] = tok_ref[0:last, :].astype(F32)
    if last < total:
        xs[last:total, :] = tok_ref[last:total, :].astype(F32)
    keep8[...] = jnp.zeros_like(keep8)
    keep8[0:images, 0:SEQ] = keep_ref[...].astype(F32)
    kb = keep8[...]
    rid = lax.broadcasted_iota(jnp.int32, kb.shape, 0)
    for i in range(images):
        kmask[i] = jnp.where(rid == i, kb, 0.0).astype(BF)
        one = jnp.ones((kb.shape[0], 128), F32).astype(BF)
        kcol[i * ROWS:(i + 1) * ROWS, :] = mm(kmask[i], one, TN)[0:ROWS]
    send(0, kcol, kcol_h)
    bias[0:1, 0:D] = vec_ref[2:3, :]
    bias[0:1, D:2 * D] = jnp.zeros((1, D), F32)
    bias[0:1, 2 * D:] = vec_ref[3:4, :]
    for i in range(images):
        x = xs[i * SEQ:i * SEQ + ROWS, :]
        cen = x - jnp.mean(x, axis=1, keepdims=True)
        inv = lax.rsqrt(jnp.mean(cen * cen, axis=1, keepdims=True) + 1e-6)
        xh = cen * inv
        rows = slice(i * ROWS, (i + 1) * ROWS)
        xh1[rows, :] = xh.astype(BF)
        rstd1[rows, :] = jnp.broadcast_to(inv, (ROWS, 128))
        h1[rows, :] = (xh * vec_ref[0:1, :] + vec_ref[1:2, :]).astype(BF)
    send(8, xh1, xh1_h)
    send(9, rstd1, rstd1_h)
    h1t[...] = h1[...].T
    send(10, h1t, h1t_h)
    loads[0].wait()
    span = images * ROWS
    pad = qkv.shape[1] - span
    for t in range(3 * n_quads):
        qkv[t, span:, :] = jnp.zeros((pad, TILE), BF)

    def proj(t, _):
        col = pl.multiple_of(t * TILE, TILE)
        r = mm(h1[...], wqkv[:, pl.ds(col, TILE)]) + bias[0:1, pl.ds(col, TILE)]
        r = r * jnp.where(t < n_quads, HEAD_DIM ** -0.5, 1.0)
        qkv[t, 0:span, :] = r.astype(BF)
        return 0

    lax.fori_loop(0, 3 * n_quads, proj, 0)
    send(1, qkv, qkv_h)
    masks = head_masks()

    def attend(it, _):
        i = it // n_quads
        j = it % n_quads
        r0 = pl.multiple_of(i * ROWS, 16)
        q4 = qkv[j, pl.ds(r0, ROWS), :]
        k4 = qkv[n_quads + j, pl.ds(r0, WIN), :]
        v4 = qkv[2 * n_quads + j, pl.ds(r0, WIN), :]
        valid = keep8[pl.ds(i, 1), :] > 0.0
        out = jnp.zeros((ROWS, TILE), F32)
        for h, m in enumerate(masks):
            s = mm(q4 * m, k4, NT)
            s = jnp.where(valid, s, -1e30)
            e = jnp.exp(s - jnp.max(s, axis=1, keepdims=True))
            pb = (e * (1.0 / jnp.sum(e, axis=1, keepdims=True))).astype(BF)
            p_s[it, h * ROWS:(h + 1) * ROWS, :] = pb
            out = out + mm(pb, v4 * m)
        o_s[j, pl.ds(r0, ROWS), :] = out.astype(BF)
        return 0

    lax.fori_loop(0, images * n_quads, attend, 0)
    send(2, p_s, p_h)
    for j in range(n_quads):
        ot[j * TILE:(j + 1) * TILE, :] = o_s[j].T
    send(3, ot, ot_h)
    loads[1].wait()
    pooled_ref[...] = jnp.zeros_like(pooled_ref)
    for i in range(images):
        rows = slice(i * ROWS, (i + 1) * ROWS)
        x = xs[i * SEQ:i * SEQ + ROWS, :]
        y = x + vec_ref[4:5, :]
        for j in range(n_quads):
            y = y + mm(o_s[j, rows, :], wout[j * TILE:(j + 1) * TILE, :])
        kc = kcol[rows, 0:1]
        pooled_ref[i:i + 1, 0:D] = jnp.sum(y * kc, axis=0, keepdims=True)
        cen = y - jnp.mean(y, axis=1, keepdims=True)
        inv = lax.rsqrt(jnp.mean(cen * cen, axis=1, keepdims=True) + 1e-6)
        xh = cen * inv
        xh2[rows, :] = xh.astype(BF)
        rstd2[rows, :] = jnp.broadcast_to(inv, (ROWS, 128))
        h2[rows, :] = (xh * vec_ref[5:6, :] + vec_ref[6:7, :]).astype(BF)
    h2t[...] = h2[...].T
    send(4, h2t, h2t_h)
    send(5, xh2, xh2_h)
    send(6, rstd2, rstd2_h)
    loads[2].wait()
    loads[3].wait()
    acc[...] = jnp.zeros_like(acc)
    a_s[span:, :] = jnp.zeros((a_s.shape[0] - span, TILE), BF)

    def feed(t, _):
        col = pl.multiple_of(t * TILE, TILE)
        ub = upb_ref[0:1, pl.ds(col, TILE)]
        for i in range(images):
            rows = slice(i * ROWS, (i + 1) * ROWS)
            u = mm(h2[rows, :], wup[:, pl.ds(col, TILE)]) + ub
            a, g = gelu_pair(u)
            a_s[rows, :] = a.astype(BF)
            gk[t, rows, :] = (g * kcol[rows, 0:1]).astype(BF)
        ap = jnp.zeros((kmask.shape[1], TILE), F32)
        for i in range(images):
            ap = ap + mm(kmask[i], a_s[i * ROWS:i * ROWS + WIN, :])
        at = pl.multiple_of((t % n_quads) * TILE, TILE)
        apool_ref[t // n_quads, :, pl.ds(at, TILE)] = ap[0:8]
        hi = ap.astype(BF)
        lo = (ap - hi.astype(F32)).astype(BF)
        w = wdown[pl.ds(col, TILE), :]
        acc[...] += mm(hi, w) + mm(lo, w)
        pltpu.make_async_copy(gk.at[t], gk_h.at[t], out_sem.at[7]).start()
        return 0

    lax.fori_loop(0, n_ff, feed, 0)
    cnt = jnp.sum(kb, axis=1, keepdims=True)[0:8]
    inv = 1.0 / jnp.maximum(cnt, 1.0)
    pooled_ref[:, 0:D] = (pooled_ref[:, 0:D] + acc[0:8, :]) * inv + vec_ref[7:8, :]
    pooled_ref[:, D:] = jnp.broadcast_to(cnt, (8, 128))
    for c in stores:
        c.wait()
    for t in range(n_ff):
        pltpu.make_async_copy(gk.at[t], gk_h.at[t], out_sem.at[7]).wait()


def forward_call(images, ff, tokens, keep, wqkv, wout, wup, wdown, vec, upb):
    span = images * ROWS
    nq = D // TILE
    wide = span + WIN - ROWS
    outs = [
        ((D, span), BF), ((3 * nq, wide, TILE), BF), ((images * nq, 4 * ROWS, TILE), BF),
        ((D, span), BF), ((D, span), BF), ((span, D), BF), ((span, D), BF), ((span, 128), F32), ((span, 128), F32),
        ((span, 128), F32), ((ff // TILE, span, TILE), BF), ((ff // D, 8, D), F32), ((8, D + 128), F32),
    ]
    anyspec = pl.BlockSpec(memory_space=pl.ANY)
    vm = pl.BlockSpec(memory_space=pltpu.VMEM)
    scratch = [
        pltpu.VMEM((D, 3 * D), BF), pltpu.VMEM((D, D), BF), pltpu.VMEM((D, ff), BF), pltpu.VMEM((ff, D), BF),
        pltpu.VMEM(((images - 1) * SEQ + ROWS + 7 & -8, D), F32),
    ] + [pltpu.VMEM(*o) for o in outs[:11]] + [
        pltpu.VMEM((span, D), BF), pltpu.VMEM((nq, span, TILE), BF), pltpu.VMEM((span, D), BF),
        pltpu.VMEM((wide, TILE), BF), pltpu.VMEM((16, WIN), F32), pltpu.VMEM((images, 16, WIN), BF),
        pltpu.VMEM((1, 3 * D), F32), pltpu.VMEM((16, D), F32),
        pltpu.SemaphoreType.DMA((4,)), pltpu.SemaphoreType.DMA((11,)),
    ]
    return pl.pallas_call(
        functools.partial(forward_kernel, images, ff),
        out_shape=[jax.ShapeDtypeStruct(s, d) for s, d in outs],
        in_specs=[vm, vm] + [anyspec] * 4 + [vm, vm],
        out_specs=[anyspec] * 11 + [vm, vm],
        scratch_shapes=scratch,
        compiler_params=pltpu.CompilerParams(vmem_limit_bytes=60 * 2**20),
        name="block_forward",
    )(tokens, keep, wqkv, wout, wup, wdown, vec, upb)


def split3(x):
    hi = x.astype(BF)
    r = x - hi.astype(F32)
    mid = r.astype(BF)
    lo = (r - mid.astype(F32)).astype(BF)
    return hi, mid, lo


NN = (((1,), (0,)), ((), ()))
MESH = pl.DeviceIdType.MESH


def mm3(x, w, dims=NN):
    hi, mid, lo = split3(x)
    return (mm(lo, w, dims) + mm(mid, w, dims)) + mm(hi, w, dims)


def place(cz, cy):
    row = lax.axis_index("row")
    col = lax.axis_index("col")
    return row, col // (2 * cy), lax.rem(col // 2, cy), lax.rem(col, 2)


def head_kernel(
    n_row, cz, cy, images, ff,
    pooled_ref, texts_ref, apool_ref, pair_ref, scale_ref, wproj_ref, wdown_h,
    loss_ref, dy_ref, da_ref, text_ref, proj_ref, down_ref,
    pg, ax, ag, wdown, p_all, t_all, c_all, a_all, gproj, gdown,
    in_sem, zs, zr, ps, pr, cs, cr,
):
    x, z, y, core = place(cz, cy)
    load = pltpu.make_async_copy(wdown_h, wdown, in_sem.at[0])
    load.start()
    half = D // 2
    plane = n_row * cy
    spot = x * cy + y

    def device(xx, zz, yy, cc):
        return (xx, (zz * cy + yy) * 2 + cc)

    z_peers = [lax.rem(z + k, cz) for k in range(1, cz)]
    p_peers = [lax.rem(spot + k, plane) for k in range(1, plane)]
    bar = pltpu.get_barrier_semaphore()
    for zz in z_peers:
        pl.semaphore_signal(bar, inc=1, device_id=device(x, zz, y, core), device_id_type=MESH)
    for pp in p_peers:
        pl.semaphore_signal(bar, inc=1, device_id=device(pp // cy, z, lax.rem(pp, cy), core), device_id_type=MESH)
    pl.semaphore_signal(bar, inc=1, device_id=device(x, z, y, 1 - core), device_id_type=MESH)
    mine = jnp.concatenate([
        pooled_ref[0:images, 0:D],
        jnp.concatenate([texts_ref[...].astype(F32), pooled_ref[0:images, D:], jnp.zeros((images, D - EMB - 128), F32)], axis=1),
    ], axis=0)
    pg[x, z, y, core] = mine
    for g in range(cz):
        ax[g, 0:images] = apool_ref[g, 0:images, 0:half]
        ax[g, images:] = apool_ref[g, 0:images, half:]
    ag[x, z, y, core] = ax[z]
    pl.semaphore_wait(bar, cz - 1 + plane - 1 + 1)

    def stage(src, dst, sems, slot, devs):
        out = []
        for k, (s, dev) in enumerate(zip(src, devs)):
            c = pltpu.make_async_remote_copy(
                s, dst, sems[0].at[slot, k], sems[1].at[slot, k], device_id=dev, device_id_type=MESH)
            c.start()
            out.append(c)
        return out

    z_devs = [device(x, zz, y, core) for zz in z_peers]
    p_devs = [device(pp // cy, z, lax.rem(pp, cy), core) for pp in p_peers]
    c_devs = [device(x, z, y, 1 - core)]
    own = pg.at[x, z, y, core]
    first = stage([own] * len(z_devs), own, (zs, zr), 0, z_devs)
    first_a = stage([ax.at[zz] for zz in z_peers], ag.at[x, z, y, core], (zs, zr), 1, z_devs)
    for c in first:
        c.wait()
    own = pg.at[x, :, y, core]
    second = stage([own] * len(p_devs), own, (ps, pr), 0, p_devs)
    for c in first_a:
        c.wait()
    own = ag.at[x, :, y, core]
    second_a = stage([own] * len(p_devs), own, (ps, pr), 1, p_devs)
    for c in second:
        c.wait()
    own = pg.at[:, :, :, core]
    third = stage([own], own, (cs, cr), 0, c_devs)
    for c in second_a:
        c.wait()
    own = ag.at[:, :, :, core]
    third_a = stage([own], own, (cs, cr), 1, c_devs)
    for c in third:
        c.wait()
    n_col = cz * cy * 2
    n_img = n_row * n_col * images
    for d in range(n_row * n_col):
        rows = slice(d * images, (d + 1) * images)
        at = (d // n_col, d % n_col // (2 * cy), d // 2 % cy, d % 2)
        p_all[rows, :] = pg[at + (slice(0, images), slice(0, D))]
        t_all[rows, :] = pg[at + (slice(images, 2 * images), slice(0, EMB))]
        c_all[rows, :] = pg[at + (slice(images, 2 * images), slice(EMB, EMB + 128))]
    scale = scale_ref[0]
    pooled = p_all[...]
    latent = mm3(pooled, wproj_ref[...])
    norm = lax.rsqrt(jnp.sum(latent * latent, axis=1, keepdims=True) + 1e-6)
    embeds = latent * norm
    eb = embeds.astype(BF)
    tb = t_all[...].astype(BF)
    logits = scale * mm(eb, tb, NT)
    row_max = jnp.max(logits, axis=1, keepdims=True)
    row_exp = jnp.exp(logits - row_max)
    row_sum = jnp.sum(row_exp, axis=1, keepdims=True)
    col_max = jnp.max(logits, axis=0, keepdims=True)
    col_exp = jnp.exp(logits - col_max)
    col_sum = jnp.sum(col_exp, axis=0, keepdims=True)
    ids = lax.broadcasted_iota(jnp.int32, (n_img, n_img), 0)
    match = (ids == pair_ref[...]).astype(F32).T
    grad = 0.5 * (row_exp / row_sum) + 0.5 * (col_exp / col_sum) - match
    lse = jnp.sum(row_max + jnp.log(row_sum), axis=0, keepdims=True) + jnp.sum(
        col_max + jnp.log(col_sum), axis=1, keepdims=True)
    hits = jnp.sum(jnp.sum(logits * match, axis=1, keepdims=True), axis=0, keepdims=True)
    loss_ref[...] = (0.5 * lse - hits) * (1.0 / n_img)
    de = scale * mm3(grad, tb)
    dz = norm * (de - embeds * jnp.sum(embeds * de, axis=1, keepdims=True))
    image_grad = mm3(dz, wproj_ref[...], NT) / c_all[:, 0:1]
    dev = x * n_col + (z * cy + y) * 2 + core
    want = lax.broadcasted_iota(jnp.int32, (16, n_img), 0) + dev * images
    have = lax.broadcasted_iota(jnp.int32, (16, n_img), 1)
    pick = (want == have).astype(F32).astype(BF)
    hi, mid, lo = split3(image_grad)
    dy = (mm(pick, lo) + mm(pick, mid)) + mm(pick, hi)
    dy_ref[...] = dy[0:8]
    dyb = dy.astype(BF)
    load.wait()

    def spread(t, _):
        col = pl.multiple_of(t * TILE, TILE)
        da_ref[:, pl.ds(col, TILE)] = mm(dyb, wdown[pl.ds(col, TILE), :], NT)[0:8]
        return 0

    lax.fori_loop(0, ff // TILE, spread, 0)
    g_hi, g_mid, g_lo = split3(grad)
    own_grad = (mm(pick, g_lo, NT) + mm(pick, g_mid, NT)) + mm(pick, g_hi, NT)
    text_ref[...] = (scale * mm3(own_grad, eb))[0:images]
    p_hi, p_lo, _ = split3(pooled)
    d_hi, d_lo, _ = split3(dz)
    gproj[...] = (mm(p_lo, d_hi, TN) + mm(p_hi, d_lo, TN)) + mm(p_hi, d_hi, TN)
    n_proj = D // n_col
    at = pl.multiple_of(((z * cy + y) * 2 + core) * n_proj, 8)
    proj_ref[...] = gproj[pl.ds(at, n_proj), :]
    for c in third_a:
        c.wait()
    for d in range(n_row * n_col):
        rows = slice(d * images, (d + 1) * images)
        at = (d // n_col, d % n_col // (2 * cy), d // 2 % cy, d % 2)
        a_all[rows, 0:half] = ag[at + (slice(0, images),)]
        a_all[rows, half:] = ag[at + (slice(images, 2 * images),)]
    acts = a_all[...]
    a_hi = acts.astype(BF)
    a_lo = (acts - a_hi.astype(F32)).astype(BF)
    for n in range(D // TILE):
        sl = slice(n * TILE, (n + 1) * TILE)
        gdown[:, sl] = mm(a_lo, hi[:, sl], TN) + mm(a_hi, hi[:, sl], TN)
    n_down = ff // n_col
    at = pl.multiple_of((y * 2 + core) * n_down, 8)
    down_ref[...] = gdown[pl.ds(at, n_down), :]


def head_call(n_row, n_col, images, ff, pooled, texts, apool, pair, scale, wproj, wdown):
    cz = ff // D
    cy = n_col // (2 * cz)
    n_img = n_row * n_col * images
    vm = pl.BlockSpec(memory_space=pltpu.VMEM)
    outs = [(1, 1), (8, D), (8, ff), (images, EMB), (D // n_col, EMB), (ff // n_col, D)]
    plane = n_row * cy
    grid = (n_row, cz, cy, 2, 2 * images)
    scratch = [
        pltpu.VMEM(grid + (D,), F32), pltpu.VMEM((cz, 2 * images, D // 2), F32), pltpu.VMEM(grid + (D // 2,), F32),
        pltpu.VMEM((ff, D), BF), pltpu.VMEM((n_img, D), F32), pltpu.VMEM((n_img, EMB), F32),
        pltpu.VMEM((n_img, 128), F32), pltpu.VMEM((n_img, D), F32), pltpu.VMEM((D, EMB), F32), pltpu.VMEM((D, D), F32),
        pltpu.SemaphoreType.DMA((1,)), pltpu.SemaphoreType.DMA((2, cz)), pltpu.SemaphoreType.DMA((2, cz)),
        pltpu.SemaphoreType.DMA((2, plane)), pltpu.SemaphoreType.DMA((2, plane)),
        pltpu.SemaphoreType.DMA((2, 1)), pltpu.SemaphoreType.DMA((2, 1)),
    ]
    return pl.pallas_call(
        functools.partial(head_kernel, n_row, cz, cy, images, ff),
        out_shape=[jax.ShapeDtypeStruct(s, F32) for s in outs],
        in_specs=[vm] * 4 + [pl.BlockSpec(memory_space=pltpu.SMEM), vm, pl.BlockSpec(memory_space=pl.ANY)],
        out_specs=[vm] * len(outs),
        scratch_shapes=scratch,
        compiler_params=pltpu.CompilerParams(
            vmem_limit_bytes=60 * 2**20, collective_id=0, has_side_effects=True),
        name="contrastive_head",
    )(pooled, texts, apool, pair, scale, wproj, wdown)


READY = [2, 5, 8, 11, 18, 23, 28, 33]
WAITS = [[(7, 0), (9, 1), (12, 2), (13, 3), (20, 4), (25, 5), (30, 6), (35, 7)], [(14, 0), (17, 1), (21, 2), (24, 3), (27, 4), (31, 5), (35, 6)], [(19, 0), (21, 1), (26, 2), (27, 3), (32, 4), (35, 5)], [(24, 0), (27, 1), (31, 2), (32, 3), (36, 4)], [(28, 0), (31, 1), (35, 2), (36, 3)]]
TAIL = [(3, 5), (2, 6), (1, 7), (4, 4), (4, 5), (3, 6), (4, 6), (2, 7), (3, 7), (4, 7)]


def backward_kernel(
    n_row, cz, cy, images, ff, n_a,
    dy_ref, da_ref, vec_ref,
    wqkv_h, wout_h, wup_h, h1t_h, qkv_h, p_h, ot_h, h2t_h, xh1_h, xh2_h, rstd1_h, rstd2_h, kcol_h, gk_h,
    tg_ref, qg_ref, og_ref, ug_ref, small_ref,
    wqkv, wout, wup, h1t, qkv, ot, h2t, xh1, xh2, rstd1, rstd2, kcol, p_s, du, dx, db, do_s, dp_s,
    g, r0, r1a, r1b, r2a, r2b, r3a, r3b, r4b, res, vc, vp, vz, sv, small_s,
    in_sem, gk_sem, p_sem, s_sem, r_sem, vs_sem, vr_sem,
):
    n_quads = D // TILE
    n_ff = ff // TILE
    n_up = ff // D
    n_chunks = n_up + 1 + n_quads
    masks = head_masks()
    x, z, y, core = place(cz, cy)
    two = n_a < D
    n_h = (D - n_a) // 2
    plane = n_row * cy
    spot = x * cy + y

    def device(xx, zz, yy, cc):
        return (xx, (zz * cy + yy) * 2 + cc)

    core_dev = device(x, z, y, 1 - core)
    y_peers = [lax.rem(y + k, cy) for k in range(1, cy)]
    z_peers = [lax.rem(z + k, cz) for k in range(1, cz)]
    x_peers = [lax.rem(x + k, n_row) for k in range(1, n_row)]
    p_peers = [lax.rem(spot + k, plane) for k in range(1, plane)]
    z_devs = [device(x, zz, y, core) for zz in z_peers]
    y_devs = [device(x, z, yy, core) for yy in y_peers]
    x_devs = [device(xx, z, y, core) for xx in x_peers]
    p_devs = [device(pp // cy, z, lax.rem(pp, cy), core) for pp in p_peers]

    loads = {}
    for k, (name, src, dst) in enumerate((
        ("kcol", kcol_h, kcol), ("h2t", h2t_h, h2t), ("wup", wup_h, wup), ("xh2", xh2_h, xh2),
        ("rstd2", rstd2_h, rstd2), ("wout", wout_h, wout), ("ot", ot_h, ot), ("qkv", qkv_h, qkv),
        ("h1t", h1t_h, h1t), ("wqkv", wqkv_h, wqkv), ("xh1", xh1_h, xh1), ("rstd1", rstd1_h, rstd1),
    )):
        loads[name] = pltpu.make_async_copy(src, dst, in_sem.at[k])

    def gcopy(t):
        col = pl.multiple_of(t * TILE, TILE)
        return pltpu.make_async_copy(gk_h.at[t], du.at[:, pl.ds(col, TILE)], gk_sem.at[t])

    loads["h2t"].start()
    for t in range(n_ff):
        gcopy(t).start()
    for name in ("kcol", "wup", "xh2", "rstd2", "wout", "ot", "qkv", "h1t", "wqkv", "xh1", "rstd1"):
        loads[name].start()

    def pcopy(step):
        i = lax.rem(step, images)
        j = step // images
        slot = lax.rem(step, 2)
        return pltpu.make_async_copy(p_h.at[i * n_quads + j], p_s.at[slot], p_sem.at[slot])

    pcopy(0).start()
    bar = pltpu.get_barrier_semaphore()
    for dev in z_devs + p_devs + [core_dev]:
        pl.semaphore_signal(bar, inc=1, device_id=dev, device_id_type=MESH)
    half = lambda which: pl.ds(pl.multiple_of(n_a + which * n_h, 128), n_h)

    def copies(p, c):
        if p == 0:
            out = [(g.at[lax.rem(c, 4), :, :, 1 - core], r0.at[c], core_dev)]
        elif p == 1:
            out = [(r0.at[c, :, yy, :, 0:n_a], r1a.at[c, k], dev) for k, (yy, dev) in enumerate(zip(y_peers, y_devs))]
            if two:
                out += [(r0.at[c, :, :, :, half(1 - x)], r1b.at[c], x_devs[0])]
        elif p == 2:
            out = [(r1a.at[c, 0, zz], r2a.at[c, k], dev) for k, (zz, dev) in enumerate(zip(z_peers, z_devs))]
            if two:
                out += [(r1b.at[c, :, yy], r2b.at[c, k], dev) for k, (yy, dev) in enumerate(zip(y_peers, y_devs))]
        elif p == 3:
            out = [(r3a.at[c, x], r3a.at[c, x], dev) for dev in x_devs]
            if two:
                out += [(r2b.at[c, 0, zz], r3b.at[c, k], dev) for k, (zz, dev) in enumerate(zip(z_peers, z_devs))]
        else:
            out = [(r3b.at[c, 0], r4b.at[c], x_devs[0])] if two else []
        base = (0, 1, 1 + cy, cz + 2 * cy - 1, 2 * cz + 2 * cy + n_row - 3)[p]
        return [
            pltpu.make_async_remote_copy(
                src, dst, s_sem.at[lax.rem(c, 4), base + k], r_sem.at[c, base + k], device_id=dev, device_id_type=MESH)
            for k, (src, dst, dev) in enumerate(out)
        ]

    def finish(p, c):
        up = lambda v: v.astype(F32)
        if p == 0:
            r0[c] = r0[c] + g[lax.rem(c, 4), :, :, core]
        elif p == 1:
            v = up(r0[c, :, y, :, 0:n_a])
            for k in range(cy - 1):
                v = v + up(r1a[c, k])
            r1a[c, 0] = v.astype(BF)
            if two:
                r1b[c] = r1b[c] + r0[c, :, :, :, half(x)]
        elif p == 2:
            v = up(r1a[c, 0, z])
            for k in range(cz - 1):
                v = v + up(r2a[c, k])
            r3a[c, x] = v.astype(BF)
            if two:
                v = up(r1b[c, :, y])
                for k in range(cy - 1):
                    v = v + up(r2b[c, k])
                r2b[c, 0] = v.astype(BF)
        elif p == 3:
            v = up(r3a[c, 0])
            for k in range(1, n_row):
                v = v + up(r3a[c, k])
            res[c, :, 0:n_a] = v
            if two:
                v = up(r2b[c, 0, z])
                for k in range(cz - 1):
                    v = v + up(r3b[c, k])
                v = v.astype(BF)
                r3b[c, 0] = v
                res[c, :, half(x)] = up(v)
        elif two:
            res[c, :, half(1 - x)] = up(r4b[c])

    def begin(p, c):
        for d in copies(p, c):
            d.start()

    def advance(p, c):
        for d in copies(p, c):
            d.wait()
        finish(p, c)
        if p < 4:
            begin(p + 1, c)

    def lookup(n, events):
        hit = n < 0
        c = jnp.int32(0)
        for at, chunk in events:
            same = n == at
            hit = hit | same
            c = jnp.where(same, chunk, c)
        return hit, c

    def tick(n):
        @pl.when(n == READY[0])
        def _():
            pl.semaphore_wait(bar, len(z_devs) + len(p_devs) + 1)

        hit, c = lookup(n, [(at, k) for k, at in enumerate(READY)])

        @pl.when(hit)
        def _():
            begin(0, c)

        for p in range(4, -1, -1):
            hit, c = lookup(n, WAITS[p])

            @pl.when(hit)
            def _(p=p, c=c):
                advance(p, c)

    def put(c, tt, part):
        col = pl.multiple_of(tt * TILE, TILE)
        g[lax.rem(c, 4), :, :, :, :, pl.ds(col, TILE)] = part.reshape(g.shape[1:5] + (TILE,)).astype(BF)

    def unit_up(t):
        n = t // n_quads
        tt = lax.rem(t, n_quads)
        col = pl.multiple_of(t * TILE, TILE)
        gcopy(t).wait()
        ub = jnp.zeros((1, TILE), F32)
        for i in range(images):
            rows = slice(i * ROWS, (i + 1) * ROWS)
            d = du[rows, pl.ds(col, TILE)].astype(F32) * da_ref[i:i + 1, pl.ds(col, TILE)]
            ub = ub + jnp.sum(d, axis=0, keepdims=True)
            du[rows, pl.ds(col, TILE)] = d.astype(BF)
        scol = pl.multiple_of(tt * TILE, TILE)
        small_s[pl.ds(8 + n, 1), pl.ds(scol, TILE)] = ub
        put(n, tt, mm(h2t[...], du[:, pl.ds(col, TILE)]))

    def unit_down(n):
        @pl.when(n == 0)
        def _():
            loads["wup"].wait()

        col = pl.multiple_of(n * TILE, TILE)
        dx[:, pl.ds(col, TILE)] = mm(du[...], wup[pl.ds(col, TILE), :], NT)

    def unit_mid():
        for name in ("kcol", "xh2", "rstd2", "wout", "ot"):
            loads[name].wait()
        dy = dy_ref[...]
        dyb = dy.astype(BF).astype(F32)
        g2 = jnp.zeros((1, D), F32)
        b2 = jnp.zeros((1, D), F32)
        bo = jnp.zeros((1, D), F32)
        bd = jnp.zeros((1, D), F32)
        for i in range(images):
            rows = slice(i * ROWS, (i + 1) * ROWS)
            kc = kcol[rows, 0:1]
            bd = bd + jnp.sum(kc, axis=0, keepdims=True) * dyb[i:i + 1, :]
            dh = dx[rows, :]
            xh = xh2[rows, :].astype(F32)
            g2 = g2 + jnp.sum(dh * xh, axis=0, keepdims=True)
            b2 = b2 + jnp.sum(dh, axis=0, keepdims=True)
            c = dh * vec_ref[5:6, :]
            m1 = jnp.mean(c, axis=1, keepdims=True)
            m2 = jnp.mean(c * xh, axis=1, keepdims=True)
            r = dy[i:i + 1, :] * kc + rstd2[rows, 0:1] * (c - m1 - xh * m2)
            dx[rows, :] = r
            rb = r.astype(BF)
            db[rows, :] = rb
            bo = bo + jnp.sum(rb.astype(F32), axis=0, keepdims=True)
        small_s[0:4, :] = jnp.zeros((4, D), F32)
        small_s[4:5, :] = bo
        small_s[5:6, :] = g2
        small_s[6:7, :] = b2
        small_s[7:8, :] = bd
        for name in ("qkv", "h1t"):
            loads[name].wait()

    def unit_out(j):
        col = pl.multiple_of(j * TILE, TILE)
        do_s[j] = mm(db[...], wout[pl.ds(col, TILE), :], NT).astype(BF)
        put(n_up, j, mm(ot[...], db[:, pl.ds(col, TILE)]))

    def unit_attend(j, i):
        r0_ = pl.multiple_of(i * ROWS, 16)
        step = j * images + i
        slot = lax.rem(step, 2)

        @pl.when(step + 1 < n_quads * images)
        def _():
            pcopy(step + 1).start()

        pcopy(step).wait()
        q4 = qkv[j, pl.ds(r0_, ROWS), :]
        k4 = qkv[n_quads + j, pl.ds(r0_, WIN), :]
        v4 = qkv[2 * n_quads + j, pl.ds(r0_, WIN), :]
        d4 = do_s[j, pl.ds(r0_, ROWS), :]
        dq = jnp.zeros((ROWS, TILE), F32)
        dk = jnp.zeros((WIN, TILE), F32)
        dv = jnp.zeros((WIN, TILE), F32)
        for h, mask in enumerate(masks):
            pb = p_s[slot, h * ROWS:(h + 1) * ROWS, :]
            dm = d4 * mask
            dv = dv + mm(pb, dm, TN)
            dpr = mm(dm, v4, NT)
            pf = pb.astype(F32)
            ds = (pf * (dpr - jnp.sum(pf * dpr, axis=1, keepdims=True))).astype(BF)
            dq = dq + mm(ds, k4 * mask)
            dk = dk + mm(ds, q4 * mask, TN)
        dq = dq * HEAD_DIM ** -0.5
        dv = dv[0:ROWS]
        sl = pl.ds(pl.multiple_of(j * TILE, TILE), TILE)
        small_s[2:3, sl] += jnp.sum(dq, axis=0, keepdims=True)
        small_s[3:4, sl] += jnp.sum(dv, axis=0, keepdims=True)
        for s, val in enumerate((dq, dk[0:ROWS], dv)):
            col = pl.multiple_of(s * D + j * TILE, TILE)
            dp_s[pl.ds(r0_, ROWS), pl.ds(col, TILE)] = val.astype(BF)

    def unit_weight(j):
        for s in range(3):
            col = pl.multiple_of(s * D + j * TILE, TILE)
            put(n_up + 1 + j, s, mm(h1t[...], dp_s[:, pl.ds(col, TILE)]))

    def unit_norm(i):
        @pl.when(i == 0)
        def _():
            for name in ("wqkv", "xh1", "rstd1"):
                loads[name].wait()

        rows = pl.ds(pl.multiple_of(i * ROWS, 16), ROWS)
        dh = mm(dp_s[rows, :], wqkv[...], NT)
        xh = xh1[rows, :].astype(F32)
        small_s[0:1, :] += jnp.sum(dh * xh, axis=0, keepdims=True)
        small_s[1:2, :] += jnp.sum(dh, axis=0, keepdims=True)
        c = dh * vec_ref[0:1, :]
        m1 = jnp.mean(c, axis=1, keepdims=True)
        m2 = jnp.mean(c * xh, axis=1, keepdims=True)
        r = dx[rows, :] + rstd1[rows, 0:1] * (c - m1 - xh * m2)
        for k in range(images):
            @pl.when(i == k)
            def _(k=k):
                tg_ref[k * SEQ:(k + 1) * SEQ, :] = r[0:SEQ]

    small_s[...] = jnp.zeros_like(small_s)
    loads["h2t"].wait()
    t_down = n_ff
    t_mid = t_down + n_quads
    t_out = t_mid + 1
    t_attend = t_out + n_quads
    t_norm = t_attend + n_quads * (images + 1)

    def unit(n, _):
        @pl.when(n < t_down)
        def _():
            unit_up(n)

        @pl.when((n >= t_down) & (n < t_mid))
        def _():
            unit_down(n - t_down)

        @pl.when(n == t_mid)
        def _():
            unit_mid()

        @pl.when((n >= t_out) & (n < t_attend))
        def _():
            unit_out(n - t_out)

        m = n - t_attend
        inner = lax.rem(m, images + 1)

        @pl.when((m >= 0) & (n < t_norm) & (inner < images))
        def _():
            unit_attend(m // (images + 1), inner)

        @pl.when((m >= 0) & (n < t_norm) & (inner == images))
        def _():
            unit_weight(m // (images + 1))

        @pl.when(n >= t_norm)
        def _():
            unit_norm(n - t_norm)

        tick(n)
        return 0

    lax.fori_loop(0, t_norm + images, unit, 0)

    def spread(src, dst, slot, devs):
        out = []
        for k, dev in enumerate(devs):
            d = pltpu.make_async_remote_copy(
                src[k], dst, vs_sem.at[slot, k], vr_sem.at[slot, k], device_id=dev, device_id_type=MESH)
            d.start()
            out.append(d)
        return out

    def total(ref, count):
        v = ref[0]
        for k in range(1, count):
            v = v + ref[k]
        return v

    part = D // cz
    for zz in range(cz):
        sv[zz, 0:8, 0:part] = small_s[0:8, zz * part:(zz + 1) * part]
        for k in range(D // part):
            sv[zz, 8 + k:9 + k, 0:part] = small_s[8 + zz:9 + zz, k * part:(k + 1) * part]
    vz[z] = sv[z]
    going = spread([sv.at[zz] for zz in z_peers], vz.at[z], 0, z_devs)
    for e, (p, c) in enumerate(TAIL):
        advance(p, c)
        if e == len(TAIL) // 3:
            for d in going:
                d.wait()
            vp[spot] = total(vz, cz)
            going = spread([vp.at[spot]] * len(p_devs), vp.at[spot], 1, p_devs)
        if e == 2 * len(TAIL) // 3:
            for d in going:
                d.wait()
            vc[core] = total(vp, plane)
            going = spread([vc.at[core]], vc.at[core], 2, [core_dev])
    for d in going:
        d.wait()
    small_ref[...] = total(vc, 2)
    for c in range(n_up):
        ug_ref[:, c * D:(c + 1) * D] = res[c]
    og_ref[...] = res[n_up]
    for j in range(n_quads):
        for s in range(3):
            qg_ref[:, s * D + j * TILE:s * D + (j + 1) * TILE] = res[n_up + 1 + j, :, s * TILE:(s + 1) * TILE]


def backward_call(n_row, n_col, images, ff, dy, da, vec, wqkv, wout, wup, acts):
    span = images * ROWS
    nq = D // TILE
    wide = span + WIN - ROWS
    cz = ff // D
    cy = n_col // (2 * cz)
    blk = D // n_col
    n_a = 256 if n_row == 2 else D
    n_h = max((D - n_a) // 2, 128)
    n_ch = ff // D + 1 + nq
    plane = n_row * cy
    n_sem = 2 * cz + 2 * cy + n_row - 2
    anyspec = pl.BlockSpec(memory_space=pl.ANY)
    vm = pl.BlockSpec(memory_space=pltpu.VMEM)
    outs = [(images * SEQ, D), (blk, 3 * D), (blk, D), (blk, ff), (16, 256)]
    B16 = lambda *s: pltpu.VMEM(s, BF)
    B32 = lambda *s: pltpu.VMEM(s, F32)
    scratch = [
        B16(D, 3 * D), B16(D, D), B16(D, ff), B16(D, span), B16(3 * nq, wide, TILE), B16(D, span), B16(D, span),
        B16(span, D), B16(span, D), B32(span, 128), B32(span, 128), B32(span, 128),
        B16(2, 4 * ROWS, TILE), B16(span, ff), B32(span, D), B16(span, D), B16(nq, span, TILE), B16(span, 3 * D),
        B16(4, cz, cy, 2, blk, D), B16(n_ch, cz, cy, blk, D),
        B16(n_ch, cy - 1, cz, blk, n_a), B16(n_ch, cz, cy, blk, n_h),
        B16(n_ch, cz - 1, blk, n_a), B16(n_ch, cy - 1, cz, blk, n_h),
        B16(n_ch, n_row, blk, n_a), B16(n_ch, cz - 1, blk, n_h), B16(n_ch, blk, n_h), B32(n_ch, blk, D),
        B32(2, 16, 256), B32(plane, 16, 256), B32(cz, 16, 256), B32(cz, 16, 256), B32(16, D),
        pltpu.SemaphoreType.DMA((12,)), pltpu.SemaphoreType.DMA((ff // TILE,)), pltpu.SemaphoreType.DMA((2,)),
        pltpu.SemaphoreType.DMA((4, n_sem)), pltpu.SemaphoreType.DMA((n_ch, n_sem)),
        pltpu.SemaphoreType.DMA((3, plane)), pltpu.SemaphoreType.DMA((3, plane)),
    ]
    return pl.pallas_call(
        functools.partial(backward_kernel, n_row, cz, cy, images, ff, n_a),
        out_shape=[jax.ShapeDtypeStruct(s, F32) for s in outs],
        in_specs=[vm] * 3 + [anyspec] * 14,
        out_specs=[vm] * len(outs),
        scratch_shapes=scratch,
        compiler_params=pltpu.CompilerParams(
            vmem_limit_bytes=62 * 2**20, collective_id=1, has_side_effects=True),
        name="block_backward",
    )(dy, da, vec, wqkv, wout, wup, *acts)


def finish_kernel(n_col, cz, images, ff, small_ref, *refs):
    n_big = (len(refs) - 4) // 3
    big, vec_ref, ub_ref, outs = refs[:n_big], refs[n_big], refs[n_big + 1], refs[n_big + 2:2 * n_big + 2]
    held, in_sem, out_sem = refs[2 * n_big + 2:-2], refs[-2], refs[-1]
    moves = []
    for src, mid, dst in zip(big, held, outs):
        rows = src.shape[0]
        step = rows if rows < 400 else 200
        for at in range(0, rows, step):
            sl = pl.ds(at, min(step, rows - at))
            k = len(moves)
            c = pltpu.make_async_copy(src.at[sl], mid.at[sl], in_sem.at[k])
            c.start()
            moves.append((c, pltpu.make_async_copy(mid.at[sl], dst.at[sl], out_sem.at[k])))
    for c, d in moves:
        c.wait()
        d.start()
    member = lax.rem(lax.axis_index("col"), n_col // cz)
    part = D // cz
    values = small_ref[...]
    src = lax.broadcasted_iota(jnp.int32, (256, 256), 0)
    lane = lax.broadcasted_iota(jnp.int32, (256, 256), 1)
    width = D // n_col
    pick = (src == lane + member * width).astype(F32).astype(BF)
    vec_ref[...] = mm3(values[0:8], pick)[:, 0:width]
    n_ub = ff // n_col
    row = lax.broadcasted_iota(jnp.int32, values.shape, 0)
    line = jnp.sum(jnp.where(row == 8 + member * n_ub // part, values, 0.0), axis=0, keepdims=True)
    pick = (src == lane + lax.rem(member * n_ub, part)).astype(F32).astype(BF)
    ub_ref[...] = mm3(jnp.broadcast_to(line, (8, 256)), pick)[0:1, 0:n_ub]
    for c, d in moves:
        d.wait()


def finish_call(n_col, images, ff, small, *big):
    vm = pl.BlockSpec(memory_space=pltpu.VMEM)
    anyspec = pl.BlockSpec(memory_space=pl.ANY)
    shapes = [jax.ShapeDtypeStruct((8, D // n_col), F32), jax.ShapeDtypeStruct((1, ff // n_col), F32)]
    shapes += [jax.ShapeDtypeStruct(b.shape, b.dtype) for b in big]
    return pl.pallas_call(
        functools.partial(finish_kernel, n_col, ff // D, images, ff),
        out_shape=shapes,
        in_specs=[vm] + [anyspec] * len(big),
        out_specs=[vm, vm] + [anyspec] * len(big),
        scratch_shapes=[pltpu.VMEM(b.shape, b.dtype) for b in big] + [pltpu.SemaphoreType.DMA((12,))] * 2,
        compiler_params=pltpu.CompilerParams(vmem_limit_bytes=62 * 2**20),
        name="results",
    )(small, *big)


def per_device(
    tokens,
    keep_mask,
    w_qkv,
    w_out,
    w_up,
    w_down,
    vectors,
    up_bias,
    w_proj,
    texts,
    pair_index,
    logit_scale,
):
    images = keep_mask.shape[0]
    ff = w_up.shape[1]
    n_row, shards = lax.axis_size("row"), lax.axis_size("col")
    acts = forward_call(
        images, ff, tokens, keep_mask, w_qkv, w_out, w_up, w_down, vectors, up_bias.reshape(1, ff)
    )
    loss, dy, da, text_grad, grad_proj, grad_down = head_call(
        n_row, shards, images, ff, acts[12], texts, acts[11], pair_index.reshape(1, -1), logit_scale, w_proj, w_down
    )
    token_grad, qkv_share, out_share, up_share, small = backward_call(
        n_row, shards, images, ff, dy, da, vectors, w_qkv, w_out, w_up, acts[:11]
    )
    vec_share, bias_share, token_grad, qkv_share, out_share, up_share, grad_down, grad_proj, text_grad = finish_call(
        shards, images, ff, small, token_grad, qkv_share, out_share, up_share, grad_down, grad_proj, text_grad
    )
    return (
        loss.reshape(1),
        token_grad,
        qkv_share,
        out_share,
        up_share,
        grad_down,
        vec_share,
        bias_share.reshape(-1),
        grad_proj,
        text_grad,
    )


def solution(mesh):
    in_specs = (
        P(("row", "col"), None),
        P(("row", "col"), None),
        P(),
        P(),
        P(),
        P(),
        P(),
        P(),
        P(),
        P(("row", "col"), None),
        P(),
        P(),
    )
    out_specs = (
        P(),
        P(("row", "col"), None),
        P("col", None),
        P("col", None),
        P("col", None),
        P("col", None),
        P(None, "col"),
        P("col"),
        P("col", None),
        P(("row", "col"), None),
    )
    return jax.shard_map(
        per_device, mesh=mesh, in_specs=in_specs, out_specs=out_specs, check_vma=False
    )
```

```python
import functools

import jax
import jax.numpy as jnp
from jax import lax
from jax.experimental import pallas as pl
from jax.experimental.pallas import tpu as pltpu
from jax.sharding import PartitionSpec as P

D = 768
HEADS = 12
HEAD_DIM = 64
SEQ = 197
EMB = 512
ROWS = 208
WIN = 256
TILE = 256
F32 = jnp.float32
BF = jnp.bfloat16
NT = (((1,), (1,)), ((), ()))
TN = (((0,), (0,)), ((), ()))


def mm(a, b, dims=(((1,), (0,)), ((), ()))):
    return lax.dot_general(a, b, dims, preferred_element_type=F32)


def head_masks():
    lane = lax.broadcasted_iota(jnp.int32, (1, TILE), 1) // HEAD_DIM
    return [(lane == h).astype(F32).astype(BF) for h in range(TILE // HEAD_DIM)]


def gelu_pair(u):
    z = jnp.abs(u)
    t = 1.0 / (1.0 + (0.3275911 * 0.7071067811865476) * z)
    e = jnp.exp(-0.5 * (u * u))
    poly = 0.5 * 1.061405429
    for c in (-1.453152027, 1.421413741, -0.284496736, 0.254829592):
        poly = poly * t + 0.5 * c
    tail = poly * t * e
    cdf = jnp.where(u >= 0.0, 1.0 - tail, tail)
    return u * cdf, cdf + (0.3989422804014327 * u) * e


def forward_kernel(
    images, ff,
    tok_ref, keep_ref, wqkv_h, wout_h, wup_h, wdown_h, vec_ref, upb_ref,
    h1t_h, qkv_h, p_h, ot_h, h2t_h, xh1_h, xh2_h, rstd1_h, rstd2_h, kcol_h, gk_h, apool_ref, pooled_ref,
    wqkv, wout, wup, wdown, xs, h1t, qkv, p_s, ot, h2t, xh1, xh2, rstd1, rstd2, kcol, gk,
    h1, o_s, h2, a_s, a_t, u_a, u_b, keep8, kmask, bias, acc,
    in_sem, out_sem,
):
    n_quads = D // TILE
    n_ff = ff // TILE
    loads = []
    for k, (src, dst) in enumerate(((wqkv_h, wqkv), (wout_h, wout), (wup_h, wup), (wdown_h, wdown))):
        c = pltpu.make_async_copy(src, dst, in_sem.at[k])
        c.start()
        loads.append(c)
    stores = []

    def send(k, src, dst):
        c = pltpu.make_async_copy(src, dst, out_sem.at[k])
        c.start()
        stores.append(c)

    total = images * SEQ
    last = total // 16 * 16
    xs[last:, :] = jnp.zeros_like(xs[last:, :])
    xs[0:last, :] = tok_ref[0:last, :].astype(F32)
    if last < total:
        xs[last:total, :] = tok_ref[last:total, :].astype(F32)
    keep8[...] = jnp.zeros_like(keep8)
    keep8[0:images, 0:SEQ] = keep_ref[...].astype(F32)
    kb = keep8[...]
    rid = lax.broadcasted_iota(jnp.int32, kb.shape, 0)
    for i in range(images):
        kmask[i] = jnp.where(rid == i, kb, 0.0).astype(BF)
        one = jnp.ones((kb.shape[0], 128), F32).astype(BF)
        kcol[i * ROWS:(i + 1) * ROWS, :] = mm(kmask[i], one, TN)[0:ROWS]
    send(0, kcol, kcol_h)
    bias[0:1, 0:D] = vec_ref[2:3, :]
    bias[0:1, D:2 * D] = jnp.zeros((1, D), F32)
    bias[0:1, 2 * D:] = vec_ref[3:4, :]
    for i in range(images):
        x = xs[i * SEQ:i * SEQ + ROWS, :]
        cen = x - jnp.mean(x, axis=1, keepdims=True)
        inv = lax.rsqrt(jnp.mean(cen * cen, axis=1, keepdims=True) + 1e-6)
        xh = cen * inv
        rows = slice(i * ROWS, (i + 1) * ROWS)
        xh1[rows, :] = xh.astype(BF)
        rstd1[rows, :] = jnp.broadcast_to(inv, (ROWS, 128))
        h1[rows, :] = (xh * vec_ref[0:1, :] + vec_ref[1:2, :]).astype(BF)
    send(8, xh1, xh1_h)
    send(9, rstd1, rstd1_h)
    h1t[...] = h1[...].T
    send(10, h1t, h1t_h)
    loads[0].wait()
    span = images * ROWS
    pad = qkv.shape[1] - span
    for t in range(3 * n_quads):
        qkv[t, span:, :] = jnp.zeros((pad, TILE), BF)

    def proj(t, _):
        col = pl.multiple_of(t * TILE, TILE)
        r = mm(h1[...], wqkv[:, pl.ds(col, TILE)]) + bias[0:1, pl.ds(col, TILE)]
        r = r * jnp.where(t < n_quads, HEAD_DIM ** -0.5, 1.0)
        qkv[t, 0:span, :] = r.astype(BF)
        return 0

    lax.fori_loop(0, 3 * n_quads, proj, 0, unroll=3)
    send(1, qkv, qkv_h)
    masks = head_masks()

    def attend(it, _):
        i = it // n_quads
        j = it % n_quads
        r0 = pl.multiple_of(i * ROWS, 16)
        q4 = qkv[j, pl.ds(r0, ROWS), :]
        k4 = qkv[n_quads + j, pl.ds(r0, WIN), :]
        v4 = qkv[2 * n_quads + j, pl.ds(r0, WIN), :]
        valid = keep8[pl.ds(i, 1), :] > 0.0
        out = jnp.zeros((ROWS, TILE), F32)
        for h, m in enumerate(masks):
            s = mm(q4 * m, k4, NT)
            s = jnp.where(valid, s, -1e30)
            e = jnp.exp(s - jnp.max(s, axis=1, keepdims=True))
            pb = (e * (1.0 / jnp.sum(e, axis=1, keepdims=True))).astype(BF)
            p_s[it, h * ROWS:(h + 1) * ROWS, :] = pb
            out = out + mm(pb, v4 * m)
        o_s[j, pl.ds(r0, ROWS), :] = out.astype(BF)
        return 0

    lax.fori_loop(0, images * n_quads, attend, 0, unroll=2)
    send(2, p_s, p_h)
    for j in range(n_quads):
        ot[j * TILE:(j + 1) * TILE, :] = o_s[j].T
    send(3, ot, ot_h)
    loads[1].wait()
    pooled_ref[...] = jnp.zeros_like(pooled_ref)
    for i in range(images):
        rows = slice(i * ROWS, (i + 1) * ROWS)
        x = xs[i * SEQ:i * SEQ + ROWS, :]
        y = x + vec_ref[4:5, :]
        for j in range(n_quads):
            y = y + mm(o_s[j, rows, :], wout[j * TILE:(j + 1) * TILE, :])
        kc = kcol[rows, 0:1]
        pooled_ref[i:i + 1, 0:D] = jnp.sum(y * kc, axis=0, keepdims=True)
        cen = y - jnp.mean(y, axis=1, keepdims=True)
        inv = lax.rsqrt(jnp.mean(cen * cen, axis=1, keepdims=True) + 1e-6)
        xh = cen * inv
        xh2[rows, :] = xh.astype(BF)
        rstd2[rows, :] = jnp.broadcast_to(inv, (ROWS, 128))
        h2[rows, :] = (xh * vec_ref[5:6, :] + vec_ref[6:7, :]).astype(BF)
    h2t[...] = h2[...].T
    send(4, h2t, h2t_h)
    send(5, xh2, xh2_h)
    send(6, rstd2, rstd2_h)
    loads[2].wait()
    loads[3].wait()
    acc[...] = jnp.zeros_like(acc)
    a_s[span:, :] = jnp.zeros((a_s.shape[0] - span, TILE), BF)
    a_t[span:, :] = jnp.zeros((a_s.shape[0] - span, TILE), BF)


    def pool(t, a_s):
        ap = jnp.zeros((kmask.shape[1], TILE), F32)
        for i in range(images):
            ap = ap + mm(kmask[i], a_s[i * ROWS:i * ROWS + WIN, :])
        at = pl.multiple_of((t % n_quads) * TILE, TILE)
        apool_ref[t // n_quads, :, pl.ds(at, TILE)] = ap[0:8]
        hi = ap.astype(BF)
        lo = (ap - hi.astype(F32)).astype(BF)
        both = mm(jnp.concatenate([hi, lo], axis=0), wdown[pl.ds(pl.multiple_of(t * TILE, TILE), TILE), :])
        acc[...] += both[0:16] + both[16:32]

    def lift(t, u_s):
        col = pl.multiple_of(t * TILE, TILE)
        u_s[...] = mm(h2[...], wup[:, pl.ds(col, TILE)]) + upb_ref[0:1, pl.ds(col, TILE)]

    def bend(t, u_s, a_s):
        for i in range(images):
            rows = slice(i * ROWS, (i + 1) * ROWS)
            a, g = gelu_pair(u_s[rows, :])
            a_s[rows, :] = a.astype(BF)
            gk[t, rows, :] = (g * kcol[rows, 0:1]).astype(BF)
        pltpu.make_async_copy(gk.at[t], gk_h.at[t], out_sem.at[7]).start()

    lift(0, u_a)

    def feed(r, _):
        t = 2 * r
        lift(t + 1, u_b)
        bend(t, u_a, a_s)
        pool(t, a_s)
        lift(jnp.minimum(t + 2, n_ff - 1), u_a)
        bend(t + 1, u_b, a_t)
        pool(t + 1, a_t)
        return 0

    lax.fori_loop(0, n_ff // 2, feed, 0)
    cnt = jnp.sum(kb, axis=1, keepdims=True)[0:8]
    inv = 1.0 / jnp.maximum(cnt, 1.0)
    pooled_ref[:, 0:D] = (pooled_ref[:, 0:D] + acc[0:8, :]) * inv + vec_ref[7:8, :]
    pooled_ref[:, D:] = jnp.broadcast_to(cnt, (8, 128))
    for c in stores:
        c.wait()
    for t in range(n_ff):
        pltpu.make_async_copy(gk.at[t], gk_h.at[t], out_sem.at[7]).wait()


def forward_call(images, ff, tokens, keep, wqkv, wout, wup, wdown, vec, upb):
    span = images * ROWS
    nq = D // TILE
    wide = span + WIN - ROWS
    outs = [
        ((D, span), BF), ((3 * nq, wide, TILE), BF), ((images * nq, 4 * ROWS, TILE), BF),
        ((D, span), BF), ((D, span), BF), ((span, D), BF), ((span, D), BF), ((span, 128), F32), ((span, 128), F32),
        ((span, 128), F32), ((ff // TILE, span, TILE), BF), ((ff // D, 8, D), F32), ((8, D + 128), F32),
    ]
    anyspec = pl.BlockSpec(memory_space=pl.ANY)
    vm = pl.BlockSpec(memory_space=pltpu.VMEM)
    scratch = [
        pltpu.VMEM((D, 3 * D), BF), pltpu.VMEM((D, D), BF), pltpu.VMEM((D, ff), BF), pltpu.VMEM((ff, D), BF),
        pltpu.VMEM(((images - 1) * SEQ + ROWS + 7 & -8, D), F32),
    ] + [pltpu.VMEM(*o) for o in outs[:11]] + [
        pltpu.VMEM((span, D), BF), pltpu.VMEM((nq, span, TILE), BF), pltpu.VMEM((span, D), BF),
        pltpu.VMEM((wide, TILE), BF), pltpu.VMEM((wide, TILE), BF), pltpu.VMEM((span, TILE), F32), pltpu.VMEM((span, TILE), F32), pltpu.VMEM((16, WIN), F32), pltpu.VMEM((images, 16, WIN), BF),
        pltpu.VMEM((1, 3 * D), F32), pltpu.VMEM((16, D), F32),
        pltpu.SemaphoreType.DMA((4,)), pltpu.SemaphoreType.DMA((11,)),
    ]
    return pl.pallas_call(
        functools.partial(forward_kernel, images, ff),
        out_shape=[jax.ShapeDtypeStruct(s, d) for s, d in outs],
        in_specs=[vm, vm] + [anyspec] * 4 + [vm, vm],
        out_specs=[anyspec] * 11 + [vm, vm],
        scratch_shapes=scratch,
        compiler_params=pltpu.CompilerParams(vmem_limit_bytes=60 * 2**20),
        name="block_forward",
    )(tokens, keep, wqkv, wout, wup, wdown, vec, upb)


def split3(x):
    hi = x.astype(BF)
    r = x - hi.astype(F32)
    mid = r.astype(BF)
    lo = (r - mid.astype(F32)).astype(BF)
    return hi, mid, lo


NN = (((1,), (0,)), ((), ()))
MESH = pl.DeviceIdType.MESH


def mm3(x, w, dims=NN):
    hi, mid, lo = split3(x)
    return (mm(lo, w, dims) + mm(mid, w, dims)) + mm(hi, w, dims)


def place(cz, cy):
    row = lax.axis_index("row")
    col = lax.axis_index("col")
    return row, col // (2 * cy), lax.rem(col // 2, cy), lax.rem(col, 2)


def head_kernel(
    n_row, cz, cy, images, ff,
    pooled_ref, texts_ref, apool_ref, pair_ref, scale_ref, wproj_ref, wdown_h,
    loss_ref, dy_ref, da_ref, text_ref, proj_ref, down_ref,
    pg, ax, ag, wdown, p_all, t_all, c_all, a_all, gproj, gdown,
    in_sem, zs, zr, ps, pr, cs, cr,
):
    x, z, y, core = place(cz, cy)
    load = pltpu.make_async_copy(wdown_h, wdown, in_sem.at[0])
    load.start()
    half = D // 2
    plane = n_row * cy
    spot = x * cy + y

    def device(xx, zz, yy, cc):
        return (xx, (zz * cy + yy) * 2 + cc)

    z_peers = [lax.rem(z + k, cz) for k in range(1, cz)]
    p_peers = [lax.rem(spot + k, plane) for k in range(1, plane)]
    bar = pltpu.get_barrier_semaphore()
    for zz in z_peers:
        pl.semaphore_signal(bar, inc=1, device_id=device(x, zz, y, core), device_id_type=MESH)
    for pp in p_peers:
        pl.semaphore_signal(bar, inc=1, device_id=device(pp // cy, z, lax.rem(pp, cy), core), device_id_type=MESH)
    pl.semaphore_signal(bar, inc=1, device_id=device(x, z, y, 1 - core), device_id_type=MESH)
    mine = jnp.concatenate([
        pooled_ref[0:images, 0:D],
        jnp.concatenate([texts_ref[...].astype(F32), pooled_ref[0:images, D:], jnp.zeros((images, D - EMB - 128), F32)], axis=1),
    ], axis=0)
    pg[x, z, y, core] = mine
    for g in range(cz):
        ax[g, 0:images] = apool_ref[g, 0:images, 0:half]
        ax[g, images:] = apool_ref[g, 0:images, half:]
    ag[x, z, y, core] = ax[z]
    pl.semaphore_wait(bar, cz - 1 + plane - 1 + 1)

    def stage(src, dst, sems, slot, devs):
        out = []
        for k, (s, dev) in enumerate(zip(src, devs)):
            c = pltpu.make_async_remote_copy(
                s, dst, sems[0].at[slot, k], sems[1].at[slot, k], device_id=dev, device_id_type=MESH)
            c.start()
            out.append(c)
        return out

    z_devs = [device(x, zz, y, core) for zz in z_peers]
    p_devs = [device(pp // cy, z, lax.rem(pp, cy), core) for pp in p_peers]
    c_devs = [device(x, z, y, 1 - core)]
    own = pg.at[x, z, y, core]
    first = stage([own] * len(z_devs), own, (zs, zr), 0, z_devs)
    first_a = stage([ax.at[zz] for zz in z_peers], ag.at[x, z, y, core], (zs, zr), 1, z_devs)
    for c in first:
        c.wait()
    own = pg.at[x, :, y, core]
    second = stage([own] * len(p_devs), own, (ps, pr), 0, p_devs)
    for c in first_a:
        c.wait()
    own = ag.at[x, :, y, core]
    second_a = stage([own] * len(p_devs), own, (ps, pr), 1, p_devs)
    for c in second:
        c.wait()
    own = pg.at[:, :, :, core]
    third = stage([own], own, (cs, cr), 0, c_devs)
    for c in second_a:
        c.wait()
    own = ag.at[:, :, :, core]
    third_a = stage([own], own, (cs, cr), 1, c_devs)
    for c in third:
        c.wait()
    n_col = cz * cy * 2
    n_img = n_row * n_col * images
    for d in range(n_row * n_col):
        rows = slice(d * images, (d + 1) * images)
        at = (d // n_col, d % n_col // (2 * cy), d // 2 % cy, d % 2)
        p_all[rows, :] = pg[at + (slice(0, images), slice(0, D))]
        t_all[rows, :] = pg[at + (slice(images, 2 * images), slice(0, EMB))]
        c_all[rows, :] = pg[at + (slice(images, 2 * images), slice(EMB, EMB + 128))]
    scale = scale_ref[0]
    pooled = p_all[...]
    latent = mm3(pooled, wproj_ref[...])
    norm = lax.rsqrt(jnp.sum(latent * latent, axis=1, keepdims=True) + 1e-6)
    embeds = latent * norm
    eb = embeds.astype(BF)
    tb = t_all[...].astype(BF)
    logits = scale * mm(eb, tb, NT)
    row_max = jnp.max(logits, axis=1, keepdims=True)
    row_exp = jnp.exp(logits - row_max)
    row_sum = jnp.sum(row_exp, axis=1, keepdims=True)
    col_max = jnp.max(logits, axis=0, keepdims=True)
    col_exp = jnp.exp(logits - col_max)
    col_sum = jnp.sum(col_exp, axis=0, keepdims=True)
    ids = lax.broadcasted_iota(jnp.int32, (n_img, n_img), 0)
    match = (ids == pair_ref[...]).astype(F32).T
    grad = 0.5 * (row_exp / row_sum) + 0.5 * (col_exp / col_sum) - match
    lse = jnp.sum(row_max + jnp.log(row_sum), axis=0, keepdims=True) + jnp.sum(
        col_max + jnp.log(col_sum), axis=1, keepdims=True)
    hits = jnp.sum(jnp.sum(logits * match, axis=1, keepdims=True), axis=0, keepdims=True)
    loss_ref[...] = (0.5 * lse - hits) * (1.0 / n_img)
    de = scale * mm3(grad, tb)
    dz = norm * (de - embeds * jnp.sum(embeds * de, axis=1, keepdims=True))
    image_grad = mm3(dz, wproj_ref[...], NT) / c_all[:, 0:1]
    dev = x * n_col + (z * cy + y) * 2 + core
    want = lax.broadcasted_iota(jnp.int32, (16, n_img), 0) + dev * images
    have = lax.broadcasted_iota(jnp.int32, (16, n_img), 1)
    pick = (want == have).astype(F32).astype(BF)
    hi, mid, lo = split3(image_grad)
    dy = (mm(pick, lo) + mm(pick, mid)) + mm(pick, hi)
    dy_ref[...] = dy[0:8]
    dyb = dy.astype(BF)
    load.wait()

    def spread(t, _):
        col = pl.multiple_of(t * TILE, TILE)
        da_ref[:, pl.ds(col, TILE)] = mm(dyb, wdown[pl.ds(col, TILE), :], NT)[0:8]
        return 0

    lax.fori_loop(0, ff // TILE, spread, 0)
    g_hi, g_mid, g_lo = split3(grad)
    own_grad = (mm(pick, g_lo, NT) + mm(pick, g_mid, NT)) + mm(pick, g_hi, NT)
    text_ref[...] = (scale * mm3(own_grad, eb))[0:images]
    p_hi, p_lo, _ = split3(pooled)
    d_hi, d_lo, _ = split3(dz)
    gproj[...] = (mm(p_lo, d_hi, TN) + mm(p_hi, d_lo, TN)) + mm(p_hi, d_hi, TN)
    n_proj = D // n_col
    at = pl.multiple_of(((z * cy + y) * 2 + core) * n_proj, 8)
    proj_ref[...] = gproj[pl.ds(at, n_proj), :]
    for c in third_a:
        c.wait()
    for d in range(n_row * n_col):
        rows = slice(d * images, (d + 1) * images)
        at = (d // n_col, d % n_col // (2 * cy), d // 2 % cy, d % 2)
        a_all[rows, 0:half] = ag[at + (slice(0, images),)]
        a_all[rows, half:] = ag[at + (slice(images, 2 * images),)]
    acts = a_all[...]
    a_hi = acts.astype(BF)
    a_lo = (acts - a_hi.astype(F32)).astype(BF)
    for n in range(D // TILE):
        sl = slice(n * TILE, (n + 1) * TILE)
        gdown[:, sl] = mm(a_lo, hi[:, sl], TN) + mm(a_hi, hi[:, sl], TN)
    n_down = ff // n_col
    at = pl.multiple_of((y * 2 + core) * n_down, 8)
    down_ref[...] = gdown[pl.ds(at, n_down), :]


def head_call(n_row, n_col, images, ff, pooled, texts, apool, pair, scale, wproj, wdown):
    cz = ff // D
    cy = n_col // (2 * cz)
    n_img = n_row * n_col * images
    vm = pl.BlockSpec(memory_space=pltpu.VMEM)
    outs = [(1, 1), (8, D), (8, ff), (images, EMB), (D // n_col, EMB), (ff // n_col, D)]
    plane = n_row * cy
    grid = (n_row, cz, cy, 2, 2 * images)
    scratch = [
        pltpu.VMEM(grid + (D,), F32), pltpu.VMEM((cz, 2 * images, D // 2), F32), pltpu.VMEM(grid + (D // 2,), F32),
        pltpu.VMEM((ff, D), BF), pltpu.VMEM((n_img, D), F32), pltpu.VMEM((n_img, EMB), F32),
        pltpu.VMEM((n_img, 128), F32), pltpu.VMEM((n_img, D), F32), pltpu.VMEM((D, EMB), F32), pltpu.VMEM((D, D), F32),
        pltpu.SemaphoreType.DMA((1,)), pltpu.SemaphoreType.DMA((2, cz)), pltpu.SemaphoreType.DMA((2, cz)),
        pltpu.SemaphoreType.DMA((2, plane)), pltpu.SemaphoreType.DMA((2, plane)),
        pltpu.SemaphoreType.DMA((2, 1)), pltpu.SemaphoreType.DMA((2, 1)),
    ]
    return pl.pallas_call(
        functools.partial(head_kernel, n_row, cz, cy, images, ff),
        out_shape=[jax.ShapeDtypeStruct(s, F32) for s in outs],
        in_specs=[vm] * 4 + [pl.BlockSpec(memory_space=pltpu.SMEM), vm, pl.BlockSpec(memory_space=pl.ANY)],
        out_specs=[vm] * len(outs),
        scratch_shapes=scratch,
        compiler_params=pltpu.CompilerParams(
            vmem_limit_bytes=60 * 2**20, collective_id=0, has_side_effects=True),
        name="contrastive_head",
    )(pooled, texts, apool, pair, scale, wproj, wdown)


READY = [2, 5, 8, 11, 18, 23, 28, 33]
WAITS = [[(6, 0), (9, 1), (12, 2), (13, 3), (20, 4), (25, 5), (30, 6), (35, 7)], [(13, 0), (15, 1), (20, 2), (23, 3), (27, 4), (32, 5), (36, 6)], [(16, 0), (20, 1), (25, 2), (27, 3), (32, 4), (36, 5)], [(24, 0), (25, 1), (29, 2), (33, 3), (36, 4)], [(28, 0), (29, 1), (33, 2), (37, 3)]]
TAIL = [(1, 7), (4, 4), (3, 5), (2, 6), (4, 5), (2, 7), (3, 6), (4, 6), (3, 7), (4, 7)]


def backward_kernel(
    n_row, cz, cy, images, ff, n_a,
    dy_ref, da_ref, vec_ref,
    wqkv_h, wout_h, wup_h, h1t_h, qkv_h, p_h, ot_h, h2t_h, xh1_h, xh2_h, rstd1_h, rstd2_h, kcol_h, gk_h,
    tg_ref, qg_ref, og_ref, ug_ref, small_ref,
    wqkv, wout, wup, h1t, qkv, ot, h2t, xh1, xh2, rstd1, rstd2, kcol, p_s, du, dx, db, do_s, dp_s,
    g, r0, r1a, r1b, r2a, r2b, r3a, r3b, r4b, res, vc, vp, vz, sv, small_s,
    in_sem, gk_sem, p_sem, s_sem, r_sem, vs_sem, vr_sem,
):
    n_quads = D // TILE
    n_ff = ff // TILE
    n_up = ff // D
    n_chunks = n_up + 1 + n_quads
    masks = head_masks()
    x, z, y, core = place(cz, cy)
    two = n_a < D
    n_h = (D - n_a) // 2
    plane = n_row * cy
    spot = x * cy + y

    def device(xx, zz, yy, cc):
        return (xx, (zz * cy + yy) * 2 + cc)

    core_dev = device(x, z, y, 1 - core)
    y_peers = [lax.rem(y + k, cy) for k in range(1, cy)]
    z_peers = [lax.rem(z + k, cz) for k in range(1, cz)]
    x_peers = [lax.rem(x + k, n_row) for k in range(1, n_row)]
    p_peers = [lax.rem(spot + k, plane) for k in range(1, plane)]
    z_devs = [device(x, zz, y, core) for zz in z_peers]
    y_devs = [device(x, z, yy, core) for yy in y_peers]
    x_devs = [device(xx, z, y, core) for xx in x_peers]
    p_devs = [device(pp // cy, z, lax.rem(pp, cy), core) for pp in p_peers]

    loads = {}
    for k, (name, src, dst) in enumerate((
        ("kcol", kcol_h, kcol), ("h2t", h2t_h, h2t), ("wup", wup_h, wup), ("xh2", xh2_h, xh2),
        ("rstd2", rstd2_h, rstd2), ("wout", wout_h, wout), ("ot", ot_h, ot), ("qkv", qkv_h, qkv),
        ("h1t", h1t_h, h1t), ("wqkv", wqkv_h, wqkv), ("xh1", xh1_h, xh1), ("rstd1", rstd1_h, rstd1),
    )):
        loads[name] = pltpu.make_async_copy(src, dst, in_sem.at[k])

    def gcopy(t):
        col = pl.multiple_of(t * TILE, TILE)
        return pltpu.make_async_copy(gk_h.at[t], du.at[:, pl.ds(col, TILE)], gk_sem.at[t])

    loads["h2t"].start()
    for t in range(n_ff):
        gcopy(t).start()
    for name in ("kcol", "wup", "xh2", "rstd2", "wout", "ot", "qkv", "h1t", "wqkv", "xh1", "rstd1"):
        loads[name].start()

    def pcopy(step):
        i = lax.rem(step, images)
        j = step // images
        slot = lax.rem(step, 2)
        return pltpu.make_async_copy(p_h.at[i * n_quads + j], p_s.at[slot], p_sem.at[slot])

    pcopy(0).start()
    bar = pltpu.get_barrier_semaphore()
    for dev in z_devs + p_devs + [core_dev]:
        pl.semaphore_signal(bar, inc=1, device_id=dev, device_id_type=MESH)
    half = lambda which: pl.ds(pl.multiple_of(n_a + which * n_h, 128), n_h)

    def copies(p, c):
        if p == 0:
            out = [(g.at[lax.rem(c, 4), :, :, 1 - core], r0.at[c], core_dev)]
        elif p == 1:
            out = [(r0.at[c, :, yy, :, 0:n_a], r1a.at[c, k], dev) for k, (yy, dev) in enumerate(zip(y_peers, y_devs))]
            if two:
                out += [(r0.at[c, :, :, :, half(1 - x)], r1b.at[c], x_devs[0])]
        elif p == 2:
            out = [(r1a.at[c, 0, zz], r2a.at[c, k], dev) for k, (zz, dev) in enumerate(zip(z_peers, z_devs))]
            if two:
                out += [(r1b.at[c, :, yy], r2b.at[c, k], dev) for k, (yy, dev) in enumerate(zip(y_peers, y_devs))]
        elif p == 3:
            out = [(r3a.at[c, x], r3a.at[c, x], dev) for dev in x_devs]
            if two:
                out += [(r2b.at[c, 0, zz], r3b.at[c, k], dev) for k, (zz, dev) in enumerate(zip(z_peers, z_devs))]
        else:
            out = [(r3b.at[c, 0], r4b.at[c], x_devs[0])] if two else []
        base = (0, 1, 1 + cy, cz + 2 * cy - 1, 2 * cz + 2 * cy + n_row - 3)[p]
        return [
            pltpu.make_async_remote_copy(
                src, dst, s_sem.at[lax.rem(c, 4), base + k], r_sem.at[c, base + k], device_id=dev, device_id_type=MESH)
            for k, (src, dst, dev) in enumerate(out)
        ]

    def finish(p, c):
        up = lambda v: v.astype(F32)
        if p == 0:
            r0[c] = r0[c] + g[lax.rem(c, 4), :, :, core]
        elif p == 1:
            v = up(r0[c, :, y, :, 0:n_a])
            for k in range(cy - 1):
                v = v + up(r1a[c, k])
            r1a[c, 0] = v.astype(BF)
            if two:
                r1b[c] = r1b[c] + r0[c, :, :, :, half(x)]
        elif p == 2:
            v = up(r1a[c, 0, z])
            for k in range(cz - 1):
                v = v + up(r2a[c, k])
            r3a[c, x] = v.astype(BF)
            if two:
                v = up(r1b[c, :, y])
                for k in range(cy - 1):
                    v = v + up(r2b[c, k])
                r2b[c, 0] = v.astype(BF)
        elif p == 3:
            v = up(r3a[c, 0])
            for k in range(1, n_row):
                v = v + up(r3a[c, k])
            res[c, :, 0:n_a] = v
            if two:
                v = up(r2b[c, 0, z])
                for k in range(cz - 1):
                    v = v + up(r3b[c, k])
                v = v.astype(BF)
                r3b[c, 0] = v
                res[c, :, half(x)] = up(v)
        elif two:
            res[c, :, half(1 - x)] = up(r4b[c])

    def begin(p, c):
        for d in copies(p, c):
            d.start()

    def advance(p, c):
        for d in copies(p, c):
            d.wait()
        finish(p, c)
        if p < 4:
            begin(p + 1, c)

    def lookup(n, events):
        hit = n < 0
        c = jnp.int32(0)
        for at, chunk in events:
            same = n == at
            hit = hit | same
            c = jnp.where(same, chunk, c)
        return hit, c

    def tick(n):
        @pl.when(n == READY[0])
        def _():
            pl.semaphore_wait(bar, len(z_devs) + len(p_devs) + 1)

        hit, c = lookup(n, [(at, k) for k, at in enumerate(READY)])

        @pl.when(hit)
        def _():
            begin(0, c)

        for p in range(4, -1, -1):
            hit, c = lookup(n, WAITS[p])

            @pl.when(hit)
            def _(p=p, c=c):
                advance(p, c)

    def put(c, tt, part):
        col = pl.multiple_of(tt * TILE, TILE)
        g[lax.rem(c, 4), :, :, :, :, pl.ds(col, TILE)] = part.reshape(g.shape[1:5] + (TILE,)).astype(BF)

    def unit_up(t):
        n = t // n_quads
        tt = lax.rem(t, n_quads)
        col = pl.multiple_of(t * TILE, TILE)
        gcopy(t).wait()
        ub = jnp.zeros((1, TILE), F32)
        for i in range(images):
            rows = slice(i * ROWS, (i + 1) * ROWS)
            d = du[rows, pl.ds(col, TILE)].astype(F32) * da_ref[i:i + 1, pl.ds(col, TILE)]
            ub = ub + jnp.sum(d, axis=0, keepdims=True)
            du[rows, pl.ds(col, TILE)] = d.astype(BF)
        scol = pl.multiple_of(tt * TILE, TILE)
        small_s[pl.ds(8 + n, 1), pl.ds(scol, TILE)] = ub
        put(n, tt, mm(h2t[...], du[:, pl.ds(col, TILE)]))

    def unit_down(n):
        @pl.when(n == 0)
        def _():
            loads["wup"].wait()

        col = pl.multiple_of(n * TILE, TILE)
        dx[:, pl.ds(col, TILE)] = mm(du[...], wup[pl.ds(col, TILE), :], NT)

    def unit_mid():
        for name in ("kcol", "xh2", "rstd2", "wout", "ot"):
            loads[name].wait()
        dy = dy_ref[...]
        dyb = dy.astype(BF).astype(F32)
        g2 = jnp.zeros((1, D), F32)
        b2 = jnp.zeros((1, D), F32)
        bo = jnp.zeros((1, D), F32)
        bd = jnp.zeros((1, D), F32)
        for i in range(images):
            rows = slice(i * ROWS, (i + 1) * ROWS)
            kc = kcol[rows, 0:1]
            bd = bd + jnp.sum(kc, axis=0, keepdims=True) * dyb[i:i + 1, :]
            dh = dx[rows, :]
            xh = xh2[rows, :].astype(F32)
            g2 = g2 + jnp.sum(dh * xh, axis=0, keepdims=True)
            b2 = b2 + jnp.sum(dh, axis=0, keepdims=True)
            c = dh * vec_ref[5:6, :]
            m1 = jnp.mean(c, axis=1, keepdims=True)
            m2 = jnp.mean(c * xh, axis=1, keepdims=True)
            r = dy[i:i + 1, :] * kc + rstd2[rows, 0:1] * (c - m1 - xh * m2)
            dx[rows, :] = r
            rb = r.astype(BF)
            db[rows, :] = rb
            bo = bo + jnp.sum(rb.astype(F32), axis=0, keepdims=True)
        small_s[0:4, :] = jnp.zeros((4, D), F32)
        small_s[4:5, :] = bo
        small_s[5:6, :] = g2
        small_s[6:7, :] = b2
        small_s[7:8, :] = bd
        for name in ("qkv", "h1t"):
            loads[name].wait()

    def unit_out(j):
        col = pl.multiple_of(j * TILE, TILE)
        do_s[j] = mm(db[...], wout[pl.ds(col, TILE), :], NT).astype(BF)
        put(n_up, j, mm(ot[...], db[:, pl.ds(col, TILE)]))

    def unit_attend(j, i):
        r0_ = pl.multiple_of(i * ROWS, 16)
        step = j * images + i
        slot = lax.rem(step, 2)

        @pl.when(step + 1 < n_quads * images)
        def _():
            pcopy(step + 1).start()

        pcopy(step).wait()
        q4 = qkv[j, pl.ds(r0_, ROWS), :]
        k4 = qkv[n_quads + j, pl.ds(r0_, WIN), :]
        v4 = qkv[2 * n_quads + j, pl.ds(r0_, WIN), :]
        d4 = do_s[j, pl.ds(r0_, ROWS), :]
        dp = mm(jnp.concatenate([d4 * mask for mask in masks], axis=0), v4, NT)
        pb = p_s[slot]
        pf = pb.astype(F32)
        ds = (pf * (dp - jnp.sum(pf * dp, axis=1, keepdims=True))).astype(BF)
        dq = jnp.zeros((ROWS, TILE), F32)
        dt = d4.T
        qt = q4.T
        dv = []
        dk = []
        for h, mask in enumerate(masks):
            rows = slice(h * ROWS, (h + 1) * ROWS)
            cut = slice(h * HEAD_DIM, (h + 1) * HEAD_DIM)
            dq = dq + mm(ds[rows], k4 * mask)
            dv.append(mm(dt[cut], pb[rows]))
            dk.append(mm(qt[cut], ds[rows]))
        dv = jnp.concatenate(dv, axis=0).T
        dk = jnp.concatenate(dk, axis=0).T
        dq = dq * HEAD_DIM ** -0.5
        dv = dv[0:ROWS]
        sl = pl.ds(pl.multiple_of(j * TILE, TILE), TILE)
        small_s[2:3, sl] += jnp.sum(dq, axis=0, keepdims=True)
        small_s[3:4, sl] += jnp.sum(dv, axis=0, keepdims=True)
        for s, val in enumerate((dq, dk[0:ROWS], dv)):
            col = pl.multiple_of(s * D + j * TILE, TILE)
            dp_s[pl.ds(r0_, ROWS), pl.ds(col, TILE)] = val.astype(BF)

    def unit_weight(j):
        for s in range(3):
            col = pl.multiple_of(s * D + j * TILE, TILE)
            put(n_up + 1 + j, s, mm(h1t[...], dp_s[:, pl.ds(col, TILE)]))

    def unit_norm(i):
        @pl.when(i == 0)
        def _():
            for name in ("wqkv", "xh1", "rstd1"):
                loads[name].wait()

        rows = pl.ds(pl.multiple_of(i * ROWS, 16), ROWS)
        dh = mm(dp_s[rows, :], wqkv[...], NT)
        xh = xh1[rows, :].astype(F32)
        small_s[0:1, :] += jnp.sum(dh * xh, axis=0, keepdims=True)
        small_s[1:2, :] += jnp.sum(dh, axis=0, keepdims=True)
        c = dh * vec_ref[0:1, :]
        m1 = jnp.mean(c, axis=1, keepdims=True)
        m2 = jnp.mean(c * xh, axis=1, keepdims=True)
        r = dx[rows, :] + rstd1[rows, 0:1] * (c - m1 - xh * m2)
        for k in range(images):
            @pl.when(i == k)
            def _(k=k):
                tg_ref[k * SEQ:(k + 1) * SEQ, :] = r[0:SEQ]

    small_s[...] = jnp.zeros_like(small_s)
    loads["h2t"].wait()
    t_down = n_ff
    t_mid = t_down + n_quads
    t_out = t_mid + 1
    t_attend = t_out + n_quads
    t_norm = t_attend + n_quads * (images + 1)

    def unit(n, _):
        @pl.when(n < t_down)
        def _():
            unit_up(n)

        @pl.when((n >= t_down) & (n < t_mid))
        def _():
            unit_down(n - t_down)

        @pl.when(n == t_mid)
        def _():
            unit_mid()

        @pl.when((n >= t_out) & (n < t_attend))
        def _():
            unit_out(n - t_out)

        m = n - t_attend
        inner = lax.rem(m, images + 1)

        @pl.when((m >= 0) & (n < t_norm) & (inner < images))
        def _():
            unit_attend(m // (images + 1), inner)

        @pl.when((m >= 0) & (n < t_norm) & (inner == images))
        def _():
            unit_weight(m // (images + 1))

        @pl.when(n >= t_norm)
        def _():
            unit_norm(n - t_norm)

        tick(n)
        return 0

    lax.fori_loop(0, t_norm + images, unit, 0)

    def spread(src, dst, slot, devs):
        out = []
        for k, dev in enumerate(devs):
            d = pltpu.make_async_remote_copy(
                src[k], dst, vs_sem.at[slot, k], vr_sem.at[slot, k], device_id=dev, device_id_type=MESH)
            d.start()
            out.append(d)
        return out

    def total(ref, count):
        v = ref[0]
        for k in range(1, count):
            v = v + ref[k]
        return v

    part = D // cz
    for zz in range(cz):
        sv[zz, 0:8, 0:part] = small_s[0:8, zz * part:(zz + 1) * part]
        for k in range(D // part):
            sv[zz, 8 + k:9 + k, 0:part] = small_s[8 + zz:9 + zz, k * part:(k + 1) * part]
    vz[z] = sv[z]
    going = spread([sv.at[zz] for zz in z_peers], vz.at[z], 0, z_devs)
    for e, (p, c) in enumerate(TAIL):
        advance(p, c)
        if e == len(TAIL) // 3:
            for d in going:
                d.wait()
            vp[spot] = total(vz, cz)
            going = spread([vp.at[spot]] * len(p_devs), vp.at[spot], 1, p_devs)
        if e == 2 * len(TAIL) // 3:
            for d in going:
                d.wait()
            vc[core] = total(vp, plane)
            going = spread([vc.at[core]], vc.at[core], 2, [core_dev])
    for d in going:
        d.wait()
    small_ref[...] = total(vc, 2)
    for c in range(n_up):
        ug_ref[:, c * D:(c + 1) * D] = res[c]
    og_ref[...] = res[n_up]
    for j in range(n_quads):
        for s in range(3):
            qg_ref[:, s * D + j * TILE:s * D + (j + 1) * TILE] = res[n_up + 1 + j, :, s * TILE:(s + 1) * TILE]


def backward_call(n_row, n_col, images, ff, dy, da, vec, wqkv, wout, wup, acts):
    span = images * ROWS
    nq = D // TILE
    wide = span + WIN - ROWS
    cz = ff // D
    cy = n_col // (2 * cz)
    blk = D // n_col
    n_a = 256 if n_row == 2 else D
    n_h = max((D - n_a) // 2, 128)
    n_ch = ff // D + 1 + nq
    plane = n_row * cy
    n_sem = 2 * cz + 2 * cy + n_row - 2
    anyspec = pl.BlockSpec(memory_space=pl.ANY)
    vm = pl.BlockSpec(memory_space=pltpu.VMEM)
    outs = [(images * SEQ, D), (blk, 3 * D), (blk, D), (blk, ff), (16, 256)]
    B16 = lambda *s: pltpu.VMEM(s, BF)
    B32 = lambda *s: pltpu.VMEM(s, F32)
    scratch = [
        B16(D, 3 * D), B16(D, D), B16(D, ff), B16(D, span), B16(3 * nq, wide, TILE), B16(D, span), B16(D, span),
        B16(span, D), B16(span, D), B32(span, 128), B32(span, 128), B32(span, 128),
        B16(2, 4 * ROWS, TILE), B16(span, ff), B32(span, D), B16(span, D), B16(nq, span, TILE), B16(span, 3 * D),
        B16(4, cz, cy, 2, blk, D), B16(n_ch, cz, cy, blk, D),
        B16(n_ch, cy - 1, cz, blk, n_a), B16(n_ch, cz, cy, blk, n_h),
        B16(n_ch, cz - 1, blk, n_a), B16(n_ch, cy - 1, cz, blk, n_h),
        B16(n_ch, n_row, blk, n_a), B16(n_ch, cz - 1, blk, n_h), B16(n_ch, blk, n_h), B32(n_ch, blk, D),
        B32(2, 16, 256), B32(plane, 16, 256), B32(cz, 16, 256), B32(cz, 16, 256), B32(16, D),
        pltpu.SemaphoreType.DMA((12,)), pltpu.SemaphoreType.DMA((ff // TILE,)), pltpu.SemaphoreType.DMA((2,)),
        pltpu.SemaphoreType.DMA((4, n_sem)), pltpu.SemaphoreType.DMA((n_ch, n_sem)),
        pltpu.SemaphoreType.DMA((3, plane)), pltpu.SemaphoreType.DMA((3, plane)),
    ]
    return pl.pallas_call(
        functools.partial(backward_kernel, n_row, cz, cy, images, ff, n_a),
        out_shape=[jax.ShapeDtypeStruct(s, F32) for s in outs],
        in_specs=[vm] * 3 + [anyspec] * 14,
        out_specs=[vm] * len(outs),
        scratch_shapes=scratch,
        compiler_params=pltpu.CompilerParams(
            vmem_limit_bytes=62 * 2**20, collective_id=1, has_side_effects=True),
        name="block_backward",
    )(dy, da, vec, wqkv, wout, wup, *acts)


def finish_kernel(n_col, cz, images, ff, small_ref, *refs):
    n_big = (len(refs) - 4) // 3
    big, vec_ref, ub_ref, outs = refs[:n_big], refs[n_big], refs[n_big + 1], refs[n_big + 2:2 * n_big + 2]
    held, in_sem, out_sem = refs[2 * n_big + 2:-2], refs[-2], refs[-1]
    moves = []
    for src, mid, dst in zip(big, held, outs):
        rows = src.shape[0]
        step = rows if rows < 400 else 200
        for at in range(0, rows, step):
            sl = pl.ds(at, min(step, rows - at))
            k = len(moves)
            c = pltpu.make_async_copy(src.at[sl], mid.at[sl], in_sem.at[k])
            c.start()
            moves.append((c, pltpu.make_async_copy(mid.at[sl], dst.at[sl], out_sem.at[k])))
    for c, d in moves:
        c.wait()
        d.start()
    member = lax.rem(lax.axis_index("col"), n_col // cz)
    part = D // cz
    values = small_ref[...]
    src = lax.broadcasted_iota(jnp.int32, (256, 256), 0)
    lane = lax.broadcasted_iota(jnp.int32, (256, 256), 1)
    width = D // n_col
    pick = (src == lane + member * width).astype(F32).astype(BF)
    vec_ref[...] = mm3(values[0:8], pick)[:, 0:width]
    n_ub = ff // n_col
    row = lax.broadcasted_iota(jnp.int32, values.shape, 0)
    line = jnp.sum(jnp.where(row == 8 + member * n_ub // part, values, 0.0), axis=0, keepdims=True)
    pick = (src == lane + lax.rem(member * n_ub, part)).astype(F32).astype(BF)
    ub_ref[...] = mm3(jnp.broadcast_to(line, (8, 256)), pick)[0:1, 0:n_ub]
    for c, d in moves:
        d.wait()


def finish_call(n_col, images, ff, small, *big):
    vm = pl.BlockSpec(memory_space=pltpu.VMEM)
    anyspec = pl.BlockSpec(memory_space=pl.ANY)
    shapes = [jax.ShapeDtypeStruct((8, D // n_col), F32), jax.ShapeDtypeStruct((1, ff // n_col), F32)]
    shapes += [jax.ShapeDtypeStruct(b.shape, b.dtype) for b in big]
    return pl.pallas_call(
        functools.partial(finish_kernel, n_col, ff // D, images, ff),
        out_shape=shapes,
        in_specs=[vm] + [anyspec] * len(big),
        out_specs=[vm, vm] + [anyspec] * len(big),
        scratch_shapes=[pltpu.VMEM(b.shape, b.dtype) for b in big] + [pltpu.SemaphoreType.DMA((12,))] * 2,
        compiler_params=pltpu.CompilerParams(vmem_limit_bytes=62 * 2**20),
        name="results",
    )(small, *big)


def per_device(
    tokens,
    keep_mask,
    w_qkv,
    w_out,
    w_up,
    w_down,
    vectors,
    up_bias,
    w_proj,
    texts,
    pair_index,
    logit_scale,
):
    images = keep_mask.shape[0]
    ff = w_up.shape[1]
    n_row, shards = lax.axis_size("row"), lax.axis_size("col")
    acts = forward_call(
        images, ff, tokens, keep_mask, w_qkv, w_out, w_up, w_down, vectors, up_bias.reshape(1, ff)
    )
    loss, dy, da, text_grad, grad_proj, grad_down = head_call(
        n_row, shards, images, ff, acts[12], texts, acts[11], pair_index.reshape(1, -1), logit_scale, w_proj, w_down
    )
    token_grad, qkv_share, out_share, up_share, small = backward_call(
        n_row, shards, images, ff, dy, da, vectors, w_qkv, w_out, w_up, acts[:11]
    )
    vec_share, bias_share, token_grad, qkv_share, out_share, up_share, grad_down, grad_proj, text_grad = finish_call(
        shards, images, ff, small, token_grad, qkv_share, out_share, up_share, grad_down, grad_proj, text_grad
    )
    return (
        loss.reshape(1),
        token_grad,
        qkv_share,
        out_share,
        up_share,
        grad_down,
        vec_share,
        bias_share.reshape(-1),
        grad_proj,
        text_grad,
    )


def solution(mesh):
    in_specs = (
        P(("row", "col"), None),
        P(("row", "col"), None),
        P(),
        P(),
        P(),
        P(),
        P(),
        P(),
        P(),
        P(("row", "col"), None),
        P(),
        P(),
    )
    out_specs = (
        P(),
        P(("row", "col"), None),
        P("col", None),
        P("col", None),
        P("col", None),
        P("col", None),
        P(None, "col"),
        P("col"),
        P("col", None),
        P(("row", "col"), None),
    )
    return jax.shard_map(
        per_device, mesh=mesh, in_specs=in_specs, out_specs=out_specs, check_vma=False
    )
```

```python
import functools

import jax
import jax.numpy as jnp
from jax import lax
from jax.experimental import pallas as pl
from jax.experimental.pallas import tpu as pltpu
from jax.sharding import PartitionSpec as P

D = 768
HEADS = 12
HEAD_DIM = 64
SEQ = 197
EMB = 512
ROWS = 208
WIN = 256
TILE = 256
F32 = jnp.float32
BF = jnp.bfloat16
NT = (((1,), (1,)), ((), ()))
TN = (((0,), (0,)), ((), ()))


def mm(a, b, dims=(((1,), (0,)), ((), ()))):
    return lax.dot_general(a, b, dims, preferred_element_type=F32)


def head_masks():
    lane = lax.broadcasted_iota(jnp.int32, (1, TILE), 1) // HEAD_DIM
    return [(lane == h).astype(F32).astype(BF) for h in range(TILE // HEAD_DIM)]


def gelu_pair(u):
    z = jnp.abs(u)
    t = 1.0 / (1.0 + (0.3275911 * 0.7071067811865476) * z)
    e = jnp.exp(-0.5 * (u * u))
    poly = 0.5 * 1.061405429
    for c in (-1.453152027, 1.421413741, -0.284496736, 0.254829592):
        poly = poly * t + 0.5 * c
    tail = poly * t * e
    cdf = jnp.where(u >= 0.0, 1.0 - tail, tail)
    return u * cdf, cdf + (0.3989422804014327 * u) * e


def forward_kernel(
    images, ff,
    tok_ref, keep_ref, wqkv_h, wout_h, wup_h, wdown_h, vec_ref, upb_ref,
    h1t_h, qkv_h, p_h, ot_h, h2t_h, xh1_h, xh2_h, rstd1_h, rstd2_h, kcol_h, gk_h, apool_ref, pooled_ref,
    wqkv, wout, wup, wdown, xs, h1t, qkv, p_s, ot, h2t, xh1, xh2, rstd1, rstd2, kcol, gk,
    h1, o_s, h2, a_s, a_t, u_a, u_b, keep8, kmask, bias, acc,
    in_sem, out_sem,
):
    n_quads = D // TILE
    n_ff = ff // TILE
    loads = []
    for k, (src, dst) in enumerate(((wqkv_h, wqkv), (wout_h, wout), (wup_h, wup), (wdown_h, wdown))):
        c = pltpu.make_async_copy(src, dst, in_sem.at[k])
        c.start()
        loads.append(c)
    stores = []

    def send(k, src, dst):
        c = pltpu.make_async_copy(src, dst, out_sem.at[k])
        c.start()
        stores.append(c)

    total = images * SEQ
    last = total // 16 * 16
    xs[last:, :] = jnp.zeros_like(xs[last:, :])
    xs[0:last, :] = tok_ref[0:last, :].astype(F32)
    if last < total:
        xs[last:total, :] = tok_ref[last:total, :].astype(F32)
    keep8[...] = jnp.zeros_like(keep8)
    keep8[0:images, 0:SEQ] = keep_ref[...].astype(F32)
    kb = keep8[...]
    rid = lax.broadcasted_iota(jnp.int32, kb.shape, 0)
    for i in range(images):
        kmask[i] = jnp.where(rid == i, kb, 0.0).astype(BF)
        one = jnp.ones((kb.shape[0], 128), F32).astype(BF)
        kcol[i * ROWS:(i + 1) * ROWS, :] = mm(kmask[i], one, TN)[0:ROWS]
    send(0, kcol, kcol_h)
    bias[0:1, 0:D] = vec_ref[2:3, :]
    bias[0:1, D:2 * D] = jnp.zeros((1, D), F32)
    bias[0:1, 2 * D:] = vec_ref[3:4, :]
    for i in range(images):
        x = xs[i * SEQ:i * SEQ + ROWS, :]
        cen = x - jnp.mean(x, axis=1, keepdims=True)
        inv = lax.rsqrt(jnp.mean(cen * cen, axis=1, keepdims=True) + 1e-6)
        xh = cen * inv
        rows = slice(i * ROWS, (i + 1) * ROWS)
        xh1[rows, :] = xh.astype(BF)
        rstd1[rows, :] = jnp.broadcast_to(inv, (ROWS, 128))
        h1[rows, :] = (xh * vec_ref[0:1, :] + vec_ref[1:2, :]).astype(BF)
    send(8, xh1, xh1_h)
    send(9, rstd1, rstd1_h)
    h1t[...] = h1[...].T
    send(10, h1t, h1t_h)
    loads[0].wait()
    span = images * ROWS
    pad = qkv.shape[1] - span
    for t in range(3 * n_quads):
        qkv[t, span:, :] = jnp.zeros((pad, TILE), BF)

    def proj(t, _):
        col = pl.multiple_of(t * TILE, TILE)
        r = mm(h1[...], wqkv[:, pl.ds(col, TILE)]) + bias[0:1, pl.ds(col, TILE)]
        r = r * jnp.where(t < n_quads, HEAD_DIM ** -0.5, 1.0)
        qkv[t, 0:span, :] = r.astype(BF)
        return 0

    lax.fori_loop(0, 3 * n_quads, proj, 0, unroll=3)
    send(1, qkv, qkv_h)
    masks = head_masks()

    def attend(it, _):
        i = it // n_quads
        j = it % n_quads
        r0 = pl.multiple_of(i * ROWS, 16)
        q4 = qkv[j, pl.ds(r0, ROWS), :]
        k4 = qkv[n_quads + j, pl.ds(r0, WIN), :]
        v4 = qkv[2 * n_quads + j, pl.ds(r0, WIN), :]
        valid = keep8[pl.ds(i, 1), :] > 0.0
        out = jnp.zeros((ROWS, TILE), F32)
        for h, m in enumerate(masks):
            s = mm(q4 * m, k4, NT)
            s = jnp.where(valid, s, -1e30)
            e = jnp.exp(s - jnp.max(s, axis=1, keepdims=True))
            pb = (e * (1.0 / jnp.sum(e, axis=1, keepdims=True))).astype(BF)
            p_s[it, h * ROWS:(h + 1) * ROWS, :] = pb
            out = out + mm(pb, v4 * m)
        o_s[j, pl.ds(r0, ROWS), :] = out.astype(BF)
        return 0

    lax.fori_loop(0, images * n_quads, attend, 0, unroll=2)
    send(2, p_s, p_h)
    for j in range(n_quads):
        ot[j * TILE:(j + 1) * TILE, :] = o_s[j].T
    send(3, ot, ot_h)
    loads[1].wait()
    pooled_ref[...] = jnp.zeros_like(pooled_ref)
    for i in range(images):
        rows = slice(i * ROWS, (i + 1) * ROWS)
        x = xs[i * SEQ:i * SEQ + ROWS, :]
        y = x + vec_ref[4:5, :]
        for j in range(n_quads):
            y = y + mm(o_s[j, rows, :], wout[j * TILE:(j + 1) * TILE, :])
        kc = kcol[rows, 0:1]
        pooled_ref[i:i + 1, 0:D] = jnp.sum(y * kc, axis=0, keepdims=True)
        cen = y - jnp.mean(y, axis=1, keepdims=True)
        inv = lax.rsqrt(jnp.mean(cen * cen, axis=1, keepdims=True) + 1e-6)
        xh = cen * inv
        xh2[rows, :] = xh.astype(BF)
        rstd2[rows, :] = jnp.broadcast_to(inv, (ROWS, 128))
        h2[rows, :] = (xh * vec_ref[5:6, :] + vec_ref[6:7, :]).astype(BF)
    h2t[...] = h2[...].T
    send(4, h2t, h2t_h)
    send(5, xh2, xh2_h)
    send(6, rstd2, rstd2_h)
    loads[2].wait()
    loads[3].wait()
    acc[...] = jnp.zeros_like(acc)
    a_s[span:, :] = jnp.zeros((a_s.shape[0] - span, TILE), BF)
    a_t[span:, :] = jnp.zeros((a_s.shape[0] - span, TILE), BF)


    def pool(t, a_s):
        ap = jnp.zeros((kmask.shape[1], TILE), F32)
        for i in range(images):
            ap = ap + mm(kmask[i], a_s[i * ROWS:i * ROWS + WIN, :])
        at = pl.multiple_of((t % n_quads) * TILE, TILE)
        apool_ref[t // n_quads, :, pl.ds(at, TILE)] = ap[0:8]
        hi = ap.astype(BF)
        lo = (ap - hi.astype(F32)).astype(BF)
        both = mm(jnp.concatenate([hi, lo], axis=0), wdown[pl.ds(pl.multiple_of(t * TILE, TILE), TILE), :])
        acc[...] += both[0:16] + both[16:32]

    def lift(t, u_s):
        col = pl.multiple_of(t * TILE, TILE)
        u_s[...] = mm(h2[...], wup[:, pl.ds(col, TILE)]) + upb_ref[0:1, pl.ds(col, TILE)]

    def bend(t, u_s, a_s):
        for i in range(images):
            rows = slice(i * ROWS, (i + 1) * ROWS)
            a, g = gelu_pair(u_s[rows, :])
            a_s[rows, :] = a.astype(BF)
            gk[t, rows, :] = (g * kcol[rows, 0:1]).astype(BF)
        pltpu.make_async_copy(gk.at[t], gk_h.at[t], out_sem.at[7]).start()

    lift(0, u_a)

    def feed(r, _):
        t = 2 * r
        lift(t + 1, u_b)
        bend(t, u_a, a_s)
        pool(t, a_s)
        lift(jnp.minimum(t + 2, n_ff - 1), u_a)
        bend(t + 1, u_b, a_t)
        pool(t + 1, a_t)
        return 0

    lax.fori_loop(0, n_ff // 2, feed, 0)
    cnt = jnp.sum(kb, axis=1, keepdims=True)[0:8]
    inv = 1.0 / jnp.maximum(cnt, 1.0)
    pooled_ref[:, 0:D] = (pooled_ref[:, 0:D] + acc[0:8, :]) * inv + vec_ref[7:8, :]
    pooled_ref[:, D:] = jnp.broadcast_to(cnt, (8, 128))
    for c in stores:
        c.wait()
    for t in range(n_ff):
        pltpu.make_async_copy(gk.at[t], gk_h.at[t], out_sem.at[7]).wait()


def forward_call(images, ff, tokens, keep, wqkv, wout, wup, wdown, vec, upb):
    span = images * ROWS
    nq = D // TILE
    wide = span + WIN - ROWS
    outs = [
        ((D, span), BF), ((3 * nq, wide, TILE), BF), ((images * nq, 4 * ROWS, TILE), BF),
        ((D, span), BF), ((D, span), BF), ((span, D), BF), ((span, D), BF), ((span, 128), F32), ((span, 128), F32),
        ((span, 128), F32), ((ff // TILE, span, TILE), BF), ((ff // D, 8, D), F32), ((8, D + 128), F32),
    ]
    anyspec = pl.BlockSpec(memory_space=pl.ANY)
    vm = pl.BlockSpec(memory_space=pltpu.VMEM)
    scratch = [
        pltpu.VMEM((D, 3 * D), BF), pltpu.VMEM((D, D), BF), pltpu.VMEM((D, ff), BF), pltpu.VMEM((ff, D), BF),
        pltpu.VMEM(((images - 1) * SEQ + ROWS + 7 & -8, D), F32),
    ] + [pltpu.VMEM(*o) for o in outs[:11]] + [
        pltpu.VMEM((span, D), BF), pltpu.VMEM((nq, span, TILE), BF), pltpu.VMEM((span, D), BF),
        pltpu.VMEM((wide, TILE), BF), pltpu.VMEM((wide, TILE), BF), pltpu.VMEM((span, TILE), F32), pltpu.VMEM((span, TILE), F32), pltpu.VMEM((16, WIN), F32), pltpu.VMEM((images, 16, WIN), BF),
        pltpu.VMEM((1, 3 * D), F32), pltpu.VMEM((16, D), F32),
        pltpu.SemaphoreType.DMA((4,)), pltpu.SemaphoreType.DMA((11,)),
    ]
    return pl.pallas_call(
        functools.partial(forward_kernel, images, ff),
        out_shape=[jax.ShapeDtypeStruct(s, d) for s, d in outs],
        in_specs=[vm, vm] + [anyspec] * 4 + [vm, vm],
        out_specs=[anyspec] * 11 + [vm, vm],
        scratch_shapes=scratch,
        compiler_params=pltpu.CompilerParams(vmem_limit_bytes=60 * 2**20),
        name="block_forward",
    )(tokens, keep, wqkv, wout, wup, wdown, vec, upb)


def split3(x):
    hi = x.astype(BF)
    r = x - hi.astype(F32)
    mid = r.astype(BF)
    lo = (r - mid.astype(F32)).astype(BF)
    return hi, mid, lo


NN = (((1,), (0,)), ((), ()))
MESH = pl.DeviceIdType.MESH


def mm3(x, w, dims=NN):
    hi, mid, lo = split3(x)
    return (mm(lo, w, dims) + mm(mid, w, dims)) + mm(hi, w, dims)


def place(cz, cy):
    row = lax.axis_index("row")
    col = lax.axis_index("col")
    return row, col // (2 * cy), lax.rem(col // 2, cy), lax.rem(col, 2)


def head_kernel(
    n_row, cz, cy, images, ff,
    pooled_ref, texts_ref, apool_ref, pair_ref, scale_ref, wproj_ref, wdown_h,
    loss_ref, dy_ref, da_ref, text_ref, proj_ref, down_ref,
    pg, tg, ax, ag, wdown, p_all, t_all, c_all, a_all, gproj, gdown,
    in_sem, zs, zr, ps, pr, cs, cr,
):
    x, z, y, core = place(cz, cy)
    load = pltpu.make_async_copy(wdown_h, wdown, in_sem.at[0])
    load.start()
    half = D // 2
    plane = n_row * cy
    spot = x * cy + y

    def device(xx, zz, yy, cc):
        return (xx, (zz * cy + yy) * 2 + cc)

    z_peers = [lax.rem(z + k, cz) for k in range(1, cz)]
    p_peers = [lax.rem(spot + k, plane) for k in range(1, plane)]
    bar = pltpu.get_barrier_semaphore()
    for zz in z_peers:
        pl.semaphore_signal(bar, inc=1, device_id=device(x, zz, y, core), device_id_type=MESH)
    for pp in p_peers:
        pl.semaphore_signal(bar, inc=1, device_id=device(pp // cy, z, lax.rem(pp, cy), core), device_id_type=MESH)
    pl.semaphore_signal(bar, inc=1, device_id=device(x, z, y, 1 - core), device_id_type=MESH)
    pg[x, z, y, core] = jnp.concatenate([pooled_ref[0:images, 0:half], pooled_ref[0:images, half:D]], axis=0)
    text = texts_ref[...].astype(F32)
    tg[x, z, y, core] = jnp.concatenate([text[:, k * 128:(k + 1) * 128] for k in range(EMB // 128)], axis=0).astype(BF)
    for g in range(cz):
        ax[g, 0:images, 0:half] = apool_ref[g, 0:images, 0:half]
        ax[g, images:, 0:half] = apool_ref[g, 0:images, half:]
        ax[g, 0:images, half:] = pooled_ref[0:images, D:]
        ax[g, images:, half:] = pooled_ref[0:images, D:]
    ag[x, z, y, core] = ax[z]
    pl.semaphore_wait(bar, cz - 1 + plane - 1 + 1)

    def stage(src, dst, sems, slot, devs):
        out = []
        for k, (s, dev) in enumerate(zip(src, devs)):
            c = pltpu.make_async_remote_copy(
                s, dst, sems[0].at[slot, k], sems[1].at[slot, k], device_id=dev, device_id_type=MESH)
            c.start()
            out.append(c)
        return out

    z_devs = [device(x, zz, y, core) for zz in z_peers]
    p_devs = [device(pp // cy, z, lax.rem(pp, cy), core) for pp in p_peers]
    c_devs = [device(x, z, y, 1 - core)]
    own = pg.at[x, z, y, core]
    own_t = tg.at[x, z, y, core]
    first = stage([own] * len(z_devs), own, (zs, zr), 0, z_devs)
    first_t = stage([own_t] * len(z_devs), own_t, (zs, zr), 2, z_devs)
    for c in first:
        c.wait()
    own = pg.at[x, :, y, core]
    second = stage([own] * len(p_devs), own, (ps, pr), 0, p_devs)
    for c in first_t:
        c.wait()
    own_t = tg.at[x, :, y, core]
    second_t = stage([own_t] * len(p_devs), own_t, (ps, pr), 2, p_devs)
    first_a = stage([ax.at[zz] for zz in z_peers], ag.at[x, z, y, core], (zs, zr), 1, z_devs)
    for c in second:
        c.wait()
    own = pg.at[:, :, :, core]
    third = stage([own], own, (cs, cr), 0, c_devs)
    for c in second_t:
        c.wait()
    own_t = tg.at[:, :, :, core]
    third_t = stage([own_t], own_t, (cs, cr), 2, c_devs)
    for c in first_a:
        c.wait()
    own = ag.at[x, :, y, core]
    second_a = stage([own] * len(p_devs), own, (ps, pr), 1, p_devs)
    for c in third:
        c.wait()
    n_col = cz * cy * 2
    n_img = n_row * n_col * images
    for d in range(n_row * n_col):
        rows = slice(d * images, (d + 1) * images)
        at = (d // n_col, d % n_col // (2 * cy), d // 2 % cy, d % 2)
        p_all[rows, 0:half] = pg[at + (slice(0, images),)]
        p_all[rows, half:] = pg[at + (slice(images, 2 * images),)]
    scale = scale_ref[0]
    pooled = p_all[...]
    latent = mm3(pooled, wproj_ref[...])
    norm = lax.rsqrt(jnp.sum(latent * latent, axis=1, keepdims=True) + 1e-6)
    embeds = latent * norm
    eb = embeds.astype(BF)
    for c in third_t:
        c.wait()
    for d in range(n_row * n_col):
        rows = slice(d * images, (d + 1) * images)
        text = tg[d // n_col, d % n_col // (2 * cy), d // 2 % cy, d % 2].astype(F32)
        for k in range(EMB // 128):
            t_all[rows, k * 128:(k + 1) * 128] = text[k * images:(k + 1) * images]
    tb = t_all[...].astype(BF)
    logits = scale * mm(eb, tb, NT)
    row_max = jnp.max(logits, axis=1, keepdims=True)
    row_exp = jnp.exp(logits - row_max)
    row_sum = jnp.sum(row_exp, axis=1, keepdims=True)
    col_max = jnp.max(logits, axis=0, keepdims=True)
    col_exp = jnp.exp(logits - col_max)
    col_sum = jnp.sum(col_exp, axis=0, keepdims=True)
    ids = lax.broadcasted_iota(jnp.int32, (n_img, n_img), 0)
    match = (ids == pair_ref[...]).astype(F32).T
    grad = 0.5 * (row_exp / row_sum) + 0.5 * (col_exp / col_sum) - match
    lse = jnp.sum(row_max + jnp.log(row_sum), axis=0, keepdims=True) + jnp.sum(
        col_max + jnp.log(col_sum), axis=1, keepdims=True)
    hits = jnp.sum(jnp.sum(logits * match, axis=1, keepdims=True), axis=0, keepdims=True)
    loss_ref[...] = (0.5 * lse - hits) * (1.0 / n_img)
    de = scale * mm3(grad, tb)
    dz = norm * (de - embeds * jnp.sum(embeds * de, axis=1, keepdims=True))
    pooled_grad = mm3(dz, wproj_ref[...], NT)
    dev = x * n_col + (z * cy + y) * 2 + core
    want = lax.broadcasted_iota(jnp.int32, (16, n_img), 0) + dev * images
    have = lax.broadcasted_iota(jnp.int32, (16, n_img), 1)
    pick = (want == have).astype(F32).astype(BF)
    hi, mid, lo = split3(pooled_grad)
    dy = (mm(pick, lo) + mm(pick, mid)) + mm(pick, hi)
    dy = dy[0:8] / jnp.maximum(pooled_ref[:, D:D + 1], 1.0)
    dy_ref[...] = dy
    dyb = jnp.concatenate([dy, jnp.zeros_like(dy)], axis=0).astype(BF)
    for c in second_a:
        c.wait()
    own = ag.at[:, :, :, core]
    third_a = stage([own], own, (cs, cr), 1, c_devs)
    load.wait()

    for t in range(ff // TILE):
        sl = slice(t * TILE, (t + 1) * TILE)
        da_ref[:, sl] = mm(dyb, wdown[sl, :], NT)[0:8]
    g_hi, g_mid, g_lo = split3(grad)
    own_grad = (mm(pick, g_lo, NT) + mm(pick, g_mid, NT)) + mm(pick, g_hi, NT)
    text_ref[...] = (scale * mm3(own_grad, eb))[0:images]
    p_hi, p_lo, _ = split3(pooled)
    d_hi, d_lo, _ = split3(dz)
    gproj[...] = (mm(p_lo, d_hi, TN) + mm(p_hi, d_lo, TN)) + mm(p_hi, d_hi, TN)
    n_proj = D // n_col
    at = pl.multiple_of(((z * cy + y) * 2 + core) * n_proj, 8)
    proj_ref[...] = gproj[pl.ds(at, n_proj), :]
    for c in third_a:
        c.wait()
    for d in range(n_row * n_col):
        rows = slice(d * images, (d + 1) * images)
        at = (d // n_col, d % n_col // (2 * cy), d // 2 % cy, d % 2)
        a_all[rows, 0:half] = ag[at + (slice(0, images), slice(0, half))]
        a_all[rows, half:] = ag[at + (slice(images, 2 * images), slice(0, half))]
        c_all[rows, :] = ag[at + (slice(0, images), slice(half, half + 128))]
    hi = (pooled_grad / c_all[:, 0:1]).astype(BF)
    acts = a_all[...]
    a_hi = acts.astype(BF)
    a_lo = (acts - a_hi.astype(F32)).astype(BF)
    for n in range(D // TILE):
        sl = slice(n * TILE, (n + 1) * TILE)
        gdown[:, sl] = mm(a_lo, hi[:, sl], TN) + mm(a_hi, hi[:, sl], TN)
    n_down = ff // n_col
    at = pl.multiple_of((y * 2 + core) * n_down, 8)
    down_ref[...] = gdown[pl.ds(at, n_down), :]


def head_call(n_row, n_col, images, ff, pooled, texts, apool, pair, scale, wproj, wdown):
    cz = ff // D
    cy = n_col // (2 * cz)
    n_img = n_row * n_col * images
    vm = pl.BlockSpec(memory_space=pltpu.VMEM)
    outs = [(1, 1), (8, D), (8, ff), (images, EMB), (D // n_col, EMB), (ff // n_col, D)]
    plane = n_row * cy
    grid = (n_row, cz, cy, 2, 2 * images)
    scratch = [
        pltpu.VMEM(grid + (D // 2,), F32), pltpu.VMEM(grid[:4] + (images * EMB // 128, 128), BF),
        pltpu.VMEM((cz, 2 * images, D // 2 + 128), F32), pltpu.VMEM(grid + (D // 2 + 128,), F32),
        pltpu.VMEM((ff, D), BF), pltpu.VMEM((n_img, D), F32), pltpu.VMEM((n_img, EMB), F32),
        pltpu.VMEM((n_img, 128), F32), pltpu.VMEM((n_img, D), F32), pltpu.VMEM((D, EMB), F32), pltpu.VMEM((D, D), F32),
        pltpu.SemaphoreType.DMA((1,)), pltpu.SemaphoreType.DMA((3, cz - 1)), pltpu.SemaphoreType.DMA((3, cz - 1)),
        pltpu.SemaphoreType.DMA((3, plane - 1)), pltpu.SemaphoreType.DMA((3, plane - 1)),
        pltpu.SemaphoreType.DMA((3, 1)), pltpu.SemaphoreType.DMA((3, 1)),
    ]
    return pl.pallas_call(
        functools.partial(head_kernel, n_row, cz, cy, images, ff),
        out_shape=[jax.ShapeDtypeStruct(s, F32) for s in outs],
        in_specs=[vm] * 4 + [pl.BlockSpec(memory_space=pltpu.SMEM), vm, pl.BlockSpec(memory_space=pl.ANY)],
        out_specs=[vm] * len(outs),
        scratch_shapes=scratch,
        compiler_params=pltpu.CompilerParams(
            vmem_limit_bytes=60 * 2**20, collective_id=0, has_side_effects=True),
        name="contrastive_head",
    )(pooled, texts, apool, pair, scale, wproj, wdown)


READY = [2, 5, 8, 11, 18, 23, 28, 33]
WAITS = [[(6, 0), (9, 1), (12, 2), (13, 3), (20, 4), (25, 5), (30, 6), (35, 7)], [(13, 0), (15, 1), (20, 2), (23, 3), (27, 4), (32, 5), (36, 6)], [(16, 0), (20, 1), (25, 2), (27, 3), (32, 4), (36, 5)], [(24, 0), (25, 1), (29, 2), (33, 3), (36, 4)], [(28, 0), (29, 1), (33, 2), (37, 3)]]
TAIL = [(1, 7), (4, 4), (3, 5), (2, 6), (4, 5), (2, 7), (3, 6), (4, 6), (3, 7), (4, 7)]


def backward_kernel(
    n_row, cz, cy, images, ff, n_a,
    dy_ref, da_ref, vec_ref,
    wqkv_h, wout_h, wup_h, h1t_h, qkv_h, p_h, ot_h, h2t_h, xh1_h, xh2_h, rstd1_h, rstd2_h, kcol_h, gk_h,
    tg_h, qg_ref, og_ref, ug_ref, small_ref,
    tg_ref, wqkv, wout, wup, h1t, qkv, ot, h2t, xh1, xh2, rstd1, rstd2, kcol, p_s, du, dx, db, do_s, dp_s,
    g, r0, r1a, r1b, r2a, r2b, r3a, r3b, r4b, res, vc, vp, vz, sv, small_s,
    in_sem, gk_sem, p_sem, s_sem, r_sem, vs_sem, vr_sem,
):
    n_quads = D // TILE
    n_ff = ff // TILE
    n_up = ff // D
    n_chunks = n_up + 1 + n_quads
    masks = head_masks()
    x, z, y, core = place(cz, cy)
    two = n_a < D
    n_h = (D - n_a) // 2
    plane = n_row * cy
    spot = x * cy + y

    def device(xx, zz, yy, cc):
        return (xx, (zz * cy + yy) * 2 + cc)

    core_dev = device(x, z, y, 1 - core)
    y_peers = [lax.rem(y + k, cy) for k in range(1, cy)]
    z_peers = [lax.rem(z + k, cz) for k in range(1, cz)]
    x_peers = [lax.rem(x + k, n_row) for k in range(1, n_row)]
    p_peers = [lax.rem(spot + k, plane) for k in range(1, plane)]
    z_devs = [device(x, zz, y, core) for zz in z_peers]
    y_devs = [device(x, z, yy, core) for yy in y_peers]
    x_devs = [device(xx, z, y, core) for xx in x_peers]
    p_devs = [device(pp // cy, z, lax.rem(pp, cy), core) for pp in p_peers]

    loads = {}
    for k, (name, src, dst) in enumerate((
        ("kcol", kcol_h, kcol), ("h2t", h2t_h, h2t), ("wup", wup_h, wup), ("xh2", xh2_h, xh2),
        ("rstd2", rstd2_h, rstd2), ("wout", wout_h, wout), ("ot", ot_h, ot), ("qkv", qkv_h, qkv),
        ("h1t", h1t_h, h1t), ("wqkv", wqkv_h, wqkv), ("xh1", xh1_h, xh1), ("rstd1", rstd1_h, rstd1),
    )):
        loads[name] = pltpu.make_async_copy(src, dst, in_sem.at[k])

    def gcopy(t):
        col = pl.multiple_of(t * TILE, TILE)
        return pltpu.make_async_copy(gk_h.at[t], du.at[:, pl.ds(col, TILE)], gk_sem.at[t])

    loads["h2t"].start()
    for t in range(n_ff):
        gcopy(t).start()
    for name in ("kcol", "wup", "xh2", "rstd2", "wout", "ot", "qkv", "h1t", "wqkv", "xh1", "rstd1"):
        loads[name].start()

    def pcopy(step):
        i = lax.rem(step, images)
        j = step // images
        slot = lax.rem(step, 2)
        return pltpu.make_async_copy(p_h.at[i * n_quads + j], p_s.at[slot], p_sem.at[slot])

    pcopy(0).start()
    bar = pltpu.get_barrier_semaphore()
    for dev in z_devs + p_devs + [core_dev]:
        pl.semaphore_signal(bar, inc=1, device_id=dev, device_id_type=MESH)
    half = lambda which: pl.ds(pl.multiple_of(n_a + which * n_h, 128), n_h)

    def copies(p, c):
        if p == 0:
            out = [(g.at[lax.rem(c, 4), :, :, 1 - core], r0.at[c], core_dev)]
        elif p == 1:
            out = [(r0.at[c, :, yy, :, 0:n_a], r1a.at[c, k], dev) for k, (yy, dev) in enumerate(zip(y_peers, y_devs))]
            if two:
                out += [(r0.at[c, :, :, :, half(1 - x)], r1b.at[c], x_devs[0])]
        elif p == 2:
            out = [(r1a.at[c, 0, zz], r2a.at[c, k], dev) for k, (zz, dev) in enumerate(zip(z_peers, z_devs))]
            if two:
                out += [(r1b.at[c, :, yy], r2b.at[c, k], dev) for k, (yy, dev) in enumerate(zip(y_peers, y_devs))]
        elif p == 3:
            out = [(r3a.at[c, x], r3a.at[c, x], dev) for dev in x_devs]
            if two:
                out += [(r2b.at[c, 0, zz], r3b.at[c, k], dev) for k, (zz, dev) in enumerate(zip(z_peers, z_devs))]
        else:
            out = [(r3b.at[c, 0], r4b.at[c], x_devs[0])] if two else []
        base = (0, 1, 1 + cy, cz + 2 * cy - 1, 2 * cz + 2 * cy + n_row - 3)[p]
        return [
            pltpu.make_async_remote_copy(
                src, dst, s_sem.at[lax.rem(c, 4), base + k], r_sem.at[c, base + k], device_id=dev, device_id_type=MESH)
            for k, (src, dst, dev) in enumerate(out)
        ]

    def finish(p, c):
        up = lambda v: v.astype(F32)
        if p == 0:
            r0[c] = r0[c] + g[lax.rem(c, 4), :, :, core]
        elif p == 1:
            v = up(r0[c, :, y, :, 0:n_a])
            for k in range(cy - 1):
                v = v + up(r1a[c, k])
            r1a[c, 0] = v.astype(BF)
            if two:
                r1b[c] = r1b[c] + r0[c, :, :, :, half(x)]
        elif p == 2:
            v = up(r1a[c, 0, z])
            for k in range(cz - 1):
                v = v + up(r2a[c, k])
            r3a[c, x] = v.astype(BF)
            if two:
                v = up(r1b[c, :, y])
                for k in range(cy - 1):
                    v = v + up(r2b[c, k])
                r2b[c, 0] = v.astype(BF)
        elif p == 3:
            v = up(r3a[c, 0])
            for k in range(1, n_row):
                v = v + up(r3a[c, k])
            res[c, :, 0:n_a] = v
            if two:
                v = up(r2b[c, 0, z])
                for k in range(cz - 1):
                    v = v + up(r3b[c, k])
                v = v.astype(BF)
                r3b[c, 0] = v
                res[c, :, half(x)] = up(v)
        elif two:
            res[c, :, half(1 - x)] = up(r4b[c])

    def begin(p, c):
        for d in copies(p, c):
            d.start()

    def advance(p, c):
        for d in copies(p, c):
            d.wait()
        finish(p, c)
        if p < 4:
            begin(p + 1, c)

    def lookup(n, events):
        hit = n < 0
        c = jnp.int32(0)
        for at, chunk in events:
            same = n == at
            hit = hit | same
            c = jnp.where(same, chunk, c)
        return hit, c

    def tick(n):
        @pl.when(n == READY[0])
        def _():
            pl.semaphore_wait(bar, len(z_devs) + len(p_devs) + 1)

        hit, c = lookup(n, [(at, k) for k, at in enumerate(READY)])

        @pl.when(hit)
        def _():
            begin(0, c)

        for p in range(4, -1, -1):
            hit, c = lookup(n, WAITS[p])

            @pl.when(hit)
            def _(p=p, c=c):
                advance(p, c)

    def put(c, tt, part):
        col = pl.multiple_of(tt * TILE, TILE)
        g[lax.rem(c, 4), :, :, :, :, pl.ds(col, TILE)] = part.reshape(g.shape[1:5] + (TILE,)).astype(BF)

    def unit_up(t):
        n = t // n_quads
        tt = lax.rem(t, n_quads)
        col = pl.multiple_of(t * TILE, TILE)
        gcopy(t).wait()
        ub = jnp.zeros((1, TILE), F32)
        for i in range(images):
            rows = slice(i * ROWS, (i + 1) * ROWS)
            d = du[rows, pl.ds(col, TILE)].astype(F32) * da_ref[i:i + 1, pl.ds(col, TILE)]
            ub = ub + jnp.sum(d, axis=0, keepdims=True)
            du[rows, pl.ds(col, TILE)] = d.astype(BF)
        scol = pl.multiple_of(tt * TILE, TILE)
        small_s[pl.ds(8 + n, 1), pl.ds(scol, TILE)] = ub
        put(n, tt, mm(h2t[...], du[:, pl.ds(col, TILE)]))

    def unit_down(n):
        @pl.when(n == 0)
        def _():
            loads["wup"].wait()

        col = pl.multiple_of(n * TILE, TILE)
        dx[:, pl.ds(col, TILE)] = mm(du[...], wup[pl.ds(col, TILE), :], NT)

    def unit_mid():
        for name in ("kcol", "xh2", "rstd2", "wout", "ot"):
            loads[name].wait()
        dy = dy_ref[...]
        dyb = dy.astype(BF).astype(F32)
        g2 = jnp.zeros((1, D), F32)
        b2 = jnp.zeros((1, D), F32)
        bo = jnp.zeros((1, D), F32)
        bd = jnp.zeros((1, D), F32)
        for i in range(images):
            rows = slice(i * ROWS, (i + 1) * ROWS)
            kc = kcol[rows, 0:1]
            bd = bd + jnp.sum(kc, axis=0, keepdims=True) * dyb[i:i + 1, :]
            dh = dx[rows, :]
            xh = xh2[rows, :].astype(F32)
            g2 = g2 + jnp.sum(dh * xh, axis=0, keepdims=True)
            b2 = b2 + jnp.sum(dh, axis=0, keepdims=True)
            c = dh * vec_ref[5:6, :]
            m1 = jnp.mean(c, axis=1, keepdims=True)
            m2 = jnp.mean(c * xh, axis=1, keepdims=True)
            r = dy[i:i + 1, :] * kc + rstd2[rows, 0:1] * (c - m1 - xh * m2)
            dx[rows, :] = r
            rb = r.astype(BF)
            db[rows, :] = rb
            bo = bo + jnp.sum(rb.astype(F32), axis=0, keepdims=True)
        small_s[0:4, :] = jnp.zeros((4, D), F32)
        small_s[4:5, :] = bo
        small_s[5:6, :] = g2
        small_s[6:7, :] = b2
        small_s[7:8, :] = bd
        for name in ("qkv", "h1t"):
            loads[name].wait()

    def unit_out(j):
        col = pl.multiple_of(j * TILE, TILE)
        do_s[j] = mm(db[...], wout[pl.ds(col, TILE), :], NT).astype(BF)
        put(n_up, j, mm(ot[...], db[:, pl.ds(col, TILE)]))

    def unit_attend(j, i):
        r0_ = pl.multiple_of(i * ROWS, 16)
        step = j * images + i
        slot = lax.rem(step, 2)

        @pl.when(step + 1 < n_quads * images)
        def _():
            pcopy(step + 1).start()

        pcopy(step).wait()
        q4 = qkv[j, pl.ds(r0_, ROWS), :]
        k4 = qkv[n_quads + j, pl.ds(r0_, WIN), :]
        v4 = qkv[2 * n_quads + j, pl.ds(r0_, WIN), :]
        d4 = do_s[j, pl.ds(r0_, ROWS), :]
        dp = mm(jnp.concatenate([d4 * mask for mask in masks], axis=0), v4, NT)
        pb = p_s[slot]
        pf = pb.astype(F32)
        ds = (pf * (dp - jnp.sum(pf * dp, axis=1, keepdims=True))).astype(BF)
        dq = jnp.zeros((ROWS, TILE), F32)
        dt = d4.T
        qt = q4.T
        dv = []
        dk = []
        for h, mask in enumerate(masks):
            rows = slice(h * ROWS, (h + 1) * ROWS)
            cut = slice(h * HEAD_DIM, (h + 1) * HEAD_DIM)
            dq = dq + mm(ds[rows], k4 * mask)
            dv.append(mm(dt[cut], pb[rows]))
            dk.append(mm(qt[cut], ds[rows]))
        dv = jnp.concatenate(dv, axis=0).T
        dk = jnp.concatenate(dk, axis=0).T
        dq = dq * HEAD_DIM ** -0.5
        dv = dv[0:ROWS]
        sl = pl.ds(pl.multiple_of(j * TILE, TILE), TILE)
        small_s[2:3, sl] += jnp.sum(dq, axis=0, keepdims=True)
        small_s[3:4, sl] += jnp.sum(dv, axis=0, keepdims=True)
        for s, val in enumerate((dq, dk[0:ROWS], dv)):
            col = pl.multiple_of(s * D + j * TILE, TILE)
            dp_s[pl.ds(r0_, ROWS), pl.ds(col, TILE)] = val.astype(BF)

    def unit_weight(j):
        for s in range(3):
            col = pl.multiple_of(s * D + j * TILE, TILE)
            put(n_up + 1 + j, s, mm(h1t[...], dp_s[:, pl.ds(col, TILE)]))

    def unit_norm(i):
        @pl.when(i == 0)
        def _():
            for name in ("wqkv", "xh1", "rstd1"):
                loads[name].wait()

        rows = pl.ds(pl.multiple_of(i * ROWS, 16), ROWS)
        dh = mm(dp_s[rows, :], wqkv[...], NT)
        xh = xh1[rows, :].astype(F32)
        small_s[0:1, :] += jnp.sum(dh * xh, axis=0, keepdims=True)
        small_s[1:2, :] += jnp.sum(dh, axis=0, keepdims=True)
        c = dh * vec_ref[0:1, :]
        m1 = jnp.mean(c, axis=1, keepdims=True)
        m2 = jnp.mean(c * xh, axis=1, keepdims=True)
        r = dx[rows, :] + rstd1[rows, 0:1] * (c - m1 - xh * m2)
        for k in range(images):
            @pl.when(i == k)
            def _(k=k):
                tg_ref[k * SEQ:(k + 1) * SEQ, :] = r[0:SEQ]

    small_s[...] = jnp.zeros_like(small_s)
    loads["h2t"].wait()
    t_down = n_ff
    t_mid = t_down + n_quads
    t_out = t_mid + 1
    t_attend = t_out + n_quads
    t_norm = t_attend + n_quads * (images + 1)

    def unit(n, _):
        @pl.when(n < t_down)
        def _():
            unit_up(n)

        @pl.when((n >= t_down) & (n < t_mid))
        def _():
            unit_down(n - t_down)

        @pl.when(n == t_mid)
        def _():
            unit_mid()

        @pl.when((n >= t_out) & (n < t_attend))
        def _():
            unit_out(n - t_out)

        m = n - t_attend
        inner = lax.rem(m, images + 1)

        @pl.when((m >= 0) & (n < t_norm) & (inner < images))
        def _():
            unit_attend(m // (images + 1), inner)

        @pl.when((m >= 0) & (n < t_norm) & (inner == images))
        def _():
            unit_weight(m // (images + 1))

        @pl.when(n >= t_norm)
        def _():
            unit_norm(n - t_norm)

        tick(n)
        return 0

    lax.fori_loop(0, t_norm + images, unit, 0)
    leave = pltpu.make_async_copy(tg_ref, tg_h, in_sem.at[12])
    leave.start()

    def spread(src, dst, slot, devs):
        out = []
        for k, dev in enumerate(devs):
            d = pltpu.make_async_remote_copy(
                src[k], dst, vs_sem.at[slot, k], vr_sem.at[slot, k], device_id=dev, device_id_type=MESH)
            d.start()
            out.append(d)
        return out

    def total(ref, count):
        v = ref[0]
        for k in range(1, count):
            v = v + ref[k]
        return v

    part = D // cz
    for zz in range(cz):
        sv[zz, 0:8, 0:part] = small_s[0:8, zz * part:(zz + 1) * part]
        for k in range(D // part):
            sv[zz, 8 + k:9 + k, 0:part] = small_s[8 + zz:9 + zz, k * part:(k + 1) * part]
    vz[z] = sv[z]
    going = spread([sv.at[zz] for zz in z_peers], vz.at[z], 0, z_devs)
    for e, (p, c) in enumerate(TAIL):
        advance(p, c)
        if e == len(TAIL) // 3:
            for d in going:
                d.wait()
            vp[spot] = total(vz, cz)
            going = spread([vp.at[spot]] * len(p_devs), vp.at[spot], 1, p_devs)
        if e == 2 * len(TAIL) // 3:
            for d in going:
                d.wait()
            vc[core] = total(vp, plane)
            going = spread([vc.at[core]], vc.at[core], 2, [core_dev])
    for d in going:
        d.wait()
    small_ref[...] = total(vc, 2)
    leave.wait()
    for c in range(n_up):
        ug_ref[:, c * D:(c + 1) * D] = res[c]
    og_ref[...] = res[n_up]
    for j in range(n_quads):
        for s in range(3):
            qg_ref[:, s * D + j * TILE:s * D + (j + 1) * TILE] = res[n_up + 1 + j, :, s * TILE:(s + 1) * TILE]


def backward_call(n_row, n_col, images, ff, dy, da, vec, wqkv, wout, wup, acts):
    span = images * ROWS
    nq = D // TILE
    wide = span + WIN - ROWS
    cz = ff // D
    cy = n_col // (2 * cz)
    blk = D // n_col
    n_a = 256 if n_row == 2 else D
    n_h = max((D - n_a) // 2, 128)
    n_ch = ff // D + 1 + nq
    plane = n_row * cy
    n_sem = 2 * cz + 2 * cy + n_row - 2
    anyspec = pl.BlockSpec(memory_space=pl.ANY)
    vm = pl.BlockSpec(memory_space=pltpu.VMEM)
    outs = [(images * SEQ, D), (blk, 3 * D), (blk, D), (blk, ff), (16, 256)]
    B16 = lambda *s: pltpu.VMEM(s, BF)
    B32 = lambda *s: pltpu.VMEM(s, F32)
    scratch = [
        B32(images * SEQ, D), B16(D, 3 * D), B16(D, D), B16(D, ff), B16(D, span), B16(3 * nq, wide, TILE), B16(D, span), B16(D, span),
        B16(span, D), B16(span, D), B32(span, 128), B32(span, 128), B32(span, 128),
        B16(2, 4 * ROWS, TILE), B16(span, ff), B32(span, D), B16(span, D), B16(nq, span, TILE), B16(span, 3 * D),
        B16(4, cz, cy, 2, blk, D), B16(n_ch, cz, cy, blk, D),
        B16(n_ch, cy - 1, cz, blk, n_a), B16(n_ch, cz, cy, blk, n_h),
        B16(n_ch, cz - 1, blk, n_a), B16(n_ch, cy - 1, cz, blk, n_h),
        B16(n_ch, n_row, blk, n_a), B16(n_ch, cz - 1, blk, n_h), B16(n_ch, blk, n_h), B32(n_ch, blk, D),
        B32(2, 16, 256), B32(plane, 16, 256), B32(cz, 16, 256), B32(cz, 16, 256), B32(16, D),
        pltpu.SemaphoreType.DMA((13,)), pltpu.SemaphoreType.DMA((ff // TILE,)), pltpu.SemaphoreType.DMA((2,)),
        pltpu.SemaphoreType.DMA((4, n_sem)), pltpu.SemaphoreType.DMA((n_ch, n_sem)),
        pltpu.SemaphoreType.DMA((3, plane)), pltpu.SemaphoreType.DMA((3, plane)),
    ]
    return pl.pallas_call(
        functools.partial(backward_kernel, n_row, cz, cy, images, ff, n_a),
        out_shape=[jax.ShapeDtypeStruct(s, F32) for s in outs],
        in_specs=[vm] * 3 + [anyspec] * 14,
        out_specs=[anyspec] + [vm] * (len(outs) - 1),
        scratch_shapes=scratch,
        compiler_params=pltpu.CompilerParams(
            vmem_limit_bytes=62 * 2**20, collective_id=1, has_side_effects=True),
        name="block_backward",
    )(dy, da, vec, wqkv, wout, wup, *acts)


def finish_kernel(n_col, cz, images, ff, small_ref, *refs):
    n_big = (len(refs) - 4) // 3
    big, vec_ref, ub_ref, outs = refs[:n_big], refs[n_big], refs[n_big + 1], refs[n_big + 2:2 * n_big + 2]
    held, in_sem, out_sem = refs[2 * n_big + 2:-2], refs[-2], refs[-1]
    moves = []
    for src, mid, dst in zip(big, held, outs):
        rows = src.shape[0]
        step = rows if rows < 400 else 200
        for at in range(0, rows, step):
            sl = pl.ds(at, min(step, rows - at))
            k = len(moves)
            c = pltpu.make_async_copy(src.at[sl], mid.at[sl], in_sem.at[k])
            c.start()
            moves.append((c, pltpu.make_async_copy(mid.at[sl], dst.at[sl], out_sem.at[k])))
    for c, d in moves:
        c.wait()
        d.start()
    member = lax.rem(lax.axis_index("col"), n_col // cz)
    part = D // cz
    values = small_ref[...]
    src = lax.broadcasted_iota(jnp.int32, (256, 256), 0)
    lane = lax.broadcasted_iota(jnp.int32, (256, 256), 1)
    width = D // n_col
    pick = (src == lane + member * width).astype(F32).astype(BF)
    vec_ref[...] = mm3(values[0:8], pick)[:, 0:width]
    n_ub = ff // n_col
    row = lax.broadcasted_iota(jnp.int32, values.shape, 0)
    line = jnp.sum(jnp.where(row == 8 + member * n_ub // part, values, 0.0), axis=0, keepdims=True)
    pick = (src == lane + lax.rem(member * n_ub, part)).astype(F32).astype(BF)
    ub_ref[...] = mm3(jnp.broadcast_to(line, (8, 256)), pick)[0:1, 0:n_ub]
    for c, d in moves:
        d.wait()


def finish_call(n_col, images, ff, small, *big):
    vm = pl.BlockSpec(memory_space=pltpu.VMEM)
    anyspec = pl.BlockSpec(memory_space=pl.ANY)
    shapes = [jax.ShapeDtypeStruct((8, D // n_col), F32), jax.ShapeDtypeStruct((1, ff // n_col), F32)]
    shapes += [jax.ShapeDtypeStruct(b.shape, b.dtype) for b in big]
    return pl.pallas_call(
        functools.partial(finish_kernel, n_col, ff // D, images, ff),
        out_shape=shapes,
        in_specs=[vm] + [anyspec] * len(big),
        out_specs=[vm, vm] + [anyspec] * len(big),
        scratch_shapes=[pltpu.VMEM(b.shape, b.dtype) for b in big] + [pltpu.SemaphoreType.DMA((12,))] * 2,
        compiler_params=pltpu.CompilerParams(vmem_limit_bytes=62 * 2**20),
        name="results",
    )(small, *big)


def per_device(
    tokens,
    keep_mask,
    w_qkv,
    w_out,
    w_up,
    w_down,
    vectors,
    up_bias,
    w_proj,
    texts,
    pair_index,
    logit_scale,
):
    images = keep_mask.shape[0]
    ff = w_up.shape[1]
    n_row, shards = lax.axis_size("row"), lax.axis_size("col")
    acts = forward_call(
        images, ff, tokens, keep_mask, w_qkv, w_out, w_up, w_down, vectors, up_bias.reshape(1, ff)
    )
    loss, dy, da, text_grad, grad_proj, grad_down = head_call(
        n_row, shards, images, ff, acts[12], texts, acts[11], pair_index.reshape(1, -1), logit_scale, w_proj, w_down
    )
    token_grad, qkv_share, out_share, up_share, small = backward_call(
        n_row, shards, images, ff, dy, da, vectors, w_qkv, w_out, w_up, acts[:11]
    )
    vec_share, bias_share, token_grad, qkv_share, out_share, up_share, grad_down, grad_proj, text_grad = finish_call(
        shards, images, ff, small, token_grad, qkv_share, out_share, up_share, grad_down, grad_proj, text_grad
    )
    return (
        loss.reshape(1),
        token_grad,
        qkv_share,
        out_share,
        up_share,
        grad_down,
        vec_share,
        bias_share.reshape(-1),
        grad_proj,
        text_grad,
    )


def solution(mesh):
    in_specs = (
        P(("row", "col"), None),
        P(("row", "col"), None),
        P(),
        P(),
        P(),
        P(),
        P(),
        P(),
        P(),
        P(("row", "col"), None),
        P(),
        P(),
    )
    out_specs = (
        P(),
        P(("row", "col"), None),
        P("col", None),
        P("col", None),
        P("col", None),
        P("col", None),
        P(None, "col"),
        P("col"),
        P("col", None),
        P(("row", "col"), None),
    )
    return jax.shard_map(
        per_device, mesh=mesh, in_specs=in_specs, out_specs=out_specs, check_vma=False
    )
```

```python
import functools

import jax
import jax.numpy as jnp
from jax import lax
from jax.experimental import pallas as pl
from jax.experimental.pallas import tpu as pltpu
from jax.sharding import PartitionSpec as P

D = 768
HEADS = 12
HEAD_DIM = 64
SEQ = 197
EMB = 512
ROWS = 208
WIN = 256
TILE = 256
F32 = jnp.float32
BF = jnp.bfloat16
NT = (((1,), (1,)), ((), ()))
TN = (((0,), (0,)), ((), ()))


def mm(a, b, dims=(((1,), (0,)), ((), ()))):
    return lax.dot_general(a, b, dims, preferred_element_type=F32)


def head_masks():
    lane = lax.broadcasted_iota(jnp.int32, (1, TILE), 1) // HEAD_DIM
    return [(lane == h).astype(F32).astype(BF) for h in range(TILE // HEAD_DIM)]


def gelu_pair(u):
    z = jnp.abs(u)
    t = 1.0 / (1.0 + (0.3275911 * 0.7071067811865476) * z)
    e = jnp.exp2((-0.5 * 1.4426950408889634) * (u * u))
    poly = 0.5 * 1.061405429
    for c in (-1.453152027, 1.421413741, -0.284496736, 0.254829592):
        poly = poly * t + 0.5 * c
    tail = poly * t * e
    cdf = jnp.where(u >= 0.0, 1.0 - tail, tail)
    return u * cdf, cdf + (0.3989422804014327 * u) * e


def forward_kernel(
    images, ff,
    tok_ref, keep_ref, wqkv_h, wout_h, wup_h, wdown_h, vec_ref, upb_ref,
    h1t_h, qkv_h, p_h, ot_h, h2t_h, xh1_h, xh2_h, rstd1_h, rstd2_h, kcol_h, gk_h, apool_ref, pooled_ref,
    wqkv, wout, wup, wdown, xs, h1t, qkv, p_s, ot, h2t, xh1, xh2, rstd1, rstd2, kcol, gk,
    h1, o_s, y_s, h2, a_s, a_t, u_a, u_b, keep8, kmask, bias, acc,
    in_sem, out_sem,
):
    n_quads = D // TILE
    n_ff = ff // TILE
    loads = []
    for k, (src, dst) in enumerate(((wqkv_h, wqkv), (wout_h, wout), (wup_h, wup), (wdown_h, wdown))):
        c = pltpu.make_async_copy(src, dst, in_sem.at[k])
        c.start()
        loads.append(c)
    stores = []

    def send(k, src, dst):
        c = pltpu.make_async_copy(src, dst, out_sem.at[k])
        c.start()
        stores.append(c)

    total = images * SEQ
    last = total // 16 * 16
    xs[last:, :] = jnp.zeros_like(xs[last:, :])
    xs[0:last, :] = tok_ref[0:last, :].astype(F32)
    if last < total:
        xs[last:total, :] = tok_ref[last:total, :].astype(F32)
    keep8[...] = jnp.zeros_like(keep8)
    keep8[0:images, 0:SEQ] = keep_ref[...].astype(F32)
    kb = keep8[...]
    rid = lax.broadcasted_iota(jnp.int32, kb.shape, 0)
    for i in range(images):
        kmask[i] = jnp.where(rid == i, kb, 0.0).astype(BF)
        one = jnp.ones((kb.shape[0], 128), F32).astype(BF)
        kcol[i * ROWS:(i + 1) * ROWS, :] = mm(kmask[i], one, TN)[0:ROWS]
    send(0, kcol, kcol_h)
    bias[0:1, 0:D] = vec_ref[2:3, :]
    bias[0:1, D:2 * D] = jnp.zeros((1, D), F32)
    bias[0:1, 2 * D:] = vec_ref[3:4, :]
    for i in range(images):
        x = xs[i * SEQ:i * SEQ + ROWS, :]
        cen = x - jnp.mean(x, axis=1, keepdims=True)
        inv = lax.rsqrt(jnp.mean(cen * cen, axis=1, keepdims=True) + 1e-6)
        xh = cen * inv
        rows = slice(i * ROWS, (i + 1) * ROWS)
        xh1[rows, :] = xh.astype(BF)
        rstd1[rows, :] = jnp.broadcast_to(inv, (ROWS, 128))
        h1[rows, :] = (xh * vec_ref[0:1, :] + vec_ref[1:2, :]).astype(BF)
    send(8, xh1, xh1_h)
    send(9, rstd1, rstd1_h)
    h1t[...] = h1[...].T
    send(10, h1t, h1t_h)
    loads[0].wait()
    span = images * ROWS
    pad = qkv.shape[1] - span
    for t in range(3 * n_quads):
        qkv[t, span:, :] = jnp.zeros((pad, TILE), BF)

    def proj(t, _):
        col = pl.multiple_of(t * TILE, TILE)
        r = mm(h1[...], wqkv[:, pl.ds(col, TILE)]) + bias[0:1, pl.ds(col, TILE)]
        r = r * jnp.where(t < n_quads, HEAD_DIM ** -0.5, 1.0)
        qkv[t, 0:span, :] = r.astype(BF)
        return 0

    lax.fori_loop(0, 3 * n_quads, proj, 0, unroll=3)
    send(1, qkv, qkv_h)
    masks = head_masks()

    def attend(it, _):
        i = it // n_quads
        j = it % n_quads
        r0 = pl.multiple_of(i * ROWS, 16)
        q4 = qkv[j, pl.ds(r0, ROWS), :]
        k4 = qkv[n_quads + j, pl.ds(r0, WIN), :]
        v4 = qkv[2 * n_quads + j, pl.ds(r0, WIN), :]
        valid = keep8[pl.ds(i, 1), :] > 0.0
        out = jnp.zeros((ROWS, TILE), F32)
        for h, m in enumerate(masks):
            s = mm(q4 * m, k4, NT)
            s = jnp.where(valid, s, -1e30)
            e = jnp.exp(s - jnp.max(s, axis=1, keepdims=True))
            pb = (e * (1.0 / jnp.sum(e, axis=1, keepdims=True))).astype(BF)
            p_s[it, h * ROWS:(h + 1) * ROWS, :] = pb
            out = out + mm(pb, v4 * m)
        o_s[pl.ds(r0, ROWS), pl.ds(pl.multiple_of(j * TILE, TILE), TILE)] = out.astype(BF)
        return 0

    lax.fori_loop(0, images * n_quads, attend, 0, unroll=2)
    send(2, p_s, p_h)
    loads[1].wait()
    for j in range(n_quads):
        sl = slice(j * TILE, (j + 1) * TILE)
        y_s[:, sl] = mm(o_s[...], wout[:, sl])
    ot[...] = o_s[...].T
    send(3, ot, ot_h)
    pooled_ref[...] = jnp.zeros_like(pooled_ref)
    for i in range(images):
        rows = slice(i * ROWS, (i + 1) * ROWS)
        x = xs[i * SEQ:i * SEQ + ROWS, :]
        y = x + vec_ref[4:5, :] + y_s[rows, :]
        kc = kcol[rows, 0:1]
        pooled_ref[i:i + 1, 0:D] = jnp.sum(y * kc, axis=0, keepdims=True)
        cen = y - jnp.mean(y, axis=1, keepdims=True)
        inv = lax.rsqrt(jnp.mean(cen * cen, axis=1, keepdims=True) + 1e-6)
        xh = cen * inv
        xh2[rows, :] = xh.astype(BF)
        rstd2[rows, :] = jnp.broadcast_to(inv, (ROWS, 128))
        h2[rows, :] = (xh * vec_ref[5:6, :] + vec_ref[6:7, :]).astype(BF)
    h2t[...] = h2[...].T
    send(4, h2t, h2t_h)
    send(5, xh2, xh2_h)
    send(6, rstd2, rstd2_h)
    loads[2].wait()
    loads[3].wait()
    acc[...] = jnp.zeros_like(acc)
    a_s[span:, :] = jnp.zeros((a_s.shape[0] - span, TILE), BF)
    a_t[span:, :] = jnp.zeros((a_s.shape[0] - span, TILE), BF)


    def pool(t, a_s):
        ap = jnp.zeros((kmask.shape[1], TILE), F32)
        for i in range(images):
            ap = ap + mm(kmask[i], a_s[i * ROWS:i * ROWS + WIN, :])
        at = pl.multiple_of((t % n_quads) * TILE, TILE)
        apool_ref[t // n_quads, :, pl.ds(at, TILE)] = ap[0:8]
        hi = ap.astype(BF)
        lo = (ap - hi.astype(F32)).astype(BF)
        both = mm(jnp.concatenate([hi, lo], axis=0), wdown[pl.ds(pl.multiple_of(t * TILE, TILE), TILE), :])
        acc[...] += both[0:16] + both[16:32]

    def lift(t, u_s):
        col = pl.multiple_of(t * TILE, TILE)
        u_s[...] = mm(h2[...], wup[:, pl.ds(col, TILE)]) + upb_ref[0:1, pl.ds(col, TILE)]

    def bend(t, u_s, a_s):
        for i in range(images):
            rows = slice(i * ROWS, (i + 1) * ROWS)
            a, g = gelu_pair(u_s[rows, :])
            a_s[rows, :] = a.astype(BF)
            gk[t, rows, :] = (g * kcol[rows, 0:1]).astype(BF)
        pltpu.make_async_copy(gk.at[t], gk_h.at[t], out_sem.at[7]).start()

    lift(0, u_a)

    def feed(r, _):
        t = 2 * r
        lift(t + 1, u_b)
        bend(t, u_a, a_s)
        pool(t, a_s)
        lift(jnp.minimum(t + 2, n_ff - 1), u_a)
        bend(t + 1, u_b, a_t)
        pool(t + 1, a_t)
        return 0

    lax.fori_loop(0, n_ff // 2, feed, 0)
    cnt = jnp.sum(kb, axis=1, keepdims=True)[0:8]
    inv = 1.0 / jnp.maximum(cnt, 1.0)
    pooled_ref[:, 0:D] = (pooled_ref[:, 0:D] + acc[0:8, :]) * inv + vec_ref[7:8, :]
    pooled_ref[:, D:] = jnp.broadcast_to(cnt, (8, 128))
    for c in stores:
        c.wait()
    for t in range(n_ff):
        pltpu.make_async_copy(gk.at[t], gk_h.at[t], out_sem.at[7]).wait()


def forward_call(images, ff, tokens, keep, wqkv, wout, wup, wdown, vec, upb):
    span = images * ROWS
    nq = D // TILE
    wide = span + WIN - ROWS
    outs = [
        ((D, span), BF), ((3 * nq, wide, TILE), BF), ((images * nq, 4 * ROWS, TILE), BF),
        ((D, span), BF), ((D, span), BF), ((span, D), BF), ((span, D), BF), ((span, 128), F32), ((span, 128), F32),
        ((span, 128), F32), ((ff // TILE, span, TILE), BF), ((ff // D, 8, D), F32), ((8, D + 128), F32),
    ]
    anyspec = pl.BlockSpec(memory_space=pl.ANY)
    vm = pl.BlockSpec(memory_space=pltpu.VMEM)
    scratch = [
        pltpu.VMEM((D, 3 * D), BF), pltpu.VMEM((D, D), BF), pltpu.VMEM((D, ff), BF), pltpu.VMEM((ff, D), BF),
        pltpu.VMEM(((images - 1) * SEQ + ROWS + 7 & -8, D), F32),
    ] + [pltpu.VMEM(*o) for o in outs[:11]] + [
        pltpu.VMEM((span, D), BF), pltpu.VMEM((span, D), BF), pltpu.VMEM((span, D), F32), pltpu.VMEM((span, D), BF),
        pltpu.VMEM((wide, TILE), BF), pltpu.VMEM((wide, TILE), BF), pltpu.VMEM((span, TILE), F32), pltpu.VMEM((span, TILE), F32), pltpu.VMEM((16, WIN), F32), pltpu.VMEM((images, 16, WIN), BF),
        pltpu.VMEM((1, 3 * D), F32), pltpu.VMEM((16, D), F32),
        pltpu.SemaphoreType.DMA((4,)), pltpu.SemaphoreType.DMA((11,)),
    ]
    return pl.pallas_call(
        functools.partial(forward_kernel, images, ff),
        out_shape=[jax.ShapeDtypeStruct(s, d) for s, d in outs],
        in_specs=[vm, vm] + [anyspec] * 4 + [vm, vm],
        out_specs=[anyspec] * 11 + [vm, vm],
        scratch_shapes=scratch,
        compiler_params=pltpu.CompilerParams(vmem_limit_bytes=60 * 2**20),
        name="block_forward",
    )(tokens, keep, wqkv, wout, wup, wdown, vec, upb)


def split3(x):
    hi = x.astype(BF)
    r = x - hi.astype(F32)
    mid = r.astype(BF)
    lo = (r - mid.astype(F32)).astype(BF)
    return hi, mid, lo


NN = (((1,), (0,)), ((), ()))
MESH = pl.DeviceIdType.MESH


def mm3(x, w, dims=NN):
    hi, mid, lo = split3(x)
    return (mm(lo, w, dims) + mm(mid, w, dims)) + mm(hi, w, dims)


def place(cz, cy):
    row = lax.axis_index("row")
    col = lax.axis_index("col")
    return row, col // (2 * cy), lax.rem(col // 2, cy), lax.rem(col, 2)


def head_kernel(
    n_row, cz, cy, images, ff,
    pooled_ref, texts_ref, apool_ref, pair_ref, scale_ref, wproj_ref, wdown_h,
    loss_ref, dy_ref, da_ref, text_ref, proj_ref, down_ref,
    pg, tg, ax, ag, wdown, p_all, t_all, c_all, a_all, gproj, gdown,
    in_sem, zs, zr, ps, pr, cs, cr,
):
    x, z, y, core = place(cz, cy)
    load = pltpu.make_async_copy(wdown_h, wdown, in_sem.at[0])
    load.start()
    half = D // 2
    plane = n_row * cy
    spot = x * cy + y

    def device(xx, zz, yy, cc):
        return (xx, (zz * cy + yy) * 2 + cc)

    z_peers = [lax.rem(z + k, cz) for k in range(1, cz)]
    p_peers = [lax.rem(spot + k, plane) for k in range(1, plane)]
    bar = pltpu.get_barrier_semaphore()
    for zz in z_peers:
        pl.semaphore_signal(bar, inc=1, device_id=device(x, zz, y, core), device_id_type=MESH)
    for pp in p_peers:
        pl.semaphore_signal(bar, inc=1, device_id=device(pp // cy, z, lax.rem(pp, cy), core), device_id_type=MESH)
    pl.semaphore_signal(bar, inc=1, device_id=device(x, z, y, 1 - core), device_id_type=MESH)
    pg[x, z, y, core] = jnp.concatenate([pooled_ref[0:images, 0:half], pooled_ref[0:images, half:D]], axis=0)
    text = texts_ref[...].astype(F32)
    tg[x, z, y, core] = jnp.concatenate([text[:, k * 128:(k + 1) * 128] for k in range(EMB // 128)], axis=0).astype(BF)
    for g in range(cz):
        ax[g, 0:images, 0:half] = apool_ref[g, 0:images, 0:half]
        ax[g, images:, 0:half] = apool_ref[g, 0:images, half:]
        ax[g, 0:images, half:] = pooled_ref[0:images, D:]
        ax[g, images:, half:] = pooled_ref[0:images, D:]
    ag[x, z, y, core] = ax[z]
    pl.semaphore_wait(bar, cz - 1 + plane - 1 + 1)

    def stage(src, dst, sems, slot, devs):
        out = []
        for k, (s, dev) in enumerate(zip(src, devs)):
            c = pltpu.make_async_remote_copy(
                s, dst, sems[0].at[slot, k], sems[1].at[slot, k], device_id=dev, device_id_type=MESH)
            c.start()
            out.append(c)
        return out

    z_devs = [device(x, zz, y, core) for zz in z_peers]
    p_devs = [device(pp // cy, z, lax.rem(pp, cy), core) for pp in p_peers]
    c_devs = [device(x, z, y, 1 - core)]
    own = pg.at[x, z, y, core]
    own_t = tg.at[x, z, y, core]
    first = stage([own] * len(z_devs), own, (zs, zr), 0, z_devs)
    first_t = stage([own_t] * len(z_devs), own_t, (zs, zr), 2, z_devs)
    for c in first:
        c.wait()
    own = pg.at[x, :, y, core]
    second = stage([own] * len(p_devs), own, (ps, pr), 0, p_devs)
    for c in first_t:
        c.wait()
    own_t = tg.at[x, :, y, core]
    second_t = stage([own_t] * len(p_devs), own_t, (ps, pr), 2, p_devs)
    first_a = stage([ax.at[zz] for zz in z_peers], ag.at[x, z, y, core], (zs, zr), 1, z_devs)
    for c in second:
        c.wait()
    own = pg.at[:, :, :, core]
    third = stage([own], own, (cs, cr), 0, c_devs)
    for c in second_t:
        c.wait()
    own_t = tg.at[:, :, :, core]
    third_t = stage([own_t], own_t, (cs, cr), 2, c_devs)
    for c in first_a:
        c.wait()
    own = ag.at[x, :, y, core]
    second_a = stage([own] * len(p_devs), own, (ps, pr), 1, p_devs)
    for c in third:
        c.wait()
    n_col = cz * cy * 2
    n_img = n_row * n_col * images
    for d in range(n_row * n_col):
        rows = slice(d * images, (d + 1) * images)
        at = (d // n_col, d % n_col // (2 * cy), d // 2 % cy, d % 2)
        p_all[rows, 0:half] = pg[at + (slice(0, images),)]
        p_all[rows, half:] = pg[at + (slice(images, 2 * images),)]
    scale = scale_ref[0]
    pooled = p_all[...]
    latent = mm3(pooled, wproj_ref[...])
    norm = lax.rsqrt(jnp.sum(latent * latent, axis=1, keepdims=True) + 1e-6)
    embeds = latent * norm
    eb = embeds.astype(BF)
    for c in third_t:
        c.wait()
    for d in range(n_row * n_col):
        rows = slice(d * images, (d + 1) * images)
        text = tg[d // n_col, d % n_col // (2 * cy), d // 2 % cy, d % 2].astype(F32)
        for k in range(EMB // 128):
            t_all[rows, k * 128:(k + 1) * 128] = text[k * images:(k + 1) * images]
    tb = t_all[...].astype(BF)
    logits = scale * mm(eb, tb, NT)
    row_max = jnp.max(logits, axis=1, keepdims=True)
    row_exp = jnp.exp(logits - row_max)
    row_sum = jnp.sum(row_exp, axis=1, keepdims=True)
    col_max = jnp.max(logits, axis=0, keepdims=True)
    col_exp = jnp.exp(logits - col_max)
    col_sum = jnp.sum(col_exp, axis=0, keepdims=True)
    ids = lax.broadcasted_iota(jnp.int32, (n_img, n_img), 0)
    match = (ids == pair_ref[...]).astype(F32).T
    grad = 0.5 * (row_exp / row_sum) + 0.5 * (col_exp / col_sum) - match
    lse = jnp.sum(row_max + jnp.log(row_sum), axis=0, keepdims=True) + jnp.sum(
        col_max + jnp.log(col_sum), axis=1, keepdims=True)
    hits = jnp.sum(jnp.sum(logits * match, axis=1, keepdims=True), axis=0, keepdims=True)
    loss_ref[...] = (0.5 * lse - hits) * (1.0 / n_img)
    de = scale * mm3(grad, tb)
    dz = norm * (de - embeds * jnp.sum(embeds * de, axis=1, keepdims=True))
    pooled_grad = mm3(dz, wproj_ref[...], NT)
    dev = x * n_col + (z * cy + y) * 2 + core
    want = lax.broadcasted_iota(jnp.int32, (16, n_img), 0) + dev * images
    have = lax.broadcasted_iota(jnp.int32, (16, n_img), 1)
    pick = (want == have).astype(F32).astype(BF)
    hi, mid, lo = split3(pooled_grad)
    dy = (mm(pick, lo) + mm(pick, mid)) + mm(pick, hi)
    dy = dy[0:8] / jnp.maximum(pooled_ref[:, D:D + 1], 1.0)
    dy_ref[...] = dy
    dyb = jnp.concatenate([dy, jnp.zeros_like(dy)], axis=0).astype(BF)
    for c in second_a:
        c.wait()
    own = ag.at[:, :, :, core]
    third_a = stage([own], own, (cs, cr), 1, c_devs)
    load.wait()

    for t in range(ff // TILE):
        sl = slice(t * TILE, (t + 1) * TILE)
        da_ref[:, sl] = mm(dyb, wdown[sl, :], NT)[0:8]
    g_hi, g_mid, g_lo = split3(grad)
    own_grad = (mm(pick, g_lo, NT) + mm(pick, g_mid, NT)) + mm(pick, g_hi, NT)
    text_ref[...] = (scale * mm3(own_grad, eb))[0:images]
    p_hi, p_lo, _ = split3(pooled)
    d_hi, d_lo, _ = split3(dz)
    gproj[...] = (mm(p_lo, d_hi, TN) + mm(p_hi, d_lo, TN)) + mm(p_hi, d_hi, TN)
    n_proj = D // n_col
    at = pl.multiple_of(((z * cy + y) * 2 + core) * n_proj, 8)
    proj_ref[...] = gproj[pl.ds(at, n_proj), :]
    for c in third_a:
        c.wait()
    for d in range(n_row * n_col):
        rows = slice(d * images, (d + 1) * images)
        at = (d // n_col, d % n_col // (2 * cy), d // 2 % cy, d % 2)
        a_all[rows, 0:half] = ag[at + (slice(0, images), slice(0, half))]
        a_all[rows, half:] = ag[at + (slice(images, 2 * images), slice(0, half))]
        c_all[rows, :] = ag[at + (slice(0, images), slice(half, half + 128))]
    hi = (pooled_grad / c_all[:, 0:1]).astype(BF)
    acts = a_all[...]
    a_hi = acts.astype(BF)
    a_lo = (acts - a_hi.astype(F32)).astype(BF)
    for n in range(D // TILE):
        sl = slice(n * TILE, (n + 1) * TILE)
        gdown[:, sl] = mm(a_lo, hi[:, sl], TN) + mm(a_hi, hi[:, sl], TN)
    n_down = ff // n_col
    at = pl.multiple_of((y * 2 + core) * n_down, 8)
    down_ref[...] = gdown[pl.ds(at, n_down), :]


def head_call(n_row, n_col, images, ff, pooled, texts, apool, pair, scale, wproj, wdown):
    cz = ff // D
    cy = n_col // (2 * cz)
    n_img = n_row * n_col * images
    vm = pl.BlockSpec(memory_space=pltpu.VMEM)
    outs = [(1, 1), (8, D), (8, ff), (images, EMB), (D // n_col, EMB), (ff // n_col, D)]
    plane = n_row * cy
    grid = (n_row, cz, cy, 2, 2 * images)
    scratch = [
        pltpu.VMEM(grid + (D // 2,), F32), pltpu.VMEM(grid[:4] + (images * EMB // 128, 128), BF),
        pltpu.VMEM((cz, 2 * images, D // 2 + 128), F32), pltpu.VMEM(grid + (D // 2 + 128,), F32),
        pltpu.VMEM((ff, D), BF), pltpu.VMEM((n_img, D), F32), pltpu.VMEM((n_img, EMB), F32),
        pltpu.VMEM((n_img, 128), F32), pltpu.VMEM((n_img, D), F32), pltpu.VMEM((D, EMB), F32), pltpu.VMEM((D, D), F32),
        pltpu.SemaphoreType.DMA((1,)), pltpu.SemaphoreType.DMA((3, cz - 1)), pltpu.SemaphoreType.DMA((3, cz - 1)),
        pltpu.SemaphoreType.DMA((3, plane - 1)), pltpu.SemaphoreType.DMA((3, plane - 1)),
        pltpu.SemaphoreType.DMA((3, 1)), pltpu.SemaphoreType.DMA((3, 1)),
    ]
    return pl.pallas_call(
        functools.partial(head_kernel, n_row, cz, cy, images, ff),
        out_shape=[jax.ShapeDtypeStruct(s, F32) for s in outs],
        in_specs=[vm] * 4 + [pl.BlockSpec(memory_space=pltpu.SMEM), vm, pl.BlockSpec(memory_space=pl.ANY)],
        out_specs=[vm] * len(outs),
        scratch_shapes=scratch,
        compiler_params=pltpu.CompilerParams(
            vmem_limit_bytes=60 * 2**20, collective_id=0, has_side_effects=True),
        name="contrastive_head",
    )(pooled, texts, apool, pair, scale, wproj, wdown)


READY = [2, 5, 8, 11, 18, 23, 28, 33]
WAITS = [[(7, 0), (9, 1), (12, 2), (13, 3), (21, 4), (26, 5), (31, 6), (35, 7)], [(13, 0), (16, 1), (20, 2), (24, 3), (28, 4), (33, 5), (36, 6)], [(16, 0), (22, 1), (24, 2), (29, 3), (32, 4), (36, 5)], [(24, 0), (28, 1), (29, 2), (34, 3), (37, 4)], [(29, 0), (33, 1), (34, 2), (37, 3)]]
TAIL = [(1, 7), (3, 5), (2, 6), (4, 4), (4, 5), (2, 7), (3, 6), (3, 7), (4, 6), (4, 7)]


def backward_kernel(
    n_row, cz, cy, images, ff, n_a,
    dy_ref, da_ref, vec_ref,
    wqkv_h, wout_h, wup_h, h1t_h, qkv_h, p_h, ot_h, h2t_h, xh1_h, xh2_h, rstd1_h, rstd2_h, kcol_h, gk_h,
    tg_h, qg_ref, og_ref, ug_ref, small_ref,
    tg_ref, wqkv, wout, wup, h1t, qkv, ot, h2t, xh1, xh2, rstd1, rstd2, kcol, p_s, du, dx, db, do_s, dp_s,
    g, r0, r1a, r1b, r2a, r2b, r3a, r3b, r4b, res, vc, vp, vz, sv, small_s,
    in_sem, gk_sem, p_sem, s_sem, r_sem, vs_sem, vr_sem,
):
    n_quads = D // TILE
    n_ff = ff // TILE
    n_up = ff // D
    n_chunks = n_up + 1 + n_quads
    masks = head_masks()
    x, z, y, core = place(cz, cy)
    two = n_a < D
    n_h = (D - n_a) // 2
    plane = n_row * cy
    spot = x * cy + y

    def device(xx, zz, yy, cc):
        return (xx, (zz * cy + yy) * 2 + cc)

    core_dev = device(x, z, y, 1 - core)
    y_peers = [lax.rem(y + k, cy) for k in range(1, cy)]
    z_peers = [lax.rem(z + k, cz) for k in range(1, cz)]
    x_peers = [lax.rem(x + k, n_row) for k in range(1, n_row)]
    p_peers = [lax.rem(spot + k, plane) for k in range(1, plane)]
    z_devs = [device(x, zz, y, core) for zz in z_peers]
    y_devs = [device(x, z, yy, core) for yy in y_peers]
    x_devs = [device(xx, z, y, core) for xx in x_peers]
    p_devs = [device(pp // cy, z, lax.rem(pp, cy), core) for pp in p_peers]

    loads = {}
    for k, (name, src, dst) in enumerate((
        ("kcol", kcol_h, kcol), ("h2t", h2t_h, h2t), ("wup", wup_h, wup), ("xh2", xh2_h, xh2),
        ("rstd2", rstd2_h, rstd2), ("wout", wout_h, wout), ("ot", ot_h, ot), ("qkv", qkv_h, qkv),
        ("h1t", h1t_h, h1t), ("wqkv", wqkv_h, wqkv), ("xh1", xh1_h, xh1), ("rstd1", rstd1_h, rstd1),
    )):
        loads[name] = pltpu.make_async_copy(src, dst, in_sem.at[k])

    def gcopy(t):
        col = pl.multiple_of(t * TILE, TILE)
        return pltpu.make_async_copy(gk_h.at[t], du.at[:, pl.ds(col, TILE)], gk_sem.at[t])

    loads["h2t"].start()
    for t in range(n_ff):
        gcopy(t).start()
    for name in ("kcol", "wup", "xh2", "rstd2", "wout", "ot", "qkv", "h1t", "wqkv", "xh1", "rstd1"):
        loads[name].start()

    def pcopy(step):
        i = lax.rem(step, images)
        j = step // images
        slot = lax.rem(step, 2)
        return pltpu.make_async_copy(p_h.at[i * n_quads + j], p_s.at[slot], p_sem.at[slot])

    pcopy(0).start()
    bar = pltpu.get_barrier_semaphore()
    for dev in z_devs + p_devs + [core_dev]:
        pl.semaphore_signal(bar, inc=1, device_id=dev, device_id_type=MESH)
    half = lambda which: pl.ds(pl.multiple_of(n_a + which * n_h, 128), n_h)

    def copies(p, c):
        if p == 0:
            out = [(g.at[lax.rem(c, 4), :, :, 1 - core], r0.at[c], core_dev)]
        elif p == 1:
            out = [(r0.at[c, :, yy, :, 0:n_a], r1a.at[c, k], dev) for k, (yy, dev) in enumerate(zip(y_peers, y_devs))]
            if two:
                out += [(r0.at[c, :, :, :, half(1 - x)], r1b.at[c], x_devs[0])]
        elif p == 2:
            out = [(r1a.at[c, 0, zz], r2a.at[c, k], dev) for k, (zz, dev) in enumerate(zip(z_peers, z_devs))]
            if two:
                out += [(r1b.at[c, :, yy], r2b.at[c, k], dev) for k, (yy, dev) in enumerate(zip(y_peers, y_devs))]
        elif p == 3:
            out = [(r3a.at[c, x], r3a.at[c, x], dev) for dev in x_devs]
            if two:
                out += [(r2b.at[c, 0, zz], r3b.at[c, k], dev) for k, (zz, dev) in enumerate(zip(z_peers, z_devs))]
        else:
            out = [(r3b.at[c, 0], r4b.at[c], x_devs[0])] if two else []
        base = (0, 1, 1 + cy, cz + 2 * cy - 1, 2 * cz + 2 * cy + n_row - 3)[p]
        return [
            pltpu.make_async_remote_copy(
                src, dst, s_sem.at[lax.rem(c, 4), base + k], r_sem.at[c, base + k], device_id=dev, device_id_type=MESH)
            for k, (src, dst, dev) in enumerate(out)
        ]

    def finish(p, c):
        up = lambda v: v.astype(F32)
        if p == 0:
            r0[c] = r0[c] + g[lax.rem(c, 4), :, :, core]
        elif p == 1:
            v = up(r0[c, :, y, :, 0:n_a])
            for k in range(cy - 1):
                v = v + up(r1a[c, k])
            r1a[c, 0] = v.astype(BF)
            if two:
                r1b[c] = r1b[c] + r0[c, :, :, :, half(x)]
        elif p == 2:
            v = up(r1a[c, 0, z])
            for k in range(cz - 1):
                v = v + up(r2a[c, k])
            r3a[c, x] = v.astype(BF)
            if two:
                v = up(r1b[c, :, y])
                for k in range(cy - 1):
                    v = v + up(r2b[c, k])
                r2b[c, 0] = v.astype(BF)
        elif p == 3:
            v = up(r3a[c, 0])
            for k in range(1, n_row):
                v = v + up(r3a[c, k])
            res[c, :, 0:n_a] = v
            if two:
                v = up(r2b[c, 0, z])
                for k in range(cz - 1):
                    v = v + up(r3b[c, k])
                v = v.astype(BF)
                r3b[c, 0] = v
                res[c, :, half(x)] = up(v)
        elif two:
            res[c, :, half(1 - x)] = up(r4b[c])

    def begin(p, c):
        for d in copies(p, c):
            d.start()

    def advance(p, c):
        for d in copies(p, c):
            d.wait()
        finish(p, c)
        if p < 4:
            begin(p + 1, c)

    def lookup(n, events):
        hit = n < 0
        c = jnp.int32(0)
        for at, chunk in events:
            same = n == at
            hit = hit | same
            c = jnp.where(same, chunk, c)
        return hit, c

    def tick(n):
        @pl.when(n == READY[0])
        def _():
            pl.semaphore_wait(bar, len(z_devs) + len(p_devs) + 1)

        hit, c = lookup(n, [(at, k) for k, at in enumerate(READY)])

        @pl.when(hit)
        def _():
            begin(0, c)

        for p in range(4, -1, -1):
            hit, c = lookup(n, WAITS[p])

            @pl.when(hit)
            def _(p=p, c=c):
                advance(p, c)

    def put(c, tt, part):
        col = pl.multiple_of(tt * TILE, TILE)
        g[lax.rem(c, 4), :, :, :, :, pl.ds(col, TILE)] = part.reshape(g.shape[1:5] + (TILE,)).astype(BF)

    def unit_up(t):
        n = t // n_quads
        tt = lax.rem(t, n_quads)
        col = pl.multiple_of(t * TILE, TILE)
        gcopy(t).wait()
        ub = jnp.zeros((1, TILE), F32)
        for i in range(images):
            rows = slice(i * ROWS, (i + 1) * ROWS)
            d = du[rows, pl.ds(col, TILE)].astype(F32) * da_ref[i:i + 1, pl.ds(col, TILE)]
            ub = ub + jnp.sum(d, axis=0, keepdims=True)
            du[rows, pl.ds(col, TILE)] = d.astype(BF)
        scol = pl.multiple_of(tt * TILE, TILE)
        small_s[pl.ds(8 + n, 1), pl.ds(scol, TILE)] = ub
        put(n, tt, mm(h2t[...], du[:, pl.ds(col, TILE)]))

    def unit_down(n):
        @pl.when(n == 0)
        def _():
            loads["wup"].wait()

        col = pl.multiple_of(n * TILE, TILE)
        dx[:, pl.ds(col, TILE)] = mm(du[...], wup[pl.ds(col, TILE), :], NT)

    def unit_mid():
        for name in ("kcol", "xh2", "rstd2", "wout", "ot"):
            loads[name].wait()
        dy = dy_ref[...]
        dyb = dy.astype(BF).astype(F32)
        g2 = jnp.zeros((1, D), F32)
        b2 = jnp.zeros((1, D), F32)
        bo = jnp.zeros((1, D), F32)
        bd = jnp.zeros((1, D), F32)
        for i in range(images):
            rows = slice(i * ROWS, (i + 1) * ROWS)
            kc = kcol[rows, 0:1]
            bd = bd + jnp.sum(kc, axis=0, keepdims=True) * dyb[i:i + 1, :]
            dh = dx[rows, :]
            xh = xh2[rows, :].astype(F32)
            g2 = g2 + jnp.sum(dh * xh, axis=0, keepdims=True)
            b2 = b2 + jnp.sum(dh, axis=0, keepdims=True)
            c = dh * vec_ref[5:6, :]
            m1 = jnp.mean(c, axis=1, keepdims=True)
            m2 = jnp.mean(c * xh, axis=1, keepdims=True)
            r = dy[i:i + 1, :] * kc + rstd2[rows, 0:1] * (c - m1 - xh * m2)
            dx[rows, :] = r
            rb = r.astype(BF)
            db[rows, :] = rb
            bo = bo + jnp.sum(rb.astype(F32), axis=0, keepdims=True)
        small_s[0:4, :] = jnp.zeros((4, D), F32)
        small_s[4:5, :] = bo
        small_s[5:6, :] = g2
        small_s[6:7, :] = b2
        small_s[7:8, :] = bd
        for name in ("qkv", "h1t"):
            loads[name].wait()

    def unit_out(j):
        col = pl.multiple_of(j * TILE, TILE)
        do_s[j] = mm(db[...], wout[pl.ds(col, TILE), :], NT).astype(BF)
        put(n_up, j, mm(ot[...], db[:, pl.ds(col, TILE)]))

    def unit_attend(j, i):
        r0_ = pl.multiple_of(i * ROWS, 16)
        step = j * images + i
        slot = lax.rem(step, 2)

        @pl.when(step + 1 < n_quads * images)
        def _():
            pcopy(step + 1).start()

        pcopy(step).wait()
        q4 = qkv[j, pl.ds(r0_, ROWS), :]
        k4 = qkv[n_quads + j, pl.ds(r0_, WIN), :]
        v4 = qkv[2 * n_quads + j, pl.ds(r0_, WIN), :]
        d4 = do_s[j, pl.ds(r0_, ROWS), :]
        dp = mm(jnp.concatenate([d4 * mask for mask in masks], axis=0), v4, NT)
        pb = p_s[slot]
        pf = pb.astype(F32)
        ds = (pf * (dp - jnp.sum(pf * dp, axis=1, keepdims=True))).astype(BF)
        dq = jnp.zeros((ROWS, TILE), F32)
        dt = d4.T
        qt = q4.T
        dv = []
        dk = []
        for h, mask in enumerate(masks):
            rows = slice(h * ROWS, (h + 1) * ROWS)
            cut = slice(h * HEAD_DIM, (h + 1) * HEAD_DIM)
            dq = dq + mm(ds[rows], k4 * mask)
            dv.append(mm(dt[cut], pb[rows]))
            dk.append(mm(qt[cut], ds[rows]))
        dv = jnp.concatenate(dv, axis=0).T
        dk = jnp.concatenate(dk, axis=0).T
        dq = dq * HEAD_DIM ** -0.5
        dv = dv[0:ROWS]
        sl = pl.ds(pl.multiple_of(j * TILE, TILE), TILE)
        small_s[2:3, sl] += jnp.sum(dq, axis=0, keepdims=True)
        small_s[3:4, sl] += jnp.sum(dv, axis=0, keepdims=True)
        for s, val in enumerate((dq, dk[0:ROWS], dv)):
            col = pl.multiple_of(s * D + j * TILE, TILE)
            dp_s[pl.ds(r0_, ROWS), pl.ds(col, TILE)] = val.astype(BF)

    def unit_weight(j):
        for s in range(3):
            col = pl.multiple_of(s * D + j * TILE, TILE)
            put(n_up + 1 + j, s, mm(h1t[...], dp_s[:, pl.ds(col, TILE)]))

    def unit_norm(i):
        @pl.when(i == 0)
        def _():
            for name in ("wqkv", "xh1", "rstd1"):
                loads[name].wait()

        rows = pl.ds(pl.multiple_of(i * ROWS, 16), ROWS)
        dh = mm(dp_s[rows, :], wqkv[...], NT)
        xh = xh1[rows, :].astype(F32)
        small_s[0:1, :] += jnp.sum(dh * xh, axis=0, keepdims=True)
        small_s[1:2, :] += jnp.sum(dh, axis=0, keepdims=True)
        c = dh * vec_ref[0:1, :]
        m1 = jnp.mean(c, axis=1, keepdims=True)
        m2 = jnp.mean(c * xh, axis=1, keepdims=True)
        r = dx[rows, :] + rstd1[rows, 0:1] * (c - m1 - xh * m2)
        for k in range(images):
            @pl.when(i == k)
            def _(k=k):
                tg_ref[k * SEQ:(k + 1) * SEQ, :] = r[0:SEQ]

    small_s[...] = jnp.zeros_like(small_s)
    loads["h2t"].wait()
    t_down = n_ff
    t_mid = t_down + n_quads
    t_out = t_mid + 1
    t_attend = t_out + n_quads
    t_norm = t_attend + n_quads * (images + 1)

    def unit(n, _):
        @pl.when(n < t_down)
        def _():
            unit_up(n)

        @pl.when((n >= t_down) & (n < t_mid))
        def _():
            unit_down(n - t_down)

        @pl.when(n == t_mid)
        def _():
            unit_mid()

        @pl.when((n >= t_out) & (n < t_attend))
        def _():
            unit_out(n - t_out)

        m = n - t_attend
        inner = lax.rem(m, images + 1)

        @pl.when((m >= 0) & (n < t_norm) & (inner < images))
        def _():
            unit_attend(m // (images + 1), inner)

        @pl.when((m >= 0) & (n < t_norm) & (inner == images))
        def _():
            unit_weight(m // (images + 1))

        @pl.when(n >= t_norm)
        def _():
            unit_norm(n - t_norm)

        tick(n)
        return 0

    lax.fori_loop(0, t_norm + images, unit, 0)
    leave = pltpu.make_async_copy(tg_ref, tg_h, in_sem.at[12])
    leave.start()

    def spread(src, dst, slot, devs):
        out = []
        for k, dev in enumerate(devs):
            d = pltpu.make_async_remote_copy(
                src[k], dst, vs_sem.at[slot, k], vr_sem.at[slot, k], device_id=dev, device_id_type=MESH)
            d.start()
            out.append(d)
        return out

    def total(ref, count):
        v = ref[0]
        for k in range(1, count):
            v = v + ref[k]
        return v

    part = D // cz
    for zz in range(cz):
        sv[zz, 0:8, 0:part] = small_s[0:8, zz * part:(zz + 1) * part]
        for k in range(D // part):
            sv[zz, 8 + k:9 + k, 0:part] = small_s[8 + zz:9 + zz, k * part:(k + 1) * part]
    vz[z] = sv[z]
    going = spread([sv.at[zz] for zz in z_peers], vz.at[z], 0, z_devs)
    for e, (p, c) in enumerate(TAIL):
        advance(p, c)
        if e == len(TAIL) // 3:
            for d in going:
                d.wait()
            vp[spot] = total(vz, cz)
            going = spread([vp.at[spot]] * len(p_devs), vp.at[spot], 1, p_devs)
        if e == 2 * len(TAIL) // 3:
            for d in going:
                d.wait()
            vc[core] = total(vp, plane)
            going = spread([vc.at[core]], vc.at[core], 2, [core_dev])
    for d in going:
        d.wait()
    small_ref[...] = total(vc, 2)
    leave.wait()
    for c in range(n_up):
        ug_ref[:, c * D:(c + 1) * D] = res[c]
    og_ref[...] = res[n_up]
    for j in range(n_quads):
        for s in range(3):
            qg_ref[:, s * D + j * TILE:s * D + (j + 1) * TILE] = res[n_up + 1 + j, :, s * TILE:(s + 1) * TILE]


def backward_call(n_row, n_col, images, ff, dy, da, vec, wqkv, wout, wup, acts):
    span = images * ROWS
    nq = D // TILE
    wide = span + WIN - ROWS
    cz = ff // D
    cy = n_col // (2 * cz)
    blk = D // n_col
    n_a = 256 if n_row == 2 else D
    n_h = max((D - n_a) // 2, 128)
    n_ch = ff // D + 1 + nq
    plane = n_row * cy
    n_sem = 2 * cz + 2 * cy + n_row - 2
    anyspec = pl.BlockSpec(memory_space=pl.ANY)
    vm = pl.BlockSpec(memory_space=pltpu.VMEM)
    outs = [(images * SEQ, D), (blk, 3 * D), (blk, D), (blk, ff), (16, 256)]
    B16 = lambda *s: pltpu.VMEM(s, BF)
    B32 = lambda *s: pltpu.VMEM(s, F32)
    scratch = [
        B32(images * SEQ, D), B16(D, 3 * D), B16(D, D), B16(D, ff), B16(D, span), B16(3 * nq, wide, TILE), B16(D, span), B16(D, span),
        B16(span, D), B16(span, D), B32(span, 128), B32(span, 128), B32(span, 128),
        B16(2, 4 * ROWS, TILE), B16(span, ff), B32(span, D), B16(span, D), B16(nq, span, TILE), B16(span, 3 * D),
        B16(4, cz, cy, 2, blk, D), B16(n_ch, cz, cy, blk, D),
        B16(n_ch, cy - 1, cz, blk, n_a), B16(n_ch, cz, cy, blk, n_h),
        B16(n_ch, cz - 1, blk, n_a), B16(n_ch, cy - 1, cz, blk, n_h),
        B16(n_ch, n_row, blk, n_a), B16(n_ch, cz - 1, blk, n_h), B16(n_ch, blk, n_h), B32(n_ch, blk, D),
        B32(2, 16, 256), B32(plane, 16, 256), B32(cz, 16, 256), B32(cz, 16, 256), B32(16, D),
        pltpu.SemaphoreType.DMA((13,)), pltpu.SemaphoreType.DMA((ff // TILE,)), pltpu.SemaphoreType.DMA((2,)),
        pltpu.SemaphoreType.DMA((4, n_sem)), pltpu.SemaphoreType.DMA((n_ch, n_sem)),
        pltpu.SemaphoreType.DMA((3, plane)), pltpu.SemaphoreType.DMA((3, plane)),
    ]
    return pl.pallas_call(
        functools.partial(backward_kernel, n_row, cz, cy, images, ff, n_a),
        out_shape=[jax.ShapeDtypeStruct(s, F32) for s in outs],
        in_specs=[vm] * 3 + [anyspec] * 14,
        out_specs=[anyspec] + [vm] * (len(outs) - 1),
        scratch_shapes=scratch,
        compiler_params=pltpu.CompilerParams(
            vmem_limit_bytes=62 * 2**20, collective_id=1, has_side_effects=True),
        name="block_backward",
    )(dy, da, vec, wqkv, wout, wup, *acts)


def finish_kernel(n_col, cz, images, ff, small_ref, *refs):
    n_big = (len(refs) - 4) // 3
    big, vec_ref, ub_ref, outs = refs[:n_big], refs[n_big], refs[n_big + 1], refs[n_big + 2:2 * n_big + 2]
    held, in_sem, out_sem = refs[2 * n_big + 2:-2], refs[-2], refs[-1]
    moves = []
    for src, mid, dst in zip(big, held, outs):
        rows = src.shape[0]
        step = rows if rows < 400 else 200
        for at in range(0, rows, step):
            sl = pl.ds(at, min(step, rows - at))
            k = len(moves)
            c = pltpu.make_async_copy(src.at[sl], mid.at[sl], in_sem.at[k])
            c.start()
            moves.append((c, pltpu.make_async_copy(mid.at[sl], dst.at[sl], out_sem.at[k])))
    for c, d in moves:
        c.wait()
        d.start()
    member = lax.rem(lax.axis_index("col"), n_col // cz)
    part = D // cz
    values = small_ref[...]
    src = lax.broadcasted_iota(jnp.int32, (256, 256), 0)
    lane = lax.broadcasted_iota(jnp.int32, (256, 256), 1)
    width = D // n_col
    pick = (src == lane + member * width).astype(F32).astype(BF)
    vec_ref[...] = mm3(values[0:8], pick)[:, 0:width]
    n_ub = ff // n_col
    row = lax.broadcasted_iota(jnp.int32, values.shape, 0)
    line = jnp.sum(jnp.where(row == 8 + member * n_ub // part, values, 0.0), axis=0, keepdims=True)
    pick = (src == lane + lax.rem(member * n_ub, part)).astype(F32).astype(BF)
    ub_ref[...] = mm3(jnp.broadcast_to(line, (8, 256)), pick)[0:1, 0:n_ub]
    for c, d in moves:
        d.wait()


def finish_call(n_col, images, ff, small, *big):
    vm = pl.BlockSpec(memory_space=pltpu.VMEM)
    anyspec = pl.BlockSpec(memory_space=pl.ANY)
    shapes = [jax.ShapeDtypeStruct((8, D // n_col), F32), jax.ShapeDtypeStruct((1, ff // n_col), F32)]
    shapes += [jax.ShapeDtypeStruct(b.shape, b.dtype) for b in big]
    return pl.pallas_call(
        functools.partial(finish_kernel, n_col, ff // D, images, ff),
        out_shape=shapes,
        in_specs=[vm] + [anyspec] * len(big),
        out_specs=[vm, vm] + [anyspec] * len(big),
        scratch_shapes=[pltpu.VMEM(b.shape, b.dtype) for b in big] + [pltpu.SemaphoreType.DMA((12,))] * 2,
        compiler_params=pltpu.CompilerParams(vmem_limit_bytes=62 * 2**20),
        name="results",
    )(small, *big)


def per_device(
    tokens,
    keep_mask,
    w_qkv,
    w_out,
    w_up,
    w_down,
    vectors,
    up_bias,
    w_proj,
    texts,
    pair_index,
    logit_scale,
):
    images = keep_mask.shape[0]
    ff = w_up.shape[1]
    n_row, shards = lax.axis_size("row"), lax.axis_size("col")
    acts = forward_call(
        images, ff, tokens, keep_mask, w_qkv, w_out, w_up, w_down, vectors, up_bias.reshape(1, ff)
    )
    loss, dy, da, text_grad, grad_proj, grad_down = head_call(
        n_row, shards, images, ff, acts[12], texts, acts[11], pair_index.reshape(1, -1), logit_scale, w_proj, w_down
    )
    token_grad, qkv_share, out_share, up_share, small = backward_call(
        n_row, shards, images, ff, dy, da, vectors, w_qkv, w_out, w_up, acts[:11]
    )
    vec_share, bias_share, token_grad, qkv_share, out_share, up_share, grad_down, grad_proj, text_grad = finish_call(
        shards, images, ff, small, token_grad, qkv_share, out_share, up_share, grad_down, grad_proj, text_grad
    )
    return (
        loss.reshape(1),
        token_grad,
        qkv_share,
        out_share,
        up_share,
        grad_down,
        vec_share,
        bias_share.reshape(-1),
        grad_proj,
        text_grad,
    )


def solution(mesh):
    in_specs = (
        P(("row", "col"), None),
        P(("row", "col"), None),
        P(),
        P(),
        P(),
        P(),
        P(),
        P(),
        P(),
        P(("row", "col"), None),
        P(),
        P(),
    )
    out_specs = (
        P(),
        P(("row", "col"), None),
        P("col", None),
        P("col", None),
        P("col", None),
        P("col", None),
        P(None, "col"),
        P("col"),
        P("col", None),
        P(("row", "col"), None),
    )
    return jax.shard_map(
        per_device, mesh=mesh, in_specs=in_specs, out_specs=out_specs, check_vma=False
    )
```
